32 devices in a mesh: dp: 8 (over z, x), group: 4 (over y, core).
Axes of the slice: x: 2, y: 2, z: 4, core: 2. Of those that a mesh axis runs over, the one named last changes fastest.
Arguments:
- enc: bfloat16 [36864, 512], P(('dp', 'group')), may hold values from -6 to 6
- visible: int32 [36864], P(('dp', 'group')), may hold values 0 or 1
- band_group: int32 [36864], P(('dp', 'group')), may hold values from 0 to 3, as said below
- cotangent: bfloat16 [36864, 512], P(('dp', 'group')), may hold values from -6 to 6
- ln1_gain: float32 [512], replicated, may hold values from 0.5 to 1.5
- ln1_bias: float32 [512], replicated, may hold values from -3 to 3
- w_qkv: bfloat16 [512, 1536], replicated, may hold values from -0.25 to 0.25
- w_out: bfloat16 [512, 512], replicated, may hold values from -1.5 to 1.5
- ln2_gain: float32 [512], replicated, may hold values from 0.5 to 1.5
- ln2_bias: float32 [512], replicated, may hold values from -3 to 3
- w_up: bfloat16 [512, 2048], replicated, may hold values from -0.25 to 0.25
- w_down: bfloat16 [2048, 512], replicated, may hold values from -0.125 to 0.125
- mask_token: float32 [512], replicated, may hold values from -5 to 5
Outputs:
- out: bfloat16 [36864, 512], P(('dp', 'group'))
- grad_enc: bfloat16 [36864, 512], P(('dp', 'group'))
- grad_ln1_gain: float32 [512], replicated
- grad_ln1_bias: float32 [512], replicated
- grad_w_qkv: float32 [512, 1536], replicated
- grad_w_out: float32 [512, 512], replicated
- grad_ln2_gain: float32 [512], replicated
- grad_ln2_bias: float32 [512], replicated
- grad_w_up: float32 [512, 2048], replicated
- grad_w_down: float32 [2048, 512], replicated
- grad_mask_token: float32 [512], replicated
The draws below stay inside these ranges and needn't reach their ends.
Inputs may be any that keep to these rules, and one draw needn't show every extreme that they name: `band_group`: in every cube, each device's 384 tokens of it hold at most 128 tokens of any one band group, and one band group of the cube has exactly 128 on every device.
All inputs are finite; a program needn't handle non-finite values. No bound on the sum of `visible` on one device may be relied on, other than what follows from the above.
Results may differ from the reference program's by a relative error of at most 0.013.
Values may be sent and summed in bfloat16 or wider, within the bound.
A program may use at most 192 MiB of HBM per device.

```python
import jax
import jax.numpy as jnp
from jax import lax

D = 512
HEADS = 16
HD = 32
FF = 2048
CUBE_TOK = 1536
CUBES = 3
QUART = 384
CAP = 128
SET = 512
TOKENS = 36864
N_DP = 8
N_GROUP = 4


def draw_band_group(key, part):
    key = jax.random.fold_in(key, 17)
    groups = CUBE_TOK // QUART
    rows_dp = TOKENS // (CUBES * CUBE_TOK)
    quarters = rows_dp * groups * CUBES
    key_first, key_second, key_label, key_shuffle = jax.random.split(key, 4)
    first = jax.random.randint(key_first, (quarters,), 0, CAP + 1)
    second = jax.random.randint(key_second, (quarters,), CAP - first, CAP + 1)
    counts = jnp.stack([jnp.full((quarters,), CAP, jnp.int32), first, second, 2 * CAP - first - second], axis=-1)
    labels = jax.vmap(lambda subkey: jax.random.permutation(subkey, groups))(jax.random.split(key_label, rows_dp * CUBES))
    labels = jnp.broadcast_to(labels.reshape(rows_dp, 1, CUBES, groups), (rows_dp, groups, CUBES, groups)).reshape(quarters, groups)
    ends = jnp.cumsum(counts, axis=-1)
    position = jnp.arange(QUART)
    segment = jnp.sum((position[None, :, None] >= ends[:, None, :]).astype(jnp.int32), axis=-1)
    ordered = jnp.take_along_axis(labels, segment, axis=-1)
    shuffle = jax.vmap(lambda subkey: jax.random.permutation(subkey, QUART))(jax.random.split(key_shuffle, quarters))
    mixed = jnp.take_along_axis(ordered, shuffle, axis=-1)
    return mixed.reshape(TOKENS).astype(jnp.int32)


def plant(values, own_key, low, high):
    longest = values.shape.index(max(values.shape))
    spots = []
    for shift in (0, 1):
        where = [jax.random.randint(jax.random.fold_in(own_key, axis), (), 0, length) for axis, length in enumerate(values.shape)]
        where[longest] = (where[longest] + shift) % values.shape[longest]
        spots.append(tuple(where))
    return values.at[spots[0]].set(low).at[spots[1]].set(high)


def shard_levels(key, shape, cuts, smallest, top_value):
    level, own = 1.0, jax.random.fold_in(key, 6)
    for dim, blocks in cuts:
        draws = jnp.exp(jax.random.uniform(jax.random.fold_in(own, dim), (blocks,), jnp.float32, smallest / len(cuts), top_value / len(cuts)))
        level = level * jnp.repeat(draws, shape[dim] // blocks).reshape([-1 if axis == dim else 1 for axis in range(len(shape))])
    return level


def noise(rng, dims, scale, limit, cuts=(), kind=jnp.bfloat16):
    entries = jax.random.normal(rng, dims, jnp.float32) * scale
    if len(cuts) > 0:
        entries = shard_levels(rng, dims, cuts, -0.22, 0.18) * entries
    return jnp.clip(entries, min=-limit, max=limit).astype(kind)


def setup_inputs(seed: int = 0) -> dict:
    splits = jax.random.split(jax.random.key(seed), 14)
    enc = noise(splits[0], (TOKENS, D), 1.0, 6.0, ((0, 32),))
    visible = plant((jax.random.randint(splits[1], (TOKENS,), 0, 10) < 9).astype(jnp.int32), jax.random.fold_in(splits[1], 1), 0, 1)
    band_group = draw_band_group(jax.random.fold_in(splits[13], 71), 0)
    cotangent = noise(splits[3], (TOKENS, D), 1.0, 6.0, ((0, 32),))
    ln1_gain = jnp.clip(1.0 + 0.1 * jax.random.normal(splits[4], (D,), jnp.float32), 0.5, 1.5)
    ln1_bias = noise(splits[5], (D,), 0.5, 3.0, (), jnp.float32)
    w_qkv = noise(splits[6], (D, 3 * D), D ** -0.5, 0.25)
    w_out = noise(splits[7], (D, D), (D // 32) ** -0.5, 1.5)
    ln2_gain = jnp.clip(1.0 + 0.1 * jax.random.normal(splits[8], (D,), jnp.float32), 0.5, 1.5)
    ln2_bias = noise(splits[9], (D,), 0.5, 3.0, (), jnp.float32)
    w_up = noise(splits[10], (D, FF), D ** -0.5, 0.25)
    w_down = noise(splits[11], (FF, D), FF ** -0.5, 0.125)
    mask_token = noise(splits[12], (D,), 1.0, 5.0, (), jnp.float32)
    return {"enc": enc, "visible": visible, "band_group": band_group, "cotangent": cotangent, "ln1_gain": ln1_gain, "ln1_bias": ln1_bias, "w_qkv": w_qkv, "w_out": w_out, "ln2_gain": ln2_gain, "ln2_bias": ln2_bias, "w_up": w_up, "w_down": w_down, "mask_token": mask_token}


EPS = 1e-05
NEG = -1e+30

@jax.custom_vjp
def low(v):
    return lax.optimization_barrier(v.astype(jnp.bfloat16)).astype(jnp.float32)

@jax.custom_vjp
def low_back(v):
    return v

def low_keep(v):
    return (low(v), None)

def low_pass(kept, grad):
    return (grad,)

def back_keep(v):
    return (v, None)

def back_low(kept, grad):
    return (low(grad),)
low.defvjp(low_keep, low_pass)
low_back.defvjp(back_keep, back_low)

def layer_norm(values, gain, offset):
    centre = values - lax.optimization_barrier(jnp.mean(values, axis=-1, keepdims=True))
    spread = lax.optimization_barrier(jnp.mean(centre * centre, axis=-1, keepdims=True))
    return centre * lax.rsqrt(spread + EPS) * gain + offset

def product(left, right):
    return jnp.dot(left, right, precision=lax.Precision.HIGHEST, preferred_element_type=jnp.float32)

def slot_tables(band_ids):
    onehot = (band_ids[:, :, None] == jnp.arange(N_GROUP, dtype=jnp.int32)[None, None, :]).astype(jnp.int32)
    ranks = lax.optimization_barrier(jnp.sum((jnp.cumsum(onehot, axis=1) - onehot) * onehot, axis=-1))
    places = band_ids * SET + jnp.arange(N_GROUP, dtype=jnp.int32)[:, None] * CAP + ranks
    places = places.reshape(CUBE_TOK).astype(jnp.int32)
    table = jnp.full((N_GROUP * SET,), CUBE_TOK, jnp.int32).at[places].set(jnp.arange(CUBE_TOK, dtype=jnp.int32))
    return (table, places)

def cube_layer(params, encoded, shown, table, places):
    ln1_gain, ln1_bias, w_qkv, w_out, ln2_gain, ln2_bias, w_up, w_down, mask_token = params
    width = encoded.shape[1]
    start_rows = jnp.where(shown[:, None] == 1, encoded, mask_token[None, :])
    normed = low_back(low(layer_norm(start_rows, ln1_gain, ln1_bias)))
    projected = product(normed, w_qkv)
    queries = low_back(low(projected[:, :width]))
    key_rows = low_back(low(projected[:, width:2 * width]))
    value_rows = low_back(low(projected[:, 2 * width:]))

    def to_sets(rows):
        padded = jnp.concatenate([rows, jnp.zeros((1, width), jnp.float32)], axis=0)
        return padded[table].reshape(N_GROUP, SET, HEADS, HD)
    live = (table < CUBE_TOK).reshape(N_GROUP, SET)
    raw = jnp.einsum('gqhd,gkhd->ghqk', to_sets(queries), to_sets(key_rows), precision=lax.Precision.HIGHEST)
    scores = low_back(raw * HD ** (-0.5))
    scores = jnp.where(live[:, None, None, :], scores, NEG)
    top = lax.optimization_barrier(jnp.max(scores, axis=-1, keepdims=True))
    expo = jnp.exp(scores - top)
    probs = expo / lax.optimization_barrier(jnp.sum(expo, axis=-1, keepdims=True))
    attended = jnp.einsum('ghqk,gkhd->gqhd', low(probs), to_sets(value_rows), precision=lax.Precision.HIGHEST)
    attended = low_back(low(attended.reshape(N_GROUP * SET, width)))
    gathered = attended[places]
    middle = start_rows + low_back(product(gathered, w_out))
    second = low(layer_norm(middle, ln2_gain, ln2_bias))
    hidden = low_back(product(second, w_up))
    active = low(jax.nn.gelu(hidden, approximate=True))
    return middle + product(active, w_down)

def reference(enc, visible, band_group, cotangent, ln1_gain, ln1_bias, w_qkv, w_out, ln2_gain, ln2_bias, w_up, w_down, mask_token):
    params = tuple((weight.astype(jnp.float32) for weight in (ln1_gain, ln1_bias, w_qkv, w_out, ln2_gain, ln2_bias, w_up, w_down, mask_token)))

    def arrange(array):
        tail = array.shape[1:]
        blocks = array.reshape((N_DP, N_GROUP, CUBES, QUART) + tail)
        return jnp.moveaxis(blocks, 2, 1).reshape((N_DP * CUBES, CUBE_TOK) + tail)

    def restore(array):
        tail = array.shape[2:]
        blocks = array.reshape((N_DP, CUBES, N_GROUP, QUART) + tail)
        return jnp.moveaxis(blocks, 1, 2).reshape((TOKENS,) + tail)

    def cube_step(totals, pieces):
        encoded, shown, band_ids, cotan = pieces
        table, places = slot_tables(band_ids.reshape(N_GROUP, QUART))

        def forward(weights, rows):
            return cube_layer(weights, rows, shown, table, places)
        result, pullback = jax.vjp(forward, params, encoded.astype(jnp.float32))
        weight_grads, row_grads = pullback(cotan.astype(jnp.float32))
        totals = jax.tree.map(lambda left, right: left + right, totals, weight_grads)
        return (totals, (result.astype(jnp.bfloat16), row_grads.astype(jnp.bfloat16)))
    zeros = jax.tree.map(jnp.zeros_like, params)
    totals, (outputs, enc_grads) = lax.scan(cube_step, zeros, (arrange(enc), arrange(visible), arrange(band_group), arrange(cotangent)))
    return (restore(outputs), restore(enc_grads), totals[0], totals[1], totals[2], totals[3], totals[4], totals[5], totals[6], totals[7], totals[8])
```

```python
import functools
import jax
import jax.numpy as jnp
from jax import lax
from jax.experimental import pallas as pl
from jax.experimental.pallas import tpu as pltpu
from jax.sharding import PartitionSpec as P

HEADS = 16
CUBE_TOK = 1536
EPS = 1e-05
LOG2E = 1.4426950408889634
LN2 = 0.6931471805599453
FLOOR = -1e20
MASKED = -1e30

NN = (((1,), (0,)), ((), ()))
NT = (((1,), (1,)), ((), ()))
TN = (((0,), (0,)), ((), ()))
MESH = pl.DeviceIdType.MESH
BF = jnp.bfloat16
F32 = jnp.float32


def dot(left, right, dims=NN):
    return lax.dot_general(left, right, dims, preferred_element_type=F32)


def norm_stats(values):
    centre = values - jnp.mean(values, axis=-1, keepdims=True)
    spread = jnp.mean(centre * centre, axis=-1, keepdims=True)
    recip = lax.rsqrt(spread + EPS)
    return centre * recip, recip


def norm_back(grad_rows, normal, recip, gain):
    scaled = grad_rows * gain
    return recip * (
        scaled
        - jnp.mean(scaled, axis=-1, keepdims=True)
        - normal * jnp.mean(scaled * normal, axis=-1, keepdims=True)
    )


def onehot(dest_row, slots):
    rows = lax.broadcasted_iota(jnp.int32, (slots, dest_row.shape[1]), 0)
    return jnp.where(rows == dest_row, 1.0, 0.0).astype(BF)


def peer(bits):
    me = lax.axis_index("group")
    for bit in bits:
        me = me + (1 - 2 * (lax.rem(me // bit, 2))) * bit
    return (lax.axis_index("dp"), me)


def copy_to(src, dst, sems, index, device):
    return pltpu.make_async_remote_copy(
        src_ref=src, dst_ref=dst, send_sem=sems[0].at[index], recv_sem=sems[1].at[index],
        device_id=device, device_id_type=MESH,
    )


def greet(devices):
    barrier = pltpu.get_barrier_semaphore()
    for device in devices:
        pl.semaphore_signal(barrier, inc=1, device_id=device, device_id_type=MESH)
    pl.semaphore_wait(barrier, len(devices))


def own_dest(ids, capacity, groups):
    tokens = ids.shape[1]
    upper = (
        lax.broadcasted_iota(jnp.int32, (tokens, tokens), 0)
        < lax.broadcasted_iota(jnp.int32, (tokens, tokens), 1)
    )
    upper = jnp.where(upper, 1.0, 0.0).astype(BF)
    total = jnp.zeros(ids.shape, F32)
    for group in range(groups):
        hit = jnp.where(ids == group, 1.0, 0.0)
        ranks = dot(hit.astype(BF), upper)
        total = total + hit * (ranks + float(group * capacity))
    return total.astype(jnp.int32)


def forward_kernel(
    enc, visible, ids, gain, offset, mask_token, w_qkv,
    att, normed, dest, kv, kaug, qt, ot, lse,
    w_mine, wq_t, qbd, vt, away, sems_in, sems_dest, sems_fwd, sems_att,
):
    cubes, quarter = normed.shape[1], normed.shape[2]
    width = enc.shape[1]
    half = width // 2
    groups = kv.shape[1]
    cap = qt.shape[3] // 2
    slots = groups * cap
    hd = width // HEADS
    pack = 128
    per = pack // hd
    packs = half // pack
    factor = LOG2E * hd ** -0.5
    sibling, across, cross = peer((1,)), peer((2,)), peer((1, 2))
    parity = lax.rem(lax.axis_index("group"), 2)

    greet((sibling, across, cross))

    dest[0] = own_dest(ids[...], cap, groups)
    to_peers = []
    for index, device in enumerate((sibling, across, cross)):
        item = copy_to(dest.at[0], dest.at[index + 1], sems_dest, index, device)
        item.start()
        to_peers.append(item)

    def own_rows(c, _):
        rows = enc[pl.ds(c * quarter, quarter), :].astype(F32)
        shown = visible[pl.ds(c * quarter, quarter), :] == 1
        rows = jnp.where(shown, rows, mask_token[...])
        normal, _ = norm_stats(rows)
        normed[0, c] = (normal * gain[...] + offset[...]).astype(BF)
        copy_to(normed.at[0, c], normed.at[2, c], sems_in, cubes + c, across).start()
        copy_to(normed.at[0, c], normed.at[1, c], sems_in, c, sibling).start()
        return 0

    lax.fori_loop(0, cubes, own_rows, 0)

    for part in range(3):
        start = pl.multiple_of(part * width + parity * half, half)
        w_mine[:, part * half:(part + 1) * half] = w_qkv[:, pl.ds(start, half)]
    wq_t[...] = w_mine[:, :half].T

    one_row = lax.broadcasted_iota(jnp.int32, (16, per * 2 * cap), 0)
    for p in range(packs):
        qbd[p] = jnp.zeros(qbd.shape[1:], BF)
        qbd[p, pack:pack + 16, :] = jnp.where(one_row == 0, 1.0, 0.0).astype(BF)
        vt[p, pack:pack + 16, :] = jnp.ones((16, vt.shape[2]), BF)

    def project(r, c):
        rows = normed[r, c]
        row = dest[r, pl.ds(c, 1), :]
        hot = onehot(row, slots)
        values = dot(rows, w_mine[:, half:]).astype(BF)
        placed = dot(hot, values).astype(BF)
        lane = lax.broadcasted_iota(jnp.int32, (cap, 128), 1)
        place = lax.broadcasted_iota(jnp.int32, (cap, 128), 0)
        for s in range(groups):
            kv[c, s, r * cap:(r + 1) * cap, :] = placed[s * cap:(s + 1) * cap, :]
            inside = jnp.logical_and(row >= s * cap, row < (s + 1) * cap)
            count = jnp.sum(jnp.where(inside, 1, 0), axis=1, keepdims=True)
            bias = jnp.where(place < count, 0.0, MASKED)
            extra = jnp.where(lane == 0, bias, jnp.where(lane < 4, 1.0, 0.0))
            kaug[c, s, r * cap:(r + 1) * cap, :] = extra.astype(BF)
        if r < 2:
            queries = (dot(wq_t[...], rows, NT) * factor).astype(BF)
            spread = dot(queries, hot, NT).astype(BF)
            for s in range(groups):
                qt[c, s, :, r * cap:(r + 1) * cap] = spread[:, s * cap:(s + 1) * cap]

    def near_rows(c, _):
        project(0, c)
        copy_to(normed.at[0, c], normed.at[1, c], sems_in, c, sibling).wait_recv()
        project(1, c)
        return 0

    for item in to_peers:
        item.wait_recv()
    lax.fori_loop(0, cubes, near_rows, 0)

    def attend(c, s):
        for p in range(packs):
            lanes = slice(p * pack, (p + 1) * pack)
            for j in range(per):
                qbd[p, j * hd:(j + 1) * hd, j * 2 * cap:(j + 1) * 2 * cap] = qt[
                    c, s, p * pack + j * hd:p * pack + (j + 1) * hd, :]
            vt[p, :pack, :] = kv[c, s, :, half + p * pack:half + (p + 1) * pack].T
            keys = jnp.concatenate([kv[c, s, :, lanes], kaug[c, s]], axis=1)
            scores = dot(keys, qbd[p])
            top = jnp.maximum(jnp.max(scores, axis=0, keepdims=True), FLOOR)
            probs = jnp.exp2(scores - top).astype(BF)
            mixed = dot(vt[p], probs)
            total = jnp.maximum(mixed[pack:pack + 1, :], 1e-30)
            lse[c, s, p:p + 1, :] = top + jnp.log2(total)
            scale = 1.0 / total
            for j in range(per):
                cols = slice(j * 2 * cap, (j + 1) * 2 * cap)
                ot[c, s, p * pack + j * hd:p * pack + (j + 1) * hd, :] = (
                    mixed[j * hd:(j + 1) * hd, cols] * scale[:, cols]
                ).astype(BF)

    def cube(c, _):
        copy_to(normed.at[0, c], normed.at[2, c], sems_in, cubes + c, across).wait_recv()
        forward = copy_to(normed.at[2, c], normed.at[3, c], sems_fwd, c, sibling)
        forward.start()
        project(2, c)
        forward.wait_recv()
        project(3, c)

        def one(s, _):
            attend(c, s)
            return 0

        lax.fori_loop(0, groups, one, 0)
        for r in (1, 0):
            hot = onehot(dest[r, pl.ds(c, 1), :], slots)
            placed = jnp.concatenate(
                [ot[c, s, :, r * cap:(r + 1) * cap] for s in range(groups)], axis=1)
            rows = dot(placed, hot).astype(BF)
            if r == 1:
                away[c] = rows
                copy_to(away.at[c], att.at[c, pl.ds(pl.multiple_of(parity * half, half), half), :],
                        sems_att, c, sibling).start()
            else:
                att[c, pl.ds(pl.multiple_of(parity * half, half), half), :] = rows
        return 0

    lax.fori_loop(0, cubes, cube, 0)

    def finish(c, _):
        copy_to(away.at[c], att.at[c, pl.ds(pl.multiple_of(parity * half, half), half), :],
                sems_att, c, sibling).wait()
        copy_to(normed.at[0, c], normed.at[2, c], sems_in, cubes + c, across).wait_send()
        copy_to(normed.at[0, c], normed.at[1, c], sems_in, c, sibling).wait_send()
        copy_to(normed.at[2, c], normed.at[3, c], sems_fwd, c, sibling).wait_send()
        return 0

    lax.fori_loop(0, cubes, finish, 0)
    for item in to_peers:
        item.wait_send()


def forward_call(enc, visible, ids, gain, offset, mask_token, w_qkv, cubes, groups):
    tokens, width = enc.shape
    quarter = tokens // cubes
    cap = quarter // 3
    half = width // 2
    packs = half // 128
    wide = (128 // (width // HEADS)) * 2 * cap
    vmem = pl.BlockSpec(memory_space=pltpu.VMEM)
    shape = jax.ShapeDtypeStruct
    dma = pltpu.SemaphoreType.DMA
    return pl.pallas_call(
        forward_kernel,
        out_shape=(
            shape((cubes, width, quarter), BF),
            shape((groups, cubes, quarter, width), BF),
            shape((groups, 8, quarter), jnp.int32),
            shape((cubes, groups, groups * cap, width), BF),
            shape((cubes, groups, groups * cap, 128), BF),
            shape((cubes, groups, half, 2 * cap), BF),
            shape((cubes, groups, half, 2 * cap), BF),
            shape((cubes, groups, 8, wide), F32),
        ),
        in_specs=[vmem] * 7,
        out_specs=(vmem,) * 8,
        scratch_shapes=[
            pltpu.VMEM((width, 3 * half), BF),
            pltpu.VMEM((half, width), BF),
            pltpu.VMEM((packs, 256, wide), BF),
            pltpu.VMEM((packs, 144, groups * cap), BF),
            pltpu.VMEM((cubes, half, quarter), BF),
            (dma((2 * cubes,)), dma((2 * cubes,))),
            (dma((3,)), dma((3,))),
            (dma((cubes,)), dma((cubes,))),
            (dma((cubes,)), dma((cubes,))),
        ],
        compiler_params=pltpu.CompilerParams(
            collective_id=0, has_side_effects=True, vmem_limit_bytes=60 * 2**20),
        name="forward",
    )(enc, visible, ids, gain, offset, mask_token, w_qkv)


def pieces(values):
    high = values.astype(BF)
    rest = values - high.astype(F32)
    mid = rest.astype(BF)
    low = (rest - mid.astype(F32)).astype(BF)
    return high, mid, low


def backward_kernel(
    grad_att, kv, kaug, qt, ot, lse, normed, dest, w_qkv, enc, visible, mask_token, gain, grad_middle,
    grad_enc, grad_qkv, small,
    w_mine, near, dot_slots, qbd, dobd, grad_kv, grad_qt, own_sum, out_sib, in_sib, out_fwd, in_fwd,
    out_across, in_across, sems_near, sems_sib, sems_fwd, sems_across,
):
    cubes, width, quarter = grad_att.shape
    half = width // 2
    groups = kv.shape[1]
    cap = qt.shape[3] // 2
    slots = groups * cap
    hd = width // HEADS
    pack = 128
    per = pack // hd
    packs = half // pack
    factor = hd ** -0.5
    sibling, across = peer((1,)), peer((2,))
    parity = lax.rem(lax.axis_index("group"), 2)
    mine = pl.ds(pl.multiple_of(parity * half, half), half)
    theirs = pl.ds(pl.multiple_of((1 - parity) * half, half), half)

    greet((sibling, across))

    def send_near(c, _):
        copy_to(grad_att.at[c, theirs, :], near.at[c], sems_near, c, sibling).start()
        return 0

    lax.fori_loop(0, cubes, send_near, 0)

    for part in range(3):
        start = pl.multiple_of(part * width + parity * half, half)
        w_mine[:, part * half:(part + 1) * half] = w_qkv[:, pl.ds(start, half)]
    one_row = lax.broadcasted_iota(jnp.int32, (16, per * 2 * cap), 0)
    for p in range(packs):
        qbd[p] = jnp.zeros(qbd.shape[1:], BF)
        dobd[p] = jnp.zeros(dobd.shape[1:], BF)
    grad_qkv[...] = jnp.zeros(grad_qkv.shape, F32)
    small[...] = jnp.zeros(small.shape, F32)

    def extra_rows(first, values):
        high, mid, low = pieces(-values)
        rows = jnp.where(
            one_row == 0, first,
            jnp.where(one_row == 1, high.astype(F32),
                      jnp.where(one_row == 2, mid.astype(F32),
                                jnp.where(one_row == 3, low.astype(F32), 0.0))))
        return rows.astype(BF)

    def attend_back(c, s):
        for p in range(packs):
            lanes = slice(p * pack, (p + 1) * pack)
            deltas = []
            for j in range(per):
                rows = slice(p * pack + j * hd, p * pack + (j + 1) * hd)
                cols = slice(j * 2 * cap, (j + 1) * 2 * cap)
                qbd[p, j * hd:(j + 1) * hd, cols] = qt[c, s, rows, :]
                grads = dot_slots[c, s, rows, :]
                dobd[p, j * hd:(j + 1) * hd, cols] = grads
                deltas.append(jnp.sum(
                    grads.astype(F32) * ot[c, s, rows, :].astype(F32), axis=0, keepdims=True))
            qbd[p, pack:pack + 16, :] = extra_rows(1.0, lse[c, s, p:p + 1, :])
            dobd[p, pack:pack + 16, :] = extra_rows(0.0, jnp.concatenate(deltas, axis=1))
            extra = kaug[c, s]
            keys = kv[c, s, :, lanes]
            values = kv[c, s, :, half + p * pack:half + (p + 1) * pack]
            probs = jnp.exp2(dot(jnp.concatenate([keys, extra], axis=1), qbd[p]))
            centred = dot(jnp.concatenate([values, extra], axis=1), dobd[p])
            grad_scores = (probs * centred).astype(BF)
            grad_kv[s, :, half + p * pack:half + (p + 1) * pack] = dot(
                probs.astype(BF), dobd[p, :pack, :], NT).astype(BF)
            grad_kv[s, :, lanes] = (dot(grad_scores, qbd[p, :pack, :], NT) * LN2).astype(BF)
            mixed = dot(keys.T, grad_scores) * factor
            for j in range(per):
                rows = slice(p * pack + j * hd, p * pack + (j + 1) * hd)
                cols = slice(j * 2 * cap, (j + 1) * 2 * cap)
                grad_qt[s, rows, :] = mixed[j * hd:(j + 1) * hd, cols].astype(BF)

    def back_project(r, c):
        hot = onehot(dest[r, pl.ds(c, 1), :], slots)
        placed = jnp.concatenate(
            [grad_kv[s, r * cap:(r + 1) * cap, :] for s in range(groups)], axis=0)
        grads = dot(hot, placed, TN).astype(BF)
        if r < 2:
            queries = jnp.concatenate(
                [grad_qt[s, :, r * cap:(r + 1) * cap] for s in range(groups)], axis=1)
            queries = dot(queries, hot).T.astype(BF)
            grads = jnp.concatenate([queries, grads], axis=1)
            grad_qkv[...] += dot(normed[r, c], grads, TN)
            return dot(grads, w_mine[...], NT)
        grad_qkv[:, half:] += dot(normed[r, c], grads, TN)
        return dot(grads, w_mine[:, half:], NT)

    def cube(c, _):
        copy_to(grad_att.at[c, theirs, :], near.at[c], sems_near, c, sibling).wait_recv()
        for r in range(2):
            rows = grad_att[c, mine, :] if r == 0 else near[c]
            hot = onehot(dest[r, pl.ds(c, 1), :], slots)
            spread = dot(rows, hot, NT).astype(BF)
            for s in range(groups):
                dot_slots[c, s, :, r * cap:(r + 1) * cap] = spread[:, s * cap:(s + 1) * cap]

        def one(s, _):
            attend_back(c, s)
            return 0

        lax.fori_loop(0, groups, one, 0)
        out_fwd[c] = back_project(3, c).astype(BF)
        forward = copy_to(out_fwd.at[c], in_fwd.at[c], sems_fwd, c, sibling)
        forward.start()
        partial = back_project(2, c)
        forward.wait_recv()
        out_across[c] = (partial + in_fwd[c].astype(F32)).astype(BF)
        copy_to(out_across.at[c], in_across.at[c], sems_across, c, across).start()
        out_sib[c] = back_project(1, c).astype(BF)
        copy_to(out_sib.at[c], in_sib.at[c], sems_sib, c, sibling).start()
        own_sum[c] = back_project(0, c)
        return 0

    lax.fori_loop(0, cubes, cube, 0)

    def last(c, _):
        rows_at = pl.ds(c * quarter, quarter)
        copy_to(out_sib.at[c], in_sib.at[c], sems_sib, c, sibling).wait_recv()
        copy_to(out_across.at[c], in_across.at[c], sems_across, c, across).wait_recv()
        grads = own_sum[c] + in_sib[c].astype(F32) + in_across[c].astype(F32)
        shown = visible[rows_at, :] == 1
        start = jnp.where(shown, enc[rows_at, :].astype(F32), mask_token[...])
        normal, recip = norm_stats(start)
        small[0:1, :] += jnp.sum(grads * normal, axis=0, keepdims=True)
        small[1:2, :] += jnp.sum(grads, axis=0, keepdims=True)
        total = grad_middle[rows_at, :] + norm_back(grads, normal, recip, gain[...])
        grad_enc[rows_at, :] = jnp.where(shown, total, 0.0).astype(BF)
        small[2:3, :] += jnp.sum(jnp.where(shown, 0.0, total), axis=0, keepdims=True)
        copy_to(grad_att.at[c, theirs, :], near.at[c], sems_near, c, sibling).wait_send()
        copy_to(out_fwd.at[c], in_fwd.at[c], sems_fwd, c, sibling).wait_send()
        copy_to(out_sib.at[c], in_sib.at[c], sems_sib, c, sibling).wait_send()
        copy_to(out_across.at[c], in_across.at[c], sems_across, c, across).wait_send()
        return 0

    lax.fori_loop(0, cubes, last, 0)


def backward_call(grad_att, kv, kaug, qt, ot, lse, normed, dest, w_qkv, enc, visible, mask_token, gain, grad_middle):
    cubes, width, quarter = grad_att.shape
    groups = kv.shape[1]
    cap = quarter // 3
    half = width // 2
    packs = half // 128
    wide = (128 // (width // HEADS)) * 2 * cap
    vmem = pl.BlockSpec(memory_space=pltpu.VMEM)
    shape = jax.ShapeDtypeStruct
    dma = pltpu.SemaphoreType.DMA
    block = pltpu.VMEM((cubes, quarter, width), BF)
    pair = (dma((cubes,)), dma((cubes,)))
    return pl.pallas_call(
        backward_kernel,
        out_shape=(
            shape(enc.shape, BF),
            shape((width, 3 * half), F32),
            shape((8, width), F32),
        ),
        in_specs=[vmem] * 14,
        out_specs=(vmem,) * 3,
        scratch_shapes=[
            pltpu.VMEM((width, 3 * half), BF),
            pltpu.VMEM((cubes, half, quarter), BF),
            pltpu.VMEM((cubes, groups, half, 2 * cap), BF),
            pltpu.VMEM((packs, 256, wide), BF),
            pltpu.VMEM((packs, 256, wide), BF),
            pltpu.VMEM((groups, groups * cap, width), BF),
            pltpu.VMEM((groups, half, 2 * cap), BF),
            pltpu.VMEM((cubes, quarter, width), F32),
            block, block, block, block, block, block,
            pair, pair, pair, pair,
        ],
        compiler_params=pltpu.CompilerParams(
            collective_id=1, has_side_effects=True, vmem_limit_bytes=60 * 2**20),
        name="backward",
    )(grad_att, kv, kaug, qt, ot, lse, normed, dest, w_qkv, enc, visible, mask_token, gain, grad_middle)


def on_device(
    enc, visible, band_group, cotangent, ln1_gain, ln1_bias, w_qkv, w_out,
    ln2_gain, ln2_bias, w_up, w_down, mask_token,
):
    groups = lax.axis_size("group")
    tok_dev, width = enc.shape
    half = width // 2
    quarter = CUBE_TOK // groups
    cubes = tok_dev // quarter
    column = visible.reshape(tok_dev, 1)
    ids = jnp.pad(band_group.reshape(cubes, quarter), ((0, 8 - cubes), (0, 0)), constant_values=-1)
    gain1, mask_row = ln1_gain[None, :], mask_token[None, :]
    att, normed, dest, kv, kaug, qt, ot, lse = forward_call(
        enc, column, ids, gain1, ln1_bias[None, :], mask_row, w_qkv, cubes, groups)
    attended = att.transpose(0, 2, 1).reshape(tok_dev, width)
    start_rows = jnp.where(column == 1, enc.astype(F32), mask_row)
    middle = start_rows + dot(attended, w_out)
    normal2, recip2 = norm_stats(middle)
    second = (normal2 * ln2_gain + ln2_bias).astype(BF)
    hidden = dot(second, w_up)
    active_full, gelu_pull = jax.vjp(lambda v: jax.nn.gelu(v, approximate=True), hidden)
    active = active_full.astype(BF)
    out = (middle + dot(active, w_down)).astype(BF)
    grad_w_down = dot(active, cotangent, TN)
    grad_hidden = gelu_pull(dot(cotangent, w_down, NT))[0].astype(BF)
    grad_w_up = dot(second, grad_hidden, TN)
    grad_second = dot(grad_hidden, w_up, NT)
    grad_ln2_gain = jnp.sum(grad_second * normal2, axis=0)
    grad_ln2_bias = jnp.sum(grad_second, axis=0)
    grad_middle = cotangent.astype(F32) + norm_back(grad_second, normal2, recip2, ln2_gain)
    grad_branch = grad_middle.astype(BF)
    grad_w_out = dot(attended, grad_branch, TN)
    grad_attended = dot(w_out, grad_branch, NT).astype(BF)
    grad_att = grad_attended.reshape(width, cubes, quarter).transpose(1, 0, 2)
    grad_enc, grad_qkv, small = backward_call(
        grad_att, kv, kaug, qt, ot, lse, normed, dest, w_qkv, enc, column, mask_row, gain1, grad_middle)
    parity = lax.rem(lax.axis_index("group"), 2)
    mine = grad_qkv.reshape(width, 3, 1, half)
    blank = jnp.zeros_like(mine)
    grad_w_qkv = jnp.where(
        parity == 0, jnp.concatenate([mine, blank], axis=2), jnp.concatenate([blank, mine], axis=2)
    ).reshape(width, 3 * width)
    summed = lax.psum(
        (small[0], small[1], grad_w_qkv, grad_w_out, grad_ln2_gain, grad_ln2_bias, grad_w_up,
         grad_w_down, small[2]), ("dp", "group"))
    return (out, grad_enc) + tuple(summed)


def solution(mesh):
    rows, line = P(("dp", "group"), None), P(("dp", "group"))
    return jax.shard_map(
        on_device, mesh=mesh, in_specs=(rows, line, line, rows) + (P(),) * 9,
        out_specs=(rows, rows) + (P(),) * 9, check_vma=False)
```

```python
import functools
import jax
import jax.numpy as jnp
from jax import lax
from jax.experimental import pallas as pl
from jax.experimental.pallas import tpu as pltpu
from jax.sharding import PartitionSpec as P

HEADS = 16
CUBE_TOK = 1536
EPS = 1e-05
LOG2E = 1.4426950408889634
LN2 = 0.6931471805599453
FLOOR = -1e20
MASKED = -1e30

NN = (((1,), (0,)), ((), ()))
NT = (((1,), (1,)), ((), ()))
TN = (((0,), (0,)), ((), ()))
MESH = pl.DeviceIdType.MESH
BF = jnp.bfloat16
F32 = jnp.float32


def dot(left, right, dims=NN):
    return lax.dot_general(left, right, dims, preferred_element_type=F32)


def norm_stats(values):
    centre = values - jnp.mean(values, axis=-1, keepdims=True)
    spread = jnp.mean(centre * centre, axis=-1, keepdims=True)
    recip = lax.rsqrt(spread + EPS)
    return centre * recip, recip


def norm_back(grad_rows, normal, recip, gain):
    scaled = grad_rows * gain
    return recip * (
        scaled
        - jnp.mean(scaled, axis=-1, keepdims=True)
        - normal * jnp.mean(scaled * normal, axis=-1, keepdims=True)
    )


def onehot(dest_row, slots):
    rows = lax.broadcasted_iota(jnp.int32, (slots, dest_row.shape[1]), 0)
    return jnp.where(rows == dest_row, 1.0, 0.0).astype(BF)


def peer(bits):
    me = lax.axis_index("group")
    for bit in bits:
        me = me + (1 - 2 * (lax.rem(me // bit, 2))) * bit
    return (lax.axis_index("dp"), me)


def copy_to(src, dst, sems, index, device):
    return pltpu.make_async_remote_copy(
        src_ref=src, dst_ref=dst, send_sem=sems[0].at[index], recv_sem=sems[1].at[index],
        device_id=device, device_id_type=MESH,
    )


def greet(devices):
    barrier = pltpu.get_barrier_semaphore()
    for device in devices:
        pl.semaphore_signal(barrier, inc=1, device_id=device, device_id_type=MESH)
    pl.semaphore_wait(barrier, len(devices))


def own_dest(ids, capacity, groups):
    tokens = ids.shape[1]
    upper = (
        lax.broadcasted_iota(jnp.int32, (tokens, tokens), 0)
        < lax.broadcasted_iota(jnp.int32, (tokens, tokens), 1)
    )
    upper = jnp.where(upper, 1.0, 0.0).astype(BF)
    total = jnp.zeros(ids.shape, F32)
    for group in range(groups):
        hit = jnp.where(ids == group, 1.0, 0.0)
        ranks = dot(hit.astype(BF), upper)
        total = total + hit * (ranks + float(group * capacity))
    return total.astype(jnp.int32)


def forward_kernel(
    enc, visible, ids, gain, offset, mask_token, w_qkv,
    att, normed_out, dest, kv_out, kaug_out, qt_out, ot_out, lse,
    normed, kv, kaug, qt, ot, w_mine, wq_t, qbd, vt, away, sems_in, sems_dest, sems_fwd, sems_att, sems_store,
):
    cubes, quarter = normed.shape[1], normed.shape[2]
    width = enc.shape[1]
    half = width // 2
    groups = kv.shape[1]
    cap = qt.shape[3] // 2
    slots = groups * cap
    hd = width // HEADS
    pack = 128
    per = pack // hd
    packs = half // pack
    factor = LOG2E * hd ** -0.5
    sibling, across, cross = peer((1,)), peer((2,)), peer((1, 2))
    parity = lax.rem(lax.axis_index("group"), 2)

    greet((sibling, across, cross))

    dest[0] = own_dest(ids[...], cap, groups)
    to_peers = []
    for index, device in enumerate((sibling, across, cross)):
        item = copy_to(dest.at[0], dest.at[index + 1], sems_dest, index, device)
        item.start()
        to_peers.append(item)

    def own_rows(c, _):
        rows = enc[pl.ds(c * quarter, quarter), :].astype(F32)
        shown = visible[pl.ds(c * quarter, quarter), :] == 1
        rows = jnp.where(shown, rows, mask_token[...])
        normal, _ = norm_stats(rows)
        normed[0, c] = (normal * gain[...] + offset[...]).astype(BF)
        copy_to(normed.at[0, c], normed.at[2, c], sems_in, cubes + c, across).start()
        copy_to(normed.at[0, c], normed.at[1, c], sems_in, c, sibling).start()
        return 0

    lax.fori_loop(0, cubes, own_rows, 0)

    for part in range(3):
        start = pl.multiple_of(part * width + parity * half, half)
        w_mine[:, part * half:(part + 1) * half] = w_qkv[:, pl.ds(start, half)]
    wq_t[...] = w_mine[:, :half].T

    one_row = lax.broadcasted_iota(jnp.int32, (16, per * 2 * cap), 0)
    for p in range(packs):
        qbd[p] = jnp.zeros(qbd.shape[1:], BF)
        qbd[p, pack:pack + 16, :] = jnp.where(one_row == 0, 1.0, 0.0).astype(BF)
        vt[p, pack:pack + 16, :] = jnp.ones((16, vt.shape[2]), BF)

    def project(r, c):
        rows = normed[r, c]
        row = dest[r, pl.ds(c, 1), :]
        hot = onehot(row, slots)
        values = dot(rows, w_mine[:, half:]).astype(BF)
        placed = dot(hot, values).astype(BF)
        lane = lax.broadcasted_iota(jnp.int32, (cap, 128), 1)
        place = lax.broadcasted_iota(jnp.int32, (cap, 128), 0)
        for s in range(groups):
            kv[c, s, r * cap:(r + 1) * cap, :] = placed[s * cap:(s + 1) * cap, :]
            inside = jnp.logical_and(row >= s * cap, row < (s + 1) * cap)
            count = jnp.sum(jnp.where(inside, 1, 0), axis=1, keepdims=True)
            bias = jnp.where(place < count, 0.0, MASKED)
            extra = jnp.where(lane == 0, bias, jnp.where(lane < 4, 1.0, 0.0))
            kaug[c, s, r * cap:(r + 1) * cap, :] = extra.astype(BF)
        if r < 2:
            queries = (dot(wq_t[...], rows, NT) * factor).astype(BF)
            spread = dot(queries, hot, NT).astype(BF)
            for s in range(groups):
                qt[c, s, :, r * cap:(r + 1) * cap] = spread[:, s * cap:(s + 1) * cap]

    def near_rows(c, _):
        project(0, c)
        copy_to(normed.at[0, c], normed.at[1, c], sems_in, c, sibling).wait_recv()
        project(1, c)
        return 0

    for item in to_peers:
        item.wait_recv()
    lax.fori_loop(0, cubes, near_rows, 0)

    def attend(c, s):
        for p in range(packs):
            lanes = slice(p * pack, (p + 1) * pack)
            for j in range(per):
                qbd[p, j * hd:(j + 1) * hd, j * 2 * cap:(j + 1) * 2 * cap] = qt[
                    c, s, p * pack + j * hd:p * pack + (j + 1) * hd, :]
            vt[p, :pack, :] = kv[c, s, :, half + p * pack:half + (p + 1) * pack].T
            keys = jnp.concatenate([kv[c, s, :, lanes], kaug[c, s]], axis=1)
            scores = dot(keys, qbd[p])
            top = jnp.maximum(jnp.max(scores, axis=0, keepdims=True), FLOOR)
            probs = jnp.exp2(scores - top).astype(BF)
            mixed = dot(vt[p], probs)
            total = jnp.maximum(mixed[pack:pack + 1, :], 1e-30)
            lse[c, s, p:p + 1, :] = top + jnp.log2(total)
            scale = 1.0 / total
            for j in range(per):
                cols = slice(j * 2 * cap, (j + 1) * 2 * cap)
                ot[c, s, p * pack + j * hd:p * pack + (j + 1) * hd, :] = (
                    mixed[j * hd:(j + 1) * hd, cols] * scale[:, cols]
                ).astype(BF)

    def stores(c):
        pairs = [(kv.at[c], kv_out.at[c]), (kaug.at[c], kaug_out.at[c]), (qt.at[c], qt_out.at[c]),
                 (ot.at[c], ot_out.at[c]), (normed.at[:, c], normed_out.at[:, c])]
        return [pltpu.make_async_copy(src, dst, sems_store.at[c, k]) for k, (src, dst) in enumerate(pairs)]

    def cube(c, _):
        copy_to(normed.at[0, c], normed.at[2, c], sems_in, cubes + c, across).wait_recv()
        forward = copy_to(normed.at[2, c], normed.at[3, c], sems_fwd, c, sibling)
        forward.start()
        project(2, c)
        forward.wait_recv()
        project(3, c)

        def one(s, _):
            attend(c, s)
            return 0

        lax.fori_loop(0, groups, one, 0)
        for r in (1, 0):
            hot = onehot(dest[r, pl.ds(c, 1), :], slots)
            placed = jnp.concatenate(
                [ot[c, s, :, r * cap:(r + 1) * cap] for s in range(groups)], axis=1)
            rows = dot(placed, hot).astype(BF)
            if r == 1:
                away[c] = rows
                copy_to(away.at[c], att.at[c, pl.ds(pl.multiple_of(parity * half, half), half), :],
                        sems_att, c, sibling).start()
            else:
                att[c, pl.ds(pl.multiple_of(parity * half, half), half), :] = rows
        for item in stores(c):
            item.start()
        return 0

    lax.fori_loop(0, cubes, cube, 0)

    def finish(c, _):
        for item in stores(c):
            item.wait()
        copy_to(away.at[c], att.at[c, pl.ds(pl.multiple_of(parity * half, half), half), :],
                sems_att, c, sibling).wait()
        copy_to(normed.at[0, c], normed.at[2, c], sems_in, cubes + c, across).wait_send()
        copy_to(normed.at[0, c], normed.at[1, c], sems_in, c, sibling).wait_send()
        copy_to(normed.at[2, c], normed.at[3, c], sems_fwd, c, sibling).wait_send()
        return 0

    lax.fori_loop(0, cubes, finish, 0)
    for item in to_peers:
        item.wait_send()


def forward_call(enc, visible, ids, gain, offset, mask_token, w_qkv, cubes, groups):
    tokens, width = enc.shape
    quarter = tokens // cubes
    cap = quarter // 3
    half = width // 2
    packs = half // 128
    wide = (128 // (width // HEADS)) * 2 * cap
    vmem = pl.BlockSpec(memory_space=pltpu.VMEM)
    far = pl.BlockSpec(memory_space=pl.ANY)
    shape = jax.ShapeDtypeStruct
    dma = pltpu.SemaphoreType.DMA
    return pl.pallas_call(
        forward_kernel,
        out_shape=(
            shape((cubes, width, quarter), BF),
            shape((groups, cubes, quarter, width), BF),
            shape((groups, 8, quarter), jnp.int32),
            shape((cubes, groups, groups * cap, width), BF),
            shape((cubes, groups, groups * cap, 128), BF),
            shape((cubes, groups, half, 2 * cap), BF),
            shape((cubes, groups, half, 2 * cap), BF),
            shape((cubes, groups, 8, wide), F32),
        ),
        in_specs=[vmem] * 7,
        out_specs=(vmem, far, vmem, far, far, far, far, vmem),
        scratch_shapes=[
            pltpu.VMEM((groups, cubes, quarter, width), BF),
            pltpu.VMEM((cubes, groups, groups * cap, width), BF),
            pltpu.VMEM((cubes, groups, groups * cap, 128), BF),
            pltpu.VMEM((cubes, groups, half, 2 * cap), BF),
            pltpu.VMEM((cubes, groups, half, 2 * cap), BF),
            pltpu.VMEM((width, 3 * half), BF),
            pltpu.VMEM((half, width), BF),
            pltpu.VMEM((packs, 256, wide), BF),
            pltpu.VMEM((packs, 144, groups * cap), BF),
            pltpu.VMEM((cubes, half, quarter), BF),
            (dma((2 * cubes,)), dma((2 * cubes,))),
            (dma((3,)), dma((3,))),
            (dma((cubes,)), dma((cubes,))),
            (dma((cubes,)), dma((cubes,))),
            dma((cubes, 5)),
        ],
        compiler_params=pltpu.CompilerParams(
            collective_id=0, has_side_effects=True, vmem_limit_bytes=60 * 2**20),
        name="forward",
    )(enc, visible, ids, gain, offset, mask_token, w_qkv)


def pieces(values):
    high = values.astype(BF)
    rest = values - high.astype(F32)
    mid = rest.astype(BF)
    low = (rest - mid.astype(F32)).astype(BF)
    return high, mid, low


def bits_of(size):
    return [1 << k for k in range(size.bit_length() - 1)]


def bit_value(name):
    axis, bit = name
    return lax.rem(lax.axis_index(axis) // bit, 2)


def flip(names):
    place = {axis: lax.axis_index(axis) for axis in ("dp", "group")}
    for axis, bit in names:
        place[axis] = place[axis] + (1 - 2 * bit_value((axis, bit))) * bit
    return (place["dp"], place["group"])


class Butterfly:
    def __init__(self, acc, send, recv, out, sems, names, base=0):
        self.base = base
        self.acc, self.send, self.recv, self.out, self.sems = acc, send, recv, out, sems
        self.names = names
        self.rows = acc.shape[0]
        self.halvings = halvings_of(self.rows, len(names))
        self.stages = len(names)

    def start_row(self, k):
        low = 0
        for j in range(min(k, self.halvings)):
            low = low + bit_value(self.names[j]) * (self.rows >> (j + 1))
        return low

    def span(self, low, count):
        return pl.ds(pl.multiple_of(low, 16), count)

    def hop(self, k):
        if k < self.halvings:
            count = self.rows >> (k + 1)
            at = self.rows - (self.rows >> k)
        else:
            count = self.rows >> self.halvings
            at = self.rows + (k - self.halvings - 1) * count
        where = pl.ds(at, count)
        return copy_to(self.send.at[where], self.recv.at[where], self.sems, k, flip([self.names[k]])), where, count

    def reduce_start(self, k):
        item, where, count = self.hop(k)
        low = self.start_row(k)
        if k < self.halvings:
            low = low + (1 - bit_value(self.names[k])) * count
        self.send[where, :] = self.acc[self.span(low, count), :].astype(BF)
        item.start()

    def reduce_finish(self, k):
        item, where, count = self.hop(k)
        item.wait()
        if k < self.halvings:
            rows = self.span(self.start_row(k + 1), count)
            self.acc[rows, :] += self.recv[where, :].astype(F32)
        else:
            rows = self.span(self.start_row(k), count)
            self.acc[rows, :] = self.send[where, :].astype(F32) + self.recv[where, :].astype(F32)

    def settle(self):
        rows = self.span(self.start_row(self.halvings), self.rows >> self.halvings)
        self.out[self.out_span(self.start_row(self.halvings), self.rows >> self.halvings), :] = (
            self.acc[rows, :].astype(BF))

    def out_span(self, low, count):
        return self.span(self.base + low, count)

    def gather(self, k):
        rows = self.out_span(self.start_row(k + 1), self.rows >> (k + 1))
        return copy_to(self.out.at[rows, :], self.out.at[rows, :], self.sems, self.stages + k, flip([self.names[k]]))


def halvings_of(rows, stages):
    count = 0
    while count < stages and (rows >> (count + 1)) % 16 == 0:
        count += 1
    return count


def staging_rows(rows, stages):
    count = halvings_of(rows, stages)
    return rows + (stages - count - 1) * (rows >> count)


def steps_of(butterflies):
    stages, halvings = butterflies[0].stages, butterflies[0].halvings
    steps = []

    def first():
        for b in butterflies:
            b.reduce_start(0)

    steps.append(first)
    for k in range(stages):
        def step(k=k):
            for b in butterflies:
                b.reduce_finish(k)
                if k + 1 < stages:
                    b.reduce_start(k + 1)
                else:
                    b.settle()
                    b.gather(halvings - 1).start()
        steps.append(step)
    for k in range(halvings - 1, -1, -1):
        def step(k=k):
            for b in butterflies:
                b.gather(k).wait()
                if k > 0:
                    b.gather(k - 1).start()
        steps.append(step)
    return steps


def path_orders(names):
    head, tail = names[:3], names[3:]
    return [head[k:] + head[:k] + tail for k in range(3)]


def small_groups(n_dp, n_group):
    names = [("group", b) for b in bits_of(n_group)] + [("dp", b) for b in bits_of(n_dp)]
    groups = [names[:3]]
    rest = names[3:]
    while rest:
        groups.append(rest[:2])
        rest = rest[2:]
    return groups


class SmallSum:
    def __init__(self, buf, sems, names):
        self.buf, self.sems, self.names = buf, sems, names
        self.count = 1 << len(names)

    def copies(self):
        place = 0
        for k, name in enumerate(self.names):
            place = place + bit_value(name) * (1 << k)
        items = []
        for t in range(1, self.count):
            others = [name for k, name in enumerate(self.names) if (t >> k) & 1]
            items.append(copy_to(self.buf.at[place], self.buf.at[place], self.sems, t, flip(others)))
        return place, items

    def start(self, values):
        place, items = self.copies()
        self.buf[place] = values
        for item in items:
            item.start()

    def finish(self):
        _, items = self.copies()
        for item in items:
            item.wait()
        total = self.buf[0]
        for j in range(1, self.count):
            total = total + self.buf[j]
        return total


def backward_kernel(
    n_dp, n_group,
    grad_att, kv_in, kaug_in, qt_in, ot_in, lse, normed_in, dest, w_qkv, enc, visible, mask_token, gain,
    grad_middle, grad_ffn, grad_ln2,
    grad_enc, sum_ffn, sum_qkv, sum_small,
    kv_at, kaug_at, qt_at, ot_at, normed_at, sems_read,
    grad_qkv, small, own_ffn, acc_ffn, pair_ffn, send_ffn, recv_ffn, send_qkv, recv_qkv, small_bufs,
    sems_load, sems_core, sems_ffn, sems_qkv, sems_pair, sems_small,
    w_mine, near, dot_slots, qbd, dobd, grad_kv, grad_qt, own_sum, out_sib, in_sib, out_fwd, in_fwd,
    out_across, in_across, sems_near, sems_sib, sems_fwd, sems_across,
):
    cubes, width, quarter = grad_att.shape
    half = width // 2
    groups = kv_at.shape[1]
    cap = qt_at.shape[3] // 2
    slots = groups * cap
    hd = width // HEADS
    pack = 128
    per = pack // hd
    packs = half // pack
    factor = hd ** -0.5
    sibling, across = peer((1,)), peer((2,))
    parity = lax.rem(lax.axis_index("group"), 2)
    mine = pl.ds(pl.multiple_of(parity * half, half), half)
    theirs = pl.ds(pl.multiple_of((1 - parity) * half, half), half)

    core = ("group", 1)
    others = [("group", b) for b in bits_of(n_group) if b > 1] + [("dp", b) for b in bits_of(n_dp)]
    orders = path_orders(others)
    rows_half = sum_ffn.shape[1] // 2
    ffn = [
        Butterfly(acc_ffn.at[p], send_ffn.at[p], recv_ffn.at[p], sum_ffn.at[p],
                  (sems_ffn[0].at[p], sems_ffn[1].at[p]), orders[p], parity * rows_half) for p in range(3)]
    qkv = [
        Butterfly(grad_qkv.at[p], send_qkv.at[p], recv_qkv.at[p], sum_qkv.at[parity, p],
                  (sems_qkv[0].at[p], sems_qkv[1].at[p]), orders[p]) for p in range(3)]
    ffn_steps, qkv_steps = steps_of(ffn), steps_of(qkv)
    smalls = [
        SmallSum(small_bufs[k], (sems_small[0].at[k], sems_small[1].at[k]), names)
        for k, names in enumerate(small_groups(n_dp, n_group))]

    def ffn_rows(side):
        return pl.ds(pl.multiple_of(side * rows_half, 16), rows_half)

    core_copy = copy_to(grad_ffn.at[:, ffn_rows(1 - parity), :], pair_ffn, sems_core, 0, sibling)
    load_ffn = pltpu.make_async_copy(grad_ffn.at[:, ffn_rows(parity), :], own_ffn, sems_load.at[0])
    spread_ffn = copy_to(
        sum_ffn.at[:, ffn_rows(parity), :], sum_ffn.at[:, ffn_rows(parity), :], sems_core, 1, sibling)

    def core_first():
        core_copy.start()
        load_ffn.start()

    def core_second():
        load_ffn.wait()
        core_copy.wait()
        for p in range(3):
            acc_ffn[p] = own_ffn[p].astype(F32) + pair_ffn[p].astype(F32)
        ffn_inner[0]()

    def core_third():
        ffn_inner[-1]()
        spread_ffn.start()

    ffn_inner = ffn_steps
    ffn_steps = [core_first, core_second] + ffn_inner[1:-1] + [core_third, spread_ffn.wait]

    def reads(c):
        k = lax.rem(c, 2)
        pairs = [(kv_in.at[c], kv_at.at[k]), (kaug_in.at[c], kaug_at.at[k]), (qt_in.at[c], qt_at.at[k]),
                 (ot_in.at[c], ot_at.at[k]), (normed_in.at[:, c], normed_at.at[k])]
        return [pltpu.make_async_copy(src, dst, sems_read.at[k, n]) for n, (src, dst) in enumerate(pairs)]

    for c in range(min(2, cubes)):
        for item in reads(c):
            item.start()

    meets = {}
    for names in small_groups(n_dp, n_group):
        for t in range(1, 1 << len(names)):
            chosen = [name for k, name in enumerate(names) if (t >> k) & 1]
            meets[tuple(chosen)] = flip(chosen)
    for name in [core] + others:
        meets[(name,)] = flip([name])
    greet(list(meets.values()))
    ffn_steps[0]()

    def send_near(c, _):
        copy_to(grad_att.at[c, theirs, :], near.at[c], sems_near, c, sibling).start()
        return 0

    lax.fori_loop(0, cubes, send_near, 0)

    for part in range(3):
        start = pl.multiple_of(part * width + parity * half, half)
        w_mine[:, part * half:(part + 1) * half] = w_qkv[:, pl.ds(start, half)]
    one_row = lax.broadcasted_iota(jnp.int32, (16, per * 2 * cap), 0)
    for p in range(packs):
        qbd[p] = jnp.zeros(qbd.shape[1:], BF)
        dobd[p] = jnp.zeros(dobd.shape[1:], BF)
    grad_qkv[...] = jnp.zeros(grad_qkv.shape, F32)
    small[...] = jnp.zeros(small.shape, F32)
    small[3:5, :] = grad_ln2[...]

    def extra_rows(first, values):
        high, mid, low = pieces(-values)
        rows = jnp.where(
            one_row == 0, first,
            jnp.where(one_row == 1, high.astype(F32),
                      jnp.where(one_row == 2, mid.astype(F32),
                                jnp.where(one_row == 3, low.astype(F32), 0.0))))
        return rows.astype(BF)

    def attend_back(c, s):
        slot = lax.rem(c, 2)
        for p in range(packs):
            lanes = slice(p * pack, (p + 1) * pack)
            deltas = []
            for j in range(per):
                rows = slice(p * pack + j * hd, p * pack + (j + 1) * hd)
                cols = slice(j * 2 * cap, (j + 1) * 2 * cap)
                qbd[p, j * hd:(j + 1) * hd, cols] = qt_at[slot, s, rows, :]
                grads = dot_slots[s, rows, :]
                dobd[p, j * hd:(j + 1) * hd, cols] = grads
                deltas.append(jnp.sum(
                    grads.astype(F32) * ot_at[slot, s, rows, :].astype(F32), axis=0, keepdims=True))
            qbd[p, pack:pack + 16, :] = extra_rows(1.0, lse[c, s, p:p + 1, :])
            dobd[p, pack:pack + 16, :] = extra_rows(0.0, jnp.concatenate(deltas, axis=1))
            extra = kaug_at[slot, s]
            keys = kv_at[slot, s, :, lanes]
            values = kv_at[slot, s, :, half + p * pack:half + (p + 1) * pack]
            probs = jnp.exp2(dot(jnp.concatenate([keys, extra], axis=1), qbd[p]))
            centred = dot(jnp.concatenate([values, extra], axis=1), dobd[p])
            grad_scores = (probs * centred).astype(BF)
            grad_kv[s, :, half + p * pack:half + (p + 1) * pack] = dot(
                probs.astype(BF), dobd[p, :pack, :], NT).astype(BF)
            grad_kv[s, :, lanes] = (dot(grad_scores, qbd[p, :pack, :], NT) * LN2).astype(BF)
            mixed = dot(keys.T, grad_scores) * factor
            for j in range(per):
                rows = slice(p * pack + j * hd, p * pack + (j + 1) * hd)
                cols = slice(j * 2 * cap, (j + 1) * 2 * cap)
                grad_qt[s, rows, :] = mixed[j * hd:(j + 1) * hd, cols].astype(BF)

    def back_project(r, c):
        hot = onehot(dest[r, pl.ds(c, 1), :], slots)
        placed = jnp.concatenate(
            [grad_kv[s, r * cap:(r + 1) * cap, :] for s in range(groups)], axis=0)
        grads = dot(hot, placed, TN).astype(BF)
        if r < 2:
            queries = jnp.concatenate(
                [grad_qt[s, :, r * cap:(r + 1) * cap] for s in range(groups)], axis=1)
            queries = dot(queries, hot).T.astype(BF)
            grads = jnp.concatenate([queries, grads], axis=1)
            weight = dot(normed_at[lax.rem(c, 2), r], grads, TN)
            for k in range(3):
                grad_qkv[k] += weight[:, k * half:(k + 1) * half]
            return dot(grads, w_mine[...], NT)
        weight = dot(normed_at[lax.rem(c, 2), r], grads, TN)
        for k in range(2):
            grad_qkv[k + 1] += weight[:, k * half:(k + 1) * half]
        return dot(grads, w_mine[:, half:], NT)

    def prepare(c):
        for item in reads(c):
            item.wait()
        copy_to(grad_att.at[c, theirs, :], near.at[c], sems_near, c, sibling).wait_recv()
        for r in range(2):
            rows = grad_att[c, mine, :] if r == 0 else near[c]
            hot = onehot(dest[r, pl.ds(c, 1), :], slots)
            spread = dot(rows, hot, NT).astype(BF)
            for s in range(groups):
                dot_slots[s, :, r * cap:(r + 1) * cap] = spread[:, s * cap:(s + 1) * cap]

    def conclude(c):
        out_fwd[c] = back_project(3, c).astype(BF)
        forward = copy_to(out_fwd.at[c], in_fwd.at[c], sems_fwd, c, sibling)
        forward.start()
        partial = back_project(2, c)
        forward.wait_recv()
        out_across[c] = (partial + in_fwd[c].astype(F32)).astype(BF)
        copy_to(out_across.at[c], in_across.at[c], sems_across, c, across).start()
        out_sib[c] = back_project(1, c).astype(BF)
        copy_to(out_sib.at[c], in_sib.at[c], sems_sib, c, sibling).start()
        own_sum[c] = back_project(0, c).astype(BF)

        def more():
            for item in reads(c + 2):
                item.start()

        pl.when(c + 2 < cubes)(more)

    units = cubes * groups
    at = [max(1, (2 * k * units) // (2 * len(ffn_steps))) for k in range(len(ffn_steps))]
    at = FFN_AT if len(ffn_steps) == len(FFN_AT) else at

    def unit(u, _):
        c, s = u // groups, lax.rem(u, groups)
        pl.when(s == 0)(lambda: prepare(c))
        attend_back(c, s)
        pl.when(s == groups - 1)(lambda: conclude(c))
        for k in range(1, len(ffn_steps)):
            if at[k] < units:
                pl.when(u == at[k])(ffn_steps[k])
        return 0

    lax.fori_loop(0, units, unit, 0)
    qkv_steps[0]()
    left = [k for k in range(1, len(ffn_steps)) if at[k] >= units]
    for k in left:
        ffn_steps[k]()

    def last(c, _):
        rows_at = pl.ds(c * quarter, quarter)
        copy_to(out_sib.at[c], in_sib.at[c], sems_sib, c, sibling).wait_recv()
        copy_to(out_across.at[c], in_across.at[c], sems_across, c, across).wait_recv()
        grads = own_sum[c].astype(F32) + in_sib[c].astype(F32) + in_across[c].astype(F32)
        shown = visible[rows_at, :] == 1
        start = jnp.where(shown, enc[rows_at, :].astype(F32), mask_token[...])
        normal, recip = norm_stats(start)
        small[0:1, :] += jnp.sum(grads * normal, axis=0, keepdims=True)
        small[1:2, :] += jnp.sum(grads, axis=0, keepdims=True)
        total = grad_middle[rows_at, :] + norm_back(grads, normal, recip, gain[...])
        grad_enc[rows_at, :] = jnp.where(shown, total, 0.0).astype(BF)
        small[2:3, :] += jnp.sum(jnp.where(shown, 0.0, total), axis=0, keepdims=True)
        copy_to(grad_att.at[c, theirs, :], near.at[c], sems_near, c, sibling).wait_send()
        copy_to(out_fwd.at[c], in_fwd.at[c], sems_fwd, c, sibling).wait_send()
        copy_to(out_sib.at[c], in_sib.at[c], sems_sib, c, sibling).wait_send()
        copy_to(out_across.at[c], in_across.at[c], sems_across, c, across).wait_send()
        return 0

    fill = list(range(cubes))
    for k in range(1, len(qkv_steps)):
        if fill:
            last(fill.pop(0), 0)
            if not fill:
                smalls[0].start(small[...])
        qkv_steps[k]()
    pair = copy_to(sum_qkv.at[parity], sum_qkv.at[parity], sems_pair, 0, sibling)
    pair.start()
    for k, item in enumerate(smalls):
        total = item.finish()
        if k + 1 < len(smalls):
            smalls[k + 1].start(total)
    sum_small[...] = total
    pair.wait()


FFN_AT = [0, 1, 3, 4, 5, 6, 8, 9, 10, 11, 12]


def backward_call(
    grad_att, kv, kaug, qt, ot, lse, normed, dest, w_qkv, enc, visible, mask_token, gain, grad_middle,
    grad_ffn, grad_ln2, n_dp, n_group,
):
    cubes, width, quarter = grad_att.shape
    groups = kv.shape[1]
    cap = quarter // 3
    half = width // 2
    packs = half // 128
    wide = (128 // (width // HEADS)) * 2 * cap
    vmem = pl.BlockSpec(memory_space=pltpu.VMEM)
    far = pl.BlockSpec(memory_space=pl.ANY)
    shape = jax.ShapeDtypeStruct
    dma = pltpu.SemaphoreType.DMA
    block = pltpu.VMEM((cubes, quarter, width), BF)
    pair = (dma((cubes,)), dma((cubes,)))
    bits = len(bits_of(n_dp)) + len(bits_of(n_group))
    rows = 3 * width
    small = small_groups(n_dp, n_group)
    ffn_rows, qkv_rows = staging_rows(rows // 2, bits - 1), staging_rows(width, bits - 1)

    def sems(stages):
        return (dma((3, 2 * stages)), dma((3, 2 * stages)))

    return pl.pallas_call(
        functools.partial(backward_kernel, n_dp, n_group),
        out_shape=(
            shape(enc.shape, BF),
            shape((3, rows, width), BF),
            shape((2, 3, width, half), BF),
            shape((8, width), F32),
        ),
        in_specs=[vmem] + [far] * 4 + [vmem, far] + [vmem] * 7 + [far, vmem],
        out_specs=(vmem,) * 4,
        scratch_shapes=[
            pltpu.VMEM((2,) + kv.shape[1:], BF),
            pltpu.VMEM((2,) + kaug.shape[1:], BF),
            pltpu.VMEM((2,) + qt.shape[1:], BF),
            pltpu.VMEM((2,) + ot.shape[1:], BF),
            pltpu.VMEM((2, groups, quarter, width), BF),
            dma((2, 5)),
            pltpu.VMEM((3, width, half), F32),
            pltpu.VMEM((8, width), F32),
            pltpu.VMEM((3, rows // 2, width), BF),
            pltpu.VMEM((3, rows // 2, width), F32),
            pltpu.VMEM((3, rows // 2, width), BF),
            pltpu.VMEM((3, ffn_rows, width), BF),
            pltpu.VMEM((3, ffn_rows, width), BF),
            pltpu.VMEM((3, qkv_rows, half), BF),
            pltpu.VMEM((3, qkv_rows, half), BF),
            tuple(pltpu.VMEM((1 << len(names), 8, width), F32) for names in small),
            dma((1,)),
            (dma((2,)), dma((2,))),
            sems(bits - 1),
            sems(bits - 1),
            (dma((1,)), dma((1,))),
            (dma((len(small), 8)), dma((len(small), 8))),
            pltpu.VMEM((width, 3 * half), BF),
            pltpu.VMEM((cubes, half, quarter), BF),
            pltpu.VMEM((groups, half, 2 * cap), BF),
            pltpu.VMEM((packs, 256, wide), BF),
            pltpu.VMEM((packs, 256, wide), BF),
            pltpu.VMEM((groups, groups * cap, width), BF),
            pltpu.VMEM((groups, half, 2 * cap), BF),
            block, block, block, block, block, block, block,
            pair, pair, pair, pair,
        ],
        compiler_params=pltpu.CompilerParams(
            collective_id=1, has_side_effects=True, vmem_limit_bytes=63 * 2**20),
        name="backward",
    )(grad_att, kv, kaug, qt, ot, lse, normed, dest, w_qkv, enc, visible, mask_token, gain, grad_middle,
      grad_ffn, grad_ln2)


def on_device(
    enc, visible, band_group, cotangent, ln1_gain, ln1_bias, w_qkv, w_out,
    ln2_gain, ln2_bias, w_up, w_down, mask_token,
):
    groups = lax.axis_size("group")
    tok_dev, width = enc.shape
    half = width // 2
    quarter = CUBE_TOK // groups
    cubes = tok_dev // quarter
    column = visible.reshape(tok_dev, 1)
    ids = jnp.pad(band_group.reshape(cubes, quarter), ((0, 8 - cubes), (0, 0)), constant_values=-1)
    gain1, mask_row = ln1_gain[None, :], mask_token[None, :]
    att, normed, dest, kv, kaug, qt, ot, lse = forward_call(
        enc, column, ids, gain1, ln1_bias[None, :], mask_row, w_qkv, cubes, groups)
    attended = att.transpose(0, 2, 1).reshape(tok_dev, width)
    start_rows = jnp.where(column == 1, enc.astype(F32), mask_row)
    middle = start_rows + dot(attended, w_out)
    normal2, recip2 = norm_stats(middle)
    second = (normal2 * ln2_gain + ln2_bias).astype(BF)
    hidden = dot(second, w_up)
    active_full, gelu_pull = jax.vjp(lambda v: jax.nn.gelu(v, approximate=True), hidden)
    active = active_full.astype(BF)
    out = (middle + dot(active, w_down)).astype(BF)
    grad_w_down = dot(active, cotangent, TN)
    grad_hidden = gelu_pull(dot(cotangent, w_down, NT))[0].astype(BF)
    grad_w_up = dot(second, grad_hidden, TN)
    grad_second = dot(grad_hidden, w_up, NT)
    grad_ln2_gain = jnp.sum(grad_second * normal2, axis=0)
    grad_ln2_bias = jnp.sum(grad_second, axis=0)
    grad_middle = cotangent.astype(F32) + norm_back(grad_second, normal2, recip2, ln2_gain)
    grad_branch = grad_middle.astype(BF)
    grad_w_out = dot(attended, grad_branch, TN)
    grad_attended = dot(w_out, grad_branch, NT).astype(BF)
    grad_att = grad_attended.reshape(width, cubes, quarter).transpose(1, 0, 2)
    grad_ffn = jnp.concatenate([
        grad_w_up.reshape(width, 4, width).transpose(1, 0, 2).reshape(4 * width, width), grad_w_down, grad_w_out,
    ], axis=0).astype(BF).reshape(3, 3 * width, width)
    grad_enc, sum_ffn, sum_qkv, small = backward_call(
        grad_att, kv, kaug, qt, ot, lse, normed, dest, w_qkv, enc, column, mask_row, gain1, grad_middle,
        grad_ffn, jnp.stack([grad_ln2_gain, grad_ln2_bias]),
        lax.axis_size("dp"), groups)
    blocks = sum_ffn.reshape(9, width, width)
    sum_up = blocks[:4].transpose(1, 0, 2).reshape(width, 4 * width).astype(F32)
    sum_down = blocks[4:8].reshape(4 * width, width).astype(F32)
    sum_out = blocks[8].astype(F32)
    sum_w_qkv = sum_qkv.transpose(2, 1, 0, 3).reshape(width, 3 * width).astype(F32)
    return (
        out, grad_enc, small[0], small[1], sum_w_qkv, sum_out, small[3], small[4], sum_up, sum_down, small[2])


def solution(mesh):
    rows, line = P(("dp", "group"), None), P(("dp", "group"))
    return jax.shard_map(
        on_device, mesh=mesh, in_specs=(rows, line, line, rows) + (P(),) * 9,
        out_specs=(rows, rows) + (P(),) * 9, check_vma=False)
```

```python
import functools
import jax
import jax.numpy as jnp
from jax import lax
from jax.experimental import pallas as pl
from jax.experimental.pallas import tpu as pltpu
from jax.sharding import PartitionSpec as P

HEADS = 16
CUBE_TOK = 1536
EPS = 1e-05
LOG2E = 1.4426950408889634
LN2 = 0.6931471805599453
GELU_A = 0.7978845608028654
GELU_B = 0.7978845608028654 * 0.044715
FLOOR = -1e20
MASKED = -1e30

NN = (((1,), (0,)), ((), ()))
NT = (((1,), (1,)), ((), ()))
TN = (((0,), (0,)), ((), ()))
MESH = pl.DeviceIdType.MESH
BF = jnp.bfloat16
F32 = jnp.float32


def dot(left, right, dims=NN):
    return lax.dot_general(left, right, dims, preferred_element_type=F32)


def norm_stats(values):
    centre = values - jnp.mean(values, axis=-1, keepdims=True)
    spread = jnp.mean(centre * centre, axis=-1, keepdims=True)
    recip = lax.rsqrt(spread + EPS)
    return centre * recip, recip


def norm_back(grad_rows, normal, recip, gain):
    scaled = grad_rows * gain
    return recip * (
        scaled
        - jnp.mean(scaled, axis=-1, keepdims=True)
        - normal * jnp.mean(scaled * normal, axis=-1, keepdims=True)
    )


def onehot(dest_row, slots):
    rows = lax.broadcasted_iota(jnp.int32, (slots, dest_row.shape[1]), 0)
    return jnp.where(rows == dest_row, 1.0, 0.0).astype(BF)


def peer(bits):
    me = lax.axis_index("group")
    for bit in bits:
        me = me + (1 - 2 * (lax.rem(me // bit, 2))) * bit
    return (lax.axis_index("dp"), me)


def copy_to(src, dst, sems, index, device):
    return pltpu.make_async_remote_copy(
        src_ref=src, dst_ref=dst, send_sem=sems[0].at[index], recv_sem=sems[1].at[index],
        device_id=device, device_id_type=MESH,
    )


def greet(devices):
    barrier = pltpu.get_barrier_semaphore()
    for device in devices:
        pl.semaphore_signal(barrier, inc=1, device_id=device, device_id_type=MESH)
    pl.semaphore_wait(barrier, len(devices))


def own_dest(ids, capacity, groups):
    tokens = ids.shape[1]
    upper = (
        lax.broadcasted_iota(jnp.int32, (tokens, tokens), 0)
        < lax.broadcasted_iota(jnp.int32, (tokens, tokens), 1)
    )
    upper = jnp.where(upper, 1.0, 0.0).astype(BF)
    total = jnp.zeros(ids.shape, F32)
    for group in range(groups):
        hit = jnp.where(ids == group, 1.0, 0.0)
        ranks = dot(hit.astype(BF), upper)
        total = total + hit * (ranks + float(group * capacity))
    return total.astype(jnp.int32)


def forward_kernel(
    enc, visible, ids, gain, offset, mask_token, w_qkv, cot, w_out, w_up, w_down, gain2, offset2,
    out, normed_out, dest, kv_out, kaug_out, qt_out, ot_out, lse, grad_att, near, middle_out, ffn_out, grad_ln2,
    att, acc, grad_middle, turn, sems_turn,
    normed, kv, kaug, qt, ot, w_mine, wq_t, qbd, vt, away, sems_in, sems_dest, sems_fwd, sems_att, sems_store,
):
    cubes, quarter = normed.shape[1], normed.shape[2]
    width = enc.shape[1]
    half = width // 2
    groups = kv.shape[1]
    cap = qt.shape[3] // 2
    slots = groups * cap
    hd = width // HEADS
    pack = 128
    per = pack // hd
    packs = half // pack
    factor = LOG2E * hd ** -0.5
    sibling, across, cross = peer((1,)), peer((2,)), peer((1, 2))
    parity = lax.rem(lax.axis_index("group"), 2)

    mine = pl.ds(pl.multiple_of(parity * half, half), half)
    theirs = pl.ds(pl.multiple_of((1 - parity) * half, half), half)
    blocks = w_up.shape[1] // width

    greet((sibling, across, cross))

    dest[0] = own_dest(ids[...], cap, groups)
    to_peers = []
    for index, device in enumerate((sibling, across, cross)):
        item = copy_to(dest.at[0], dest.at[index + 1], sems_dest, index, device)
        item.start()
        to_peers.append(item)

    def start_rows(c):
        rows = enc[pl.ds(c * quarter, quarter), :].astype(F32)
        shown = visible[pl.ds(c * quarter, quarter), :] == 1
        return jnp.where(shown, rows, mask_token[...])

    def own_rows(c, _):
        normal, _ = norm_stats(start_rows(c))
        normed[0, c] = (normal * gain[...] + offset[...]).astype(BF)
        copy_to(normed.at[0, c], normed.at[2, c], sems_in, cubes + c, across).start()
        copy_to(normed.at[0, c], normed.at[1, c], sems_in, c, sibling).start()
        return 0

    lax.fori_loop(0, cubes, own_rows, 0)

    for part in range(3):
        start = pl.multiple_of(part * width + parity * half, half)
        w_mine[:, part * half:(part + 1) * half] = w_qkv[:, pl.ds(start, half)]
    wq_t[...] = w_mine[:, :half].T

    one_row = lax.broadcasted_iota(jnp.int32, (16, per * 2 * cap), 0)
    for p in range(packs):
        qbd[p] = jnp.zeros(qbd.shape[1:], BF)
        qbd[p, pack:pack + 16, :] = jnp.where(one_row == 0, 1.0, 0.0).astype(BF)
        vt[p, pack:pack + 16, :] = jnp.ones((16, vt.shape[2]), BF)

    def project(r, c):
        rows = normed[r, c]
        row = dest[r, pl.ds(c, 1), :]
        hot = onehot(row, slots)
        values = dot(rows, w_mine[:, half:]).astype(BF)
        placed = dot(hot, values).astype(BF)
        lane = lax.broadcasted_iota(jnp.int32, (cap, 128), 1)
        place = lax.broadcasted_iota(jnp.int32, (cap, 128), 0)
        for s in range(groups):
            kv[c, s, r * cap:(r + 1) * cap, :] = placed[s * cap:(s + 1) * cap, :]
            inside = jnp.logical_and(row >= s * cap, row < (s + 1) * cap)
            count = jnp.sum(jnp.where(inside, 1, 0), axis=1, keepdims=True)
            bias = jnp.where(place < count, 0.0, MASKED)
            extra = jnp.where(lane == 0, bias, jnp.where(lane < 4, 1.0, 0.0))
            kaug[c, s, r * cap:(r + 1) * cap, :] = extra.astype(BF)
        if r < 2:
            queries = (dot(wq_t[...], rows, NT) * factor).astype(BF)
            spread = dot(queries, hot, NT).astype(BF)
            for s in range(groups):
                qt[c, s, :, r * cap:(r + 1) * cap] = spread[:, s * cap:(s + 1) * cap]

    def near_rows(c, _):
        project(0, c)
        copy_to(normed.at[0, c], normed.at[1, c], sems_in, c, sibling).wait_recv()
        project(1, c)
        return 0

    for item in to_peers:
        item.wait_recv()
    lax.fori_loop(0, cubes, near_rows, 0)

    def attend(c, s):
        for p in range(packs):
            lanes = slice(p * pack, (p + 1) * pack)
            for j in range(per):
                qbd[p, j * hd:(j + 1) * hd, j * 2 * cap:(j + 1) * 2 * cap] = qt[
                    c, s, p * pack + j * hd:p * pack + (j + 1) * hd, :]
            vt[p, :pack, :] = kv[c, s, :, half + p * pack:half + (p + 1) * pack].T
            keys = jnp.concatenate([kv[c, s, :, lanes], kaug[c, s]], axis=1)
            scores = dot(keys, qbd[p])
            top = jnp.maximum(jnp.max(scores, axis=0, keepdims=True), FLOOR)
            probs = jnp.exp2(scores - top).astype(BF)
            mixed = dot(vt[p], probs)
            total = jnp.maximum(mixed[pack:pack + 1, :], 1e-30)
            lse[c, s, p:p + 1, :] = top + jnp.log2(total)
            scale = 1.0 / total
            for j in range(per):
                cols = slice(j * 2 * cap, (j + 1) * 2 * cap)
                ot[c, s, p * pack + j * hd:p * pack + (j + 1) * hd, :] = (
                    mixed[j * hd:(j + 1) * hd, cols] * scale[:, cols]
                ).astype(BF)

    def stores(c):
        pairs = [(kv.at[c], kv_out.at[c]), (kaug.at[c], kaug_out.at[c]), (qt.at[c], qt_out.at[c]),
                 (ot.at[c], ot_out.at[c]), (normed.at[:, c], normed_out.at[:, c])]
        return [pltpu.make_async_copy(src, dst, sems_store.at[c, k]) for k, (src, dst) in enumerate(pairs)]

    def attended_copy(c):
        return copy_to(away.at[c], att.at[c, mine, :], sems_att, c, sibling)

    def turn_copy(c):
        return copy_to(turn.at[c], near.at[c], sems_turn, c, sibling)

    def feed_forward(c):
        rows_at = pl.ds(c * quarter, quarter)
        attended_copy(c).wait_recv()
        attended = att[c]
        middle = start_rows(c) + dot(attended, w_out[...], TN)
        normal, recip = norm_stats(middle)
        second = (normal * gain2[...] + offset2[...]).astype(BF)
        cotan = cot[rows_at, :]

        def block(j, carry):
            result, grads = carry
            cols = pl.ds(pl.multiple_of(j * width, width), width)
            hidden = dot(second, w_up[:, cols])
            square = hidden * hidden
            tanh = jnp.tanh(hidden * (GELU_A + GELU_B * square))
            slope = 0.5 * (1.0 + tanh)
            active = (hidden * slope).astype(BF)
            slope = slope + 0.5 * hidden * (1.0 - tanh * tanh) * (GELU_A + 3.0 * GELU_B * square)
            grad_hidden = (dot(cotan, w_down[cols, :], NT) * slope).astype(BF)
            acc[blocks + j] += dot(active, cotan, TN)
            acc[j] += dot(second, grad_hidden, TN)
            return (result + dot(active, w_down[cols, :]), grads + dot(grad_hidden, w_up[:, cols], NT))

        result, grads = lax.fori_loop(0, blocks, block, (middle, jnp.zeros(middle.shape, F32)))
        out[rows_at, :] = result.astype(BF)
        grad_ln2[0:1, :] += jnp.sum(grads * normal, axis=0, keepdims=True)
        grad_ln2[1:2, :] += jnp.sum(grads, axis=0, keepdims=True)
        total = cotan.astype(F32) + norm_back(grads, normal, recip, gain2[...])
        grad_middle[c] = total
        branch = total.astype(BF)
        acc[2 * blocks] += dot(attended, branch)
        back = dot(w_out[...], branch, NT).astype(BF)
        grad_att[c] = back
        turn[c] = grad_att[c, theirs, :]
        turn_copy(c).start()
        pltpu.make_async_copy(grad_middle.at[c], middle_out.at[rows_at, :], sems_store.at[c, 5]).start()

    def cube(c, _):
        copy_to(normed.at[0, c], normed.at[2, c], sems_in, cubes + c, across).wait_recv()
        forward = copy_to(normed.at[2, c], normed.at[3, c], sems_fwd, c, sibling)
        forward.start()
        project(2, c)
        forward.wait_recv()
        project(3, c)

        def one(s, _):
            attend(c, s)
            return 0

        lax.fori_loop(0, groups, one, 0)
        for r in (1, 0):
            hot = onehot(dest[r, pl.ds(c, 1), :], slots)
            placed = jnp.concatenate(
                [ot[c, s, :, r * cap:(r + 1) * cap] for s in range(groups)], axis=1)
            rows = dot(placed, hot).astype(BF)
            if r == 1:
                away[c] = rows
                attended_copy(c).start()
            else:
                att[c, mine, :] = rows
        for item in stores(c):
            item.start()
        return 0

    for k in range(acc.shape[0]):
        acc[k] = jnp.zeros(acc.shape[1:], F32)
    grad_ln2[...] = jnp.zeros(grad_ln2.shape, F32)

    def cube_and_last(c, _):
        cube(c, 0)
        pl.when(c > 0)(lambda: feed_forward(c - 1))
        return 0

    lax.fori_loop(0, cubes, cube_and_last, 0)
    feed_forward(cubes - 1)
    for k in range(acc.shape[0]):
        ffn_out[k] = acc[k].astype(BF)

    def finish(c, _):
        rows_at = pl.ds(c * quarter, quarter)
        for item in stores(c):
            item.wait()
        pltpu.make_async_copy(grad_middle.at[c], middle_out.at[rows_at, :], sems_store.at[c, 5]).wait()
        attended_copy(c).wait_send()
        turn_copy(c).wait()
        copy_to(normed.at[0, c], normed.at[2, c], sems_in, cubes + c, across).wait_send()
        copy_to(normed.at[0, c], normed.at[1, c], sems_in, c, sibling).wait_send()
        copy_to(normed.at[2, c], normed.at[3, c], sems_fwd, c, sibling).wait_send()
        return 0

    lax.fori_loop(0, cubes, finish, 0)
    for item in to_peers:
        item.wait_send()


def forward_call(enc, visible, ids, gain, offset, mask_token, w_qkv, cot, w_out, w_up, w_down, gain2, offset2,
                 cubes, groups):
    tokens, width = enc.shape
    quarter = tokens // cubes
    cap = quarter // 3
    half = width // 2
    packs = half // 128
    blocks = w_up.shape[1] // width
    wide = (128 // (width // HEADS)) * 2 * cap
    vmem = pl.BlockSpec(memory_space=pltpu.VMEM)
    far = pl.BlockSpec(memory_space=pl.ANY)
    shape = jax.ShapeDtypeStruct
    dma = pltpu.SemaphoreType.DMA
    return pl.pallas_call(
        forward_kernel,
        out_shape=(
            shape((tokens, width), BF),
            shape((groups, cubes, quarter, width), BF),
            shape((groups, 8, quarter), jnp.int32),
            shape((cubes, groups, groups * cap, width), BF),
            shape((cubes, groups, groups * cap, 128), BF),
            shape((cubes, groups, half, 2 * cap), BF),
            shape((cubes, groups, half, 2 * cap), BF),
            shape((cubes, groups, 8, wide), F32),
            shape((cubes, width, quarter), BF),
            shape((cubes, half, quarter), BF),
            shape((tokens, width), F32),
            shape((2 * blocks + 1, width, width), BF),
            shape((2, width), F32),
        ),
        in_specs=[vmem] * 13,
        out_specs=(vmem, far, vmem, far, far, far, far, vmem, vmem, vmem, far, vmem, vmem),
        scratch_shapes=[
            pltpu.VMEM((cubes, width, quarter), BF),
            pltpu.VMEM((2 * blocks + 1, width, width), F32),
            pltpu.VMEM((cubes, quarter, width), F32),
            pltpu.VMEM((cubes, half, quarter), BF),
            (dma((cubes,)), dma((cubes,))),
            pltpu.VMEM((groups, cubes, quarter, width), BF),
            pltpu.VMEM((cubes, groups, groups * cap, width), BF),
            pltpu.VMEM((cubes, groups, groups * cap, 128), BF),
            pltpu.VMEM((cubes, groups, half, 2 * cap), BF),
            pltpu.VMEM((cubes, groups, half, 2 * cap), BF),
            pltpu.VMEM((width, 3 * half), BF),
            pltpu.VMEM((half, width), BF),
            pltpu.VMEM((packs, 256, wide), BF),
            pltpu.VMEM((packs, 144, groups * cap), BF),
            pltpu.VMEM((cubes, half, quarter), BF),
            (dma((2 * cubes,)), dma((2 * cubes,))),
            (dma((3,)), dma((3,))),
            (dma((cubes,)), dma((cubes,))),
            (dma((cubes,)), dma((cubes,))),
            dma((cubes, 6)),
        ],
        compiler_params=pltpu.CompilerParams(
            collective_id=0, has_side_effects=True, vmem_limit_bytes=63 * 2**20),
        name="forward",
    )(enc, visible, ids, gain, offset, mask_token, w_qkv, cot, w_out, w_up, w_down, gain2, offset2)


def pieces(values):
    high = values.astype(BF)
    rest = values - high.astype(F32)
    mid = rest.astype(BF)
    low = (rest - mid.astype(F32)).astype(BF)
    return high, mid, low


def bits_of(size):
    return [1 << k for k in range(size.bit_length() - 1)]


def bit_value(name):
    axis, bit = name
    return lax.rem(lax.axis_index(axis) // bit, 2)


def flip(names):
    place = {axis: lax.axis_index(axis) for axis in ("dp", "group")}
    for axis, bit in names:
        place[axis] = place[axis] + (1 - 2 * bit_value((axis, bit))) * bit
    return (place["dp"], place["group"])


class Butterfly:
    def __init__(self, acc, send, recv, out, sems, names, base=0):
        self.base = base
        self.acc, self.send, self.recv, self.out, self.sems = acc, send, recv, out, sems
        self.names = names
        self.rows = acc.shape[0]
        self.halvings = halvings_of(self.rows, len(names))
        self.stages = len(names)

    def start_row(self, k):
        low = 0
        for j in range(min(k, self.halvings)):
            low = low + bit_value(self.names[j]) * (self.rows >> (j + 1))
        return low

    def span(self, low, count):
        return pl.ds(pl.multiple_of(low, 16), count)

    def hop(self, k):
        if k < self.halvings:
            count = self.rows >> (k + 1)
            at = self.rows - (self.rows >> k)
        else:
            count = self.rows >> self.halvings
            at = self.rows + (k - self.halvings - 1) * count
        where = pl.ds(at, count)
        return copy_to(self.send.at[where], self.recv.at[where], self.sems, k, flip([self.names[k]])), where, count

    def reduce_start(self, k):
        item, where, count = self.hop(k)
        low = self.start_row(k)
        if k < self.halvings:
            low = low + (1 - bit_value(self.names[k])) * count
        self.send[where, :] = self.acc[self.span(low, count), :].astype(BF)
        item.start()

    def reduce_finish(self, k):
        item, where, count = self.hop(k)
        item.wait()
        if k < self.halvings:
            rows = self.span(self.start_row(k + 1), count)
            self.acc[rows, :] += self.recv[where, :].astype(F32)
        else:
            rows = self.span(self.start_row(k), count)
            self.acc[rows, :] = self.send[where, :].astype(F32) + self.recv[where, :].astype(F32)

    def settle(self):
        rows = self.span(self.start_row(self.halvings), self.rows >> self.halvings)
        self.out[self.out_span(self.start_row(self.halvings), self.rows >> self.halvings), :] = (
            self.acc[rows, :].astype(BF))

    def out_span(self, low, count):
        return self.span(self.base + low, count)

    def gather(self, k):
        rows = self.out_span(self.start_row(k + 1), self.rows >> (k + 1))
        return copy_to(self.out.at[rows, :], self.out.at[rows, :], self.sems, self.stages + k, flip([self.names[k]]))


def halvings_of(rows, stages):
    count = 0
    while count < stages and (rows >> (count + 1)) % 16 == 0:
        count += 1
    return count


def staging_rows(rows, stages):
    count = halvings_of(rows, stages)
    return rows + (stages - count - 1) * (rows >> count)


def steps_of(butterflies):
    stages, halvings = butterflies[0].stages, butterflies[0].halvings
    steps = []

    def first():
        for b in butterflies:
            b.reduce_start(0)

    steps.append(first)
    for k in range(stages):
        def step(k=k):
            for b in butterflies:
                b.reduce_finish(k)
                if k + 1 < stages:
                    b.reduce_start(k + 1)
                else:
                    b.settle()
                    b.gather(halvings - 1).start()
        steps.append(step)
    for k in range(halvings - 1, -1, -1):
        def step(k=k):
            for b in butterflies:
                b.gather(k).wait()
                if k > 0:
                    b.gather(k - 1).start()
        steps.append(step)
    return steps


def path_orders(names):
    head, tail = names[:3], names[3:]
    return [head[k:] + head[:k] + tail for k in range(3)]


def small_groups(n_dp, n_group):
    names = [("group", b) for b in bits_of(n_group)] + [("dp", b) for b in bits_of(n_dp)]
    groups = [names[:3]]
    rest = names[3:]
    while rest:
        groups.append(rest[:2])
        rest = rest[2:]
    return groups


class SmallSum:
    def __init__(self, buf, sems, names):
        self.buf, self.sems, self.names = buf, sems, names
        self.count = 1 << len(names)

    def copies(self):
        place = 0
        for k, name in enumerate(self.names):
            place = place + bit_value(name) * (1 << k)
        items = []
        for t in range(1, self.count):
            others = [name for k, name in enumerate(self.names) if (t >> k) & 1]
            items.append(copy_to(self.buf.at[place], self.buf.at[place], self.sems, t, flip(others)))
        return place, items

    def start(self, values):
        place, items = self.copies()
        self.buf[place] = values
        for item in items:
            item.start()

    def finish(self):
        _, items = self.copies()
        for item in items:
            item.wait()
        total = self.buf[0]
        for j in range(1, self.count):
            total = total + self.buf[j]
        return total


def backward_kernel(
    n_dp, n_group,
    grad_att, near, kv_in, kaug_in, qt_in, ot_in, lse, normed_in, dest, w_qkv, enc, visible, mask_token, gain,
    grad_middle, grad_ffn, grad_ln2,
    grad_enc, sum_ffn, sum_qkv, sum_small,
    kv_at, kaug_at, qt_at, ot_at, normed_at, sems_read,
    grad_qkv, small, own_ffn, acc_ffn, pair_ffn, send_ffn, recv_ffn, send_qkv, recv_qkv, small_bufs,
    sems_load, sems_core, sems_ffn, sems_qkv, sems_pair, sems_small,
    w_mine, dot_slots, qbd, dobd, grad_kv, grad_qt, own_sum, out_sib, in_sib, out_fwd, in_fwd,
    out_across, in_across, sems_sib, sems_fwd, sems_across,
):
    cubes, width, quarter = grad_att.shape
    half = width // 2
    groups = kv_at.shape[1]
    cap = qt_at.shape[3] // 2
    slots = groups * cap
    hd = width // HEADS
    pack = 128
    per = pack // hd
    packs = half // pack
    factor = hd ** -0.5
    sibling, across = peer((1,)), peer((2,))
    parity = lax.rem(lax.axis_index("group"), 2)
    mine = pl.ds(pl.multiple_of(parity * half, half), half)

    core = ("group", 1)
    others = [("group", b) for b in bits_of(n_group) if b > 1] + [("dp", b) for b in bits_of(n_dp)]
    orders = path_orders(others)
    rows_half = sum_ffn.shape[1] // 2
    ffn = [
        Butterfly(acc_ffn.at[p], send_ffn.at[p], recv_ffn.at[p], sum_ffn.at[p],
                  (sems_ffn[0].at[p], sems_ffn[1].at[p]), orders[p], parity * rows_half) for p in range(3)]
    qkv = [
        Butterfly(grad_qkv.at[p], send_qkv.at[p], recv_qkv.at[p], sum_qkv.at[parity, p],
                  (sems_qkv[0].at[p], sems_qkv[1].at[p]), orders[p]) for p in range(3)]
    ffn_steps, qkv_steps = steps_of(ffn), steps_of(qkv)
    smalls = [
        SmallSum(small_bufs[k], (sems_small[0].at[k], sems_small[1].at[k]), names)
        for k, names in enumerate(small_groups(n_dp, n_group))]

    def ffn_rows(side):
        return pl.ds(pl.multiple_of(side * rows_half, 16), rows_half)

    core_copy = copy_to(grad_ffn.at[:, ffn_rows(1 - parity), :], pair_ffn, sems_core, 0, sibling)
    load_ffn = pltpu.make_async_copy(grad_ffn.at[:, ffn_rows(parity), :], own_ffn, sems_load.at[0])
    spread_ffn = copy_to(
        sum_ffn.at[:, ffn_rows(parity), :], sum_ffn.at[:, ffn_rows(parity), :], sems_core, 1, sibling)

    def core_first():
        core_copy.start()
        load_ffn.start()

    def core_second():
        load_ffn.wait()
        core_copy.wait()
        for p in range(3):
            acc_ffn[p] = own_ffn[p].astype(F32) + pair_ffn[p].astype(F32)
        ffn_inner[0]()

    def core_third():
        ffn_inner[-1]()
        spread_ffn.start()

    ffn_inner = ffn_steps
    ffn_steps = [core_first, core_second] + ffn_inner[1:-1] + [core_third, spread_ffn.wait]

    def reads(c):
        k = lax.rem(c, 2)
        pairs = [(kv_in.at[c], kv_at.at[k]), (kaug_in.at[c], kaug_at.at[k]), (qt_in.at[c], qt_at.at[k]),
                 (ot_in.at[c], ot_at.at[k]), (normed_in.at[:, c], normed_at.at[k])]
        return [pltpu.make_async_copy(src, dst, sems_read.at[k, n]) for n, (src, dst) in enumerate(pairs)]

    for c in range(min(2, cubes)):
        for item in reads(c):
            item.start()

    meets = {}
    for names in small_groups(n_dp, n_group):
        for t in range(1, 1 << len(names)):
            chosen = [name for k, name in enumerate(names) if (t >> k) & 1]
            meets[tuple(chosen)] = flip(chosen)
    for name in [core] + others:
        meets[(name,)] = flip([name])
    greet(list(meets.values()))
    ffn_steps[0]()

    for part in range(3):
        start = pl.multiple_of(part * width + parity * half, half)
        w_mine[:, part * half:(part + 1) * half] = w_qkv[:, pl.ds(start, half)]
    one_row = lax.broadcasted_iota(jnp.int32, (16, per * 2 * cap), 0)
    for p in range(packs):
        qbd[p] = jnp.zeros(qbd.shape[1:], BF)
        dobd[p] = jnp.zeros(dobd.shape[1:], BF)
    grad_qkv[...] = jnp.zeros(grad_qkv.shape, F32)
    small[...] = jnp.zeros(small.shape, F32)
    small[3:5, :] = grad_ln2[...]

    def extra_rows(first, values):
        high, mid, low = pieces(-values)
        rows = jnp.where(
            one_row == 0, first,
            jnp.where(one_row == 1, high.astype(F32),
                      jnp.where(one_row == 2, mid.astype(F32),
                                jnp.where(one_row == 3, low.astype(F32), 0.0))))
        return rows.astype(BF)

    def attend_back(c, s):
        slot = lax.rem(c, 2)
        for p in range(packs):
            lanes = slice(p * pack, (p + 1) * pack)
            deltas = []
            for j in range(per):
                rows = slice(p * pack + j * hd, p * pack + (j + 1) * hd)
                cols = slice(j * 2 * cap, (j + 1) * 2 * cap)
                qbd[p, j * hd:(j + 1) * hd, cols] = qt_at[slot, s, rows, :]
                grads = dot_slots[s, rows, :]
                dobd[p, j * hd:(j + 1) * hd, cols] = grads
                deltas.append(jnp.sum(
                    grads.astype(F32) * ot_at[slot, s, rows, :].astype(F32), axis=0, keepdims=True))
            qbd[p, pack:pack + 16, :] = extra_rows(1.0, lse[c, s, p:p + 1, :])
            dobd[p, pack:pack + 16, :] = extra_rows(0.0, jnp.concatenate(deltas, axis=1))
            extra = kaug_at[slot, s]
            keys = kv_at[slot, s, :, lanes]
            values = kv_at[slot, s, :, half + p * pack:half + (p + 1) * pack]
            probs = jnp.exp2(dot(jnp.concatenate([keys, extra], axis=1), qbd[p]))
            centred = dot(jnp.concatenate([values, extra], axis=1), dobd[p])
            grad_scores = (probs * centred).astype(BF)
            grad_kv[s, :, half + p * pack:half + (p + 1) * pack] = dot(
                probs.astype(BF), dobd[p, :pack, :], NT).astype(BF)
            grad_kv[s, :, lanes] = (dot(grad_scores, qbd[p, :pack, :], NT) * LN2).astype(BF)
            mixed = dot(keys.T, grad_scores) * factor
            for j in range(per):
                rows = slice(p * pack + j * hd, p * pack + (j + 1) * hd)
                cols = slice(j * 2 * cap, (j + 1) * 2 * cap)
                grad_qt[s, rows, :] = mixed[j * hd:(j + 1) * hd, cols].astype(BF)

    def back_project(r, c):
        hot = onehot(dest[r, pl.ds(c, 1), :], slots)
        placed = jnp.concatenate(
            [grad_kv[s, r * cap:(r + 1) * cap, :] for s in range(groups)], axis=0)
        grads = dot(hot, placed, TN).astype(BF)
        if r < 2:
            queries = jnp.concatenate(
                [grad_qt[s, :, r * cap:(r + 1) * cap] for s in range(groups)], axis=1)
            queries = dot(queries, hot).T.astype(BF)
            grads = jnp.concatenate([queries, grads], axis=1)
            weight = dot(normed_at[lax.rem(c, 2), r], grads, TN)
            for k in range(3):
                grad_qkv[k] += weight[:, k * half:(k + 1) * half]
            return dot(grads, w_mine[...], NT)
        weight = dot(normed_at[lax.rem(c, 2), r], grads, TN)
        for k in range(2):
            grad_qkv[k + 1] += weight[:, k * half:(k + 1) * half]
        return dot(grads, w_mine[:, half:], NT)

    def prepare(c):
        for item in reads(c):
            item.wait()
        for r in range(2):
            rows = grad_att[c, mine, :] if r == 0 else near[c]
            hot = onehot(dest[r, pl.ds(c, 1), :], slots)
            spread = dot(rows, hot, NT).astype(BF)
            for s in range(groups):
                dot_slots[s, :, r * cap:(r + 1) * cap] = spread[:, s * cap:(s + 1) * cap]

    def conclude(c):
        out_fwd[c] = back_project(3, c).astype(BF)
        forward = copy_to(out_fwd.at[c], in_fwd.at[c], sems_fwd, c, sibling)
        forward.start()
        partial = back_project(2, c)
        forward.wait_recv()
        out_across[c] = (partial + in_fwd[c].astype(F32)).astype(BF)
        copy_to(out_across.at[c], in_across.at[c], sems_across, c, across).start()
        out_sib[c] = back_project(1, c).astype(BF)
        copy_to(out_sib.at[c], in_sib.at[c], sems_sib, c, sibling).start()
        own_sum[c] = back_project(0, c).astype(BF)

        def more():
            for item in reads(c + 2):
                item.start()

        pl.when(c + 2 < cubes)(more)

    units = cubes * groups
    at = [max(1, (2 * k * units) // (2 * len(ffn_steps))) for k in range(len(ffn_steps))]
    at = FFN_AT if len(ffn_steps) == len(FFN_AT) else at

    def unit(u, _):
        c, s = u // groups, lax.rem(u, groups)
        pl.when(s == 0)(lambda: prepare(c))
        attend_back(c, s)
        pl.when(s == groups - 1)(lambda: conclude(c))
        for k in range(1, len(ffn_steps)):
            if at[k] < units:
                pl.when(u == at[k])(ffn_steps[k])
        return 0

    lax.fori_loop(0, units, unit, 0)
    qkv_steps[0]()
    left = [k for k in range(1, len(ffn_steps)) if at[k] >= units]
    for k in left:
        ffn_steps[k]()

    def last(c, _):
        rows_at = pl.ds(c * quarter, quarter)
        copy_to(out_sib.at[c], in_sib.at[c], sems_sib, c, sibling).wait_recv()
        copy_to(out_across.at[c], in_across.at[c], sems_across, c, across).wait_recv()
        grads = own_sum[c].astype(F32) + in_sib[c].astype(F32) + in_across[c].astype(F32)
        shown = visible[rows_at, :] == 1
        start = jnp.where(shown, enc[rows_at, :].astype(F32), mask_token[...])
        normal, recip = norm_stats(start)
        small[0:1, :] += jnp.sum(grads * normal, axis=0, keepdims=True)
        small[1:2, :] += jnp.sum(grads, axis=0, keepdims=True)
        total = grad_middle[rows_at, :] + norm_back(grads, normal, recip, gain[...])
        grad_enc[rows_at, :] = jnp.where(shown, total, 0.0).astype(BF)
        small[2:3, :] += jnp.sum(jnp.where(shown, 0.0, total), axis=0, keepdims=True)
        copy_to(out_fwd.at[c], in_fwd.at[c], sems_fwd, c, sibling).wait_send()
        copy_to(out_sib.at[c], in_sib.at[c], sems_sib, c, sibling).wait_send()
        copy_to(out_across.at[c], in_across.at[c], sems_across, c, across).wait_send()
        return 0

    fill = list(range(cubes))
    for k in range(1, len(qkv_steps)):
        if fill:
            last(fill.pop(0), 0)
            if not fill:
                smalls[0].start(small[...])
        qkv_steps[k]()
    pair = copy_to(sum_qkv.at[parity], sum_qkv.at[parity], sems_pair, 0, sibling)
    pair.start()
    for k, item in enumerate(smalls):
        total = item.finish()
        if k + 1 < len(smalls):
            smalls[k + 1].start(total)
    sum_small[...] = total
    pair.wait()


FFN_AT = [0, 1, 3, 4, 5, 6, 8, 9, 10, 11, 12]


def backward_call(
    grad_att, near, kv, kaug, qt, ot, lse, normed, dest, w_qkv, enc, visible, mask_token, gain, grad_middle,
    grad_ffn, grad_ln2, n_dp, n_group,
):
    cubes, width, quarter = grad_att.shape
    groups = kv.shape[1]
    cap = quarter // 3
    half = width // 2
    packs = half // 128
    wide = (128 // (width // HEADS)) * 2 * cap
    vmem = pl.BlockSpec(memory_space=pltpu.VMEM)
    far = pl.BlockSpec(memory_space=pl.ANY)
    shape = jax.ShapeDtypeStruct
    dma = pltpu.SemaphoreType.DMA
    block = pltpu.VMEM((cubes, quarter, width), BF)
    pair = (dma((cubes,)), dma((cubes,)))
    bits = len(bits_of(n_dp)) + len(bits_of(n_group))
    rows = 3 * width
    small = small_groups(n_dp, n_group)
    ffn_rows, qkv_rows = staging_rows(rows // 2, bits - 1), staging_rows(width, bits - 1)

    def sems(stages):
        return (dma((3, 2 * stages)), dma((3, 2 * stages)))

    return pl.pallas_call(
        functools.partial(backward_kernel, n_dp, n_group),
        out_shape=(
            shape(enc.shape, BF),
            shape((3, rows, width), BF),
            shape((2, 3, width, half), BF),
            shape((8, width), F32),
        ),
        in_specs=[vmem] * 2 + [far] * 4 + [vmem, far] + [vmem] * 7 + [far, vmem],
        out_specs=(vmem,) * 4,
        scratch_shapes=[
            pltpu.VMEM((2,) + kv.shape[1:], BF),
            pltpu.VMEM((2,) + kaug.shape[1:], BF),
            pltpu.VMEM((2,) + qt.shape[1:], BF),
            pltpu.VMEM((2,) + ot.shape[1:], BF),
            pltpu.VMEM((2, groups, quarter, width), BF),
            dma((2, 5)),
            pltpu.VMEM((3, width, half), F32),
            pltpu.VMEM((8, width), F32),
            pltpu.VMEM((3, rows // 2, width), BF),
            pltpu.VMEM((3, rows // 2, width), F32),
            pltpu.VMEM((3, rows // 2, width), BF),
            pltpu.VMEM((3, ffn_rows, width), BF),
            pltpu.VMEM((3, ffn_rows, width), BF),
            pltpu.VMEM((3, qkv_rows, half), BF),
            pltpu.VMEM((3, qkv_rows, half), BF),
            tuple(pltpu.VMEM((1 << len(names), 8, width), F32) for names in small),
            dma((1,)),
            (dma((2,)), dma((2,))),
            sems(bits - 1),
            sems(bits - 1),
            (dma((1,)), dma((1,))),
            (dma((len(small), 8)), dma((len(small), 8))),
            pltpu.VMEM((width, 3 * half), BF),
            pltpu.VMEM((groups, half, 2 * cap), BF),
            pltpu.VMEM((packs, 256, wide), BF),
            pltpu.VMEM((packs, 256, wide), BF),
            pltpu.VMEM((groups, groups * cap, width), BF),
            pltpu.VMEM((groups, half, 2 * cap), BF),
            block, block, block, block, block, block, block,
            pair, pair, pair,
        ],
        compiler_params=pltpu.CompilerParams(
            collective_id=1, has_side_effects=True, vmem_limit_bytes=63 * 2**20),
        name="backward",
    )(grad_att, near, kv, kaug, qt, ot, lse, normed, dest, w_qkv, enc, visible, mask_token, gain, grad_middle,
      grad_ffn, grad_ln2)


def cast_kernel(ups, downs, outs, qkvs, up, down, out, qkv):
    width, half = outs.shape[1], qkvs.shape[3]
    for k in range(ups.shape[0]):
        up[:, k * width:(k + 1) * width] = ups[k].astype(F32)
    down[...] = downs[...].astype(F32)
    out[...] = outs[...].astype(F32)
    for part in range(3):
        for side in range(2):
            at = part * width + side * half
            qkv[:, at:at + half] = qkvs[side, part].astype(F32)


def cast_call(ffn, qkv):
    width = qkv.shape[2]
    blocks = ffn.shape[0] // (2 * width)
    steps = 8
    rows = width // steps
    tall = blocks * rows
    shape = jax.ShapeDtypeStruct
    return pl.pallas_call(
        cast_kernel,
        grid=(steps,),
        in_specs=[
            pl.BlockSpec((blocks, rows, width), lambda i: (0, i, 0)),
            pl.BlockSpec((tall, width), lambda i: (steps + i, 0)),
            pl.BlockSpec((rows, width), lambda i: (2 * blocks * steps + i, 0)),
            pl.BlockSpec((2, 3, rows, width // 2), lambda i: (0, 0, i, 0)),
        ],
        out_specs=[
            pl.BlockSpec((rows, blocks * width), lambda i: (i, 0)),
            pl.BlockSpec((tall, width), lambda i: (i, 0)),
            pl.BlockSpec((rows, width), lambda i: (i, 0)),
            pl.BlockSpec((rows, 3 * width), lambda i: (i, 0)),
        ],
        out_shape=(
            shape((width, blocks * width), F32),
            shape((blocks * width, width), F32),
            shape((width, width), F32),
            shape((width, 3 * width), F32),
        ),
        name="cast",
    )(ffn.reshape(2 * blocks + 1, width, width), ffn, ffn, qkv)


def on_device(
    enc, visible, band_group, cotangent, ln1_gain, ln1_bias, w_qkv, w_out,
    ln2_gain, ln2_bias, w_up, w_down, mask_token,
):
    groups = lax.axis_size("group")
    tok_dev, width = enc.shape
    quarter = CUBE_TOK // groups
    cubes = tok_dev // quarter
    column = visible.reshape(tok_dev, 1)
    ids = jnp.pad(band_group.reshape(cubes, quarter), ((0, 8 - cubes), (0, 0)), constant_values=-1)
    gain1, mask_row = ln1_gain[None, :], mask_token[None, :]
    (out, normed, dest, kv, kaug, qt, ot, lse, grad_att, near, grad_middle, grad_ffn, grad_ln2) = forward_call(
        enc, column, ids, gain1, ln1_bias[None, :], mask_row, w_qkv, cotangent, w_out, w_up, w_down,
        ln2_gain[None, :], ln2_bias[None, :], cubes, groups)
    grad_enc, sum_ffn, sum_qkv, small = backward_call(
        grad_att, near, kv, kaug, qt, ot, lse, normed, dest, w_qkv, enc, column, mask_row, gain1, grad_middle,
        grad_ffn.reshape(3, 3 * width, width), grad_ln2, lax.axis_size("dp"), groups)
    sum_up, sum_down, sum_out, sum_w_qkv = cast_call(sum_ffn.reshape(9 * width, width), sum_qkv)
    return (
        out, grad_enc, small[0], small[1], sum_w_qkv, sum_out, small[3], small[4], sum_up, sum_down, small[2])


def solution(mesh):
    rows, line = P(("dp", "group"), None), P(("dp", "group"))
    return jax.shard_map(
        on_device, mesh=mesh, in_specs=(rows, line, line, rows) + (P(),) * 9,
        out_specs=(rows, rows) + (P(),) * 9, check_vma=False)
```

```python
import functools
import jax
import jax.numpy as jnp
from jax import lax
from jax.experimental import pallas as pl
from jax.experimental.pallas import tpu as pltpu
from jax.sharding import PartitionSpec as P

HEADS = 16
CUBE_TOK = 1536
EPS = 1e-05
LOG2E = 1.4426950408889634
LN2 = 0.6931471805599453
GELU_A = 0.7978845608028654
GELU_B = 0.7978845608028654 * 0.044715
FLOOR = -1e20
MASKED = -1e30

NN = (((1,), (0,)), ((), ()))
NT = (((1,), (1,)), ((), ()))
TN = (((0,), (0,)), ((), ()))
MESH = pl.DeviceIdType.MESH
BF = jnp.bfloat16
F32 = jnp.float32


def dot(left, right, dims=NN):
    return lax.dot_general(left, right, dims, preferred_element_type=F32)


def norm_stats(values):
    centre = values - jnp.mean(values, axis=-1, keepdims=True)
    spread = jnp.mean(centre * centre, axis=-1, keepdims=True)
    recip = lax.rsqrt(spread + EPS)
    return centre * recip, recip


def norm_back(grad_rows, normal, recip, gain):
    scaled = grad_rows * gain
    return recip * (
        scaled
        - jnp.mean(scaled, axis=-1, keepdims=True)
        - normal * jnp.mean(scaled * normal, axis=-1, keepdims=True)
    )


def onehot(dest_row, slots):
    rows = lax.broadcasted_iota(jnp.int32, (slots, dest_row.shape[1]), 0)
    return jnp.where(rows == dest_row, 1.0, 0.0).astype(BF)


def peer(bits):
    me = lax.axis_index("group")
    for bit in bits:
        me = me + (1 - 2 * (lax.rem(me // bit, 2))) * bit
    return (lax.axis_index("dp"), me)


def copy_to(src, dst, sems, index, device):
    return pltpu.make_async_remote_copy(
        src_ref=src, dst_ref=dst, send_sem=sems[0].at[index], recv_sem=sems[1].at[index],
        device_id=device, device_id_type=MESH,
    )


def greet(devices):
    barrier = pltpu.get_barrier_semaphore()
    for device in devices:
        pl.semaphore_signal(barrier, inc=1, device_id=device, device_id_type=MESH)
    pl.semaphore_wait(barrier, len(devices))


def own_dest(ids, capacity, groups):
    tokens = ids.shape[1]
    upper = (
        lax.broadcasted_iota(jnp.int32, (tokens, tokens), 0)
        < lax.broadcasted_iota(jnp.int32, (tokens, tokens), 1)
    )
    upper = jnp.where(upper, 1.0, 0.0).astype(BF)
    total = jnp.zeros(ids.shape, F32)
    for group in range(groups):
        hit = jnp.where(ids == group, 1.0, 0.0)
        ranks = dot(hit.astype(BF), upper)
        total = total + hit * (ranks + float(group * capacity))
    return total.astype(jnp.int32)


def bits_of(size):
    return [1 << k for k in range(size.bit_length() - 1)]


def bit_value(name):
    axis, bit = name
    return lax.rem(lax.axis_index(axis) // bit, 2)


def flip(names):
    place = {axis: lax.axis_index(axis) for axis in ("dp", "group")}
    for axis, bit in names:
        place[axis] = place[axis] + (1 - 2 * bit_value((axis, bit))) * bit
    return (place["dp"], place["group"])


class Butterfly:
    def __init__(self, acc, send, recv, settled, out, sems, names):
        self.acc, self.send, self.recv, self.settled, self.out = acc, send, recv, settled, out
        self.sems, self.names = sems, names
        self.rows = acc.shape[0]
        self.halvings = halvings_of(self.rows, len(names))
        self.stages = len(names)

    def start_row(self, k):
        low = 0
        for j in range(min(k, self.halvings)):
            low = low + bit_value(self.names[j]) * (self.rows >> (j + 1))
        return low

    def span(self, low, count):
        return pl.ds(pl.multiple_of(low, 16), count)

    def hop(self, k):
        if k < self.halvings:
            count = self.rows >> (k + 1)
            at = self.rows - (self.rows >> k)
        else:
            count = self.rows >> self.halvings
            at = self.rows + (k - self.halvings - 1) * count
        where = pl.ds(at, count)
        return copy_to(self.send.at[where], self.recv.at[where], self.sems, k, flip([self.names[k]])), where, count

    def reduce_start(self, k):
        item, where, count = self.hop(k)
        low = self.start_row(k)
        if k < self.halvings:
            low = low + (1 - bit_value(self.names[k])) * count
        self.send[where, :] = self.acc[self.span(low, count), :].astype(BF)
        item.start()

    def reduce_finish(self, k):
        item, where, count = self.hop(k)
        item.wait()
        if k < self.halvings:
            rows = self.span(self.start_row(k + 1), count)
            self.acc[rows, :] += self.recv[where, :].astype(F32)
        else:
            rows = self.span(self.start_row(k), count)
            self.acc[rows, :] = self.send[where, :].astype(F32) + self.recv[where, :].astype(F32)

    def own_piece(self):
        return self.span(self.start_row(self.halvings), self.rows >> self.halvings)

    def keep(self):
        return pltpu.make_async_copy(
            self.settled, self.out.at[self.own_piece(), :], self.sems[0].at[self.stages + self.halvings])

    def settle(self):
        self.settled[...] = self.acc[self.own_piece(), :].astype(BF)
        self.keep().start()

    def gather(self, k):
        rows = self.span(self.start_row(k + 1), self.rows >> (k + 1))
        src = self.settled if k == self.halvings - 1 else self.out.at[rows, :]
        return copy_to(src, self.out.at[rows, :], self.sems, self.stages + k, flip([self.names[k]]))


def halvings_of(rows, stages):
    count = 0
    while count < stages and (rows >> (count + 1)) % 16 == 0:
        count += 1
    return count


def staging_rows(rows, stages):
    count = halvings_of(rows, stages)
    return rows + (stages - count - 1) * (rows >> count)


def reduce_steps(butterflies):
    stages = butterflies[0].stages

    def first():
        for b in butterflies:
            b.reduce_start(0)

    steps = [first]
    for k in range(stages):
        def step(k=k):
            for b in butterflies:
                b.reduce_finish(k)
                if k + 1 < stages:
                    b.reduce_start(k + 1)
                else:
                    b.settle()
        steps.append(step)
    return steps


def gather_steps(butterflies):
    halvings = max(b.halvings for b in butterflies)

    def first():
        for b in butterflies:
            b.gather(b.halvings - 1).start()

    steps = [first]
    for k in range(halvings - 1, -1, -1):
        def step(k=k):
            for b in butterflies:
                if k < b.halvings:
                    b.gather(k).wait()
                    if k == b.halvings - 1:
                        b.keep().wait()
                    if k > 0:
                        b.gather(k - 1).start()
        steps.append(step)
    return steps


def joined(before, after):
    def both():
        before[-1]()
        after[0]()

    return before[:-1] + [both] + after[1:]


def path_orders(names, count):
    head, tail = names[:count], names[count:]
    return [head[k:] + head[:k] + tail for k in range(count)]


def chip_bits(n_dp, n_group):
    return [("group", b) for b in bits_of(n_group) if b > 1] + [("dp", b) for b in bits_of(n_dp)]


def lanes_of(p):
    return slice(p * 128, (p + 1) * 128)


PARTS = 4

def small_groups(n_dp, n_group):
    names = [("group", b) for b in bits_of(n_group)] + [("dp", b) for b in bits_of(n_dp)]
    groups = [names[:3]]
    rest = names[3:]
    while rest:
        groups.append(rest[:2])
        rest = rest[2:]
    return groups


class SmallSum:
    def __init__(self, buf, sems, names):
        self.buf, self.sems, self.names = buf, sems, names
        self.count = 1 << len(names)

    def copies(self):
        place = 0
        for k, name in enumerate(self.names):
            place = place + bit_value(name) * (1 << k)
        items = []
        for t in range(1, self.count):
            others = [name for k, name in enumerate(self.names) if (t >> k) & 1]
            items.append(copy_to(self.buf.at[place], self.buf.at[place], self.sems, t, flip(others)))
        return place, items

    def start(self, values):
        place, items = self.copies()
        self.buf[place] = values
        for item in items:
            item.start()

    def finish(self):
        _, items = self.copies()
        for item in items:
            item.wait()
        total = self.buf[0]
        for j in range(1, self.count):
            total = total + self.buf[j]
        return total


def forward_kernel(
    enc, visible, ids, gain, offset, mask_token, w_qkv,
    att, normed_out, dest, kv_out, kaug_out, qt_out, ot_out, lse,
    sems_load,
    normed, kv, kaug, qt, ot, w_mine, wq_t, qbd, vt, away, sems_in, sems_dest, sems_fwd, sems_att, sems_store,
):
    cubes, quarter = normed.shape[1], normed.shape[2]
    width = enc.shape[1]
    half = width // 2
    groups = kv.shape[1]
    cap = qt.shape[3] // 2
    slots = groups * cap
    hd = width // HEADS
    pack = 128
    per = pack // hd
    packs = half // pack
    factor = LOG2E * hd ** -0.5
    sibling, across, cross = peer((1,)), peer((2,)), peer((1, 2))
    parity = lax.rem(lax.axis_index("group"), 2)

    mine = pl.ds(pl.multiple_of(parity * half, half), half)

    loads = [pltpu.make_async_copy(w_qkv.at[:, pl.ds(pl.multiple_of(p * width + parity * half, half), half)],
                                   w_mine.at[:, p * half:(p + 1) * half], sems_load.at[p]) for p in range(3)]
    for item in loads:
        item.start()

    greet([sibling, across, cross])

    dest[0] = own_dest(ids[...], cap, groups)
    to_peers = []
    for index, device in enumerate((sibling, across, cross)):
        item = copy_to(dest.at[0], dest.at[index + 1], sems_dest, index, device)
        item.start()
        to_peers.append(item)

    def start_rows(c):
        rows = enc[pl.ds(c * quarter, quarter), :].astype(F32)
        shown = visible[pl.ds(c * quarter, quarter), :] == 1
        return jnp.where(shown, rows, mask_token[...])

    def own_rows(c, _):
        normal, _ = norm_stats(start_rows(c))
        normed[0, c] = (normal * gain[...] + offset[...]).astype(BF)
        copy_to(normed.at[0, c], normed.at[2, c], sems_in, cubes + c, across).start()
        copy_to(normed.at[0, c], normed.at[1, c], sems_in, c, sibling).start()
        return 0

    lax.fori_loop(0, cubes, own_rows, 0)

    for item in loads:
        item.wait()
    wq_t[...] = w_mine[:, :half].T

    one_row = lax.broadcasted_iota(jnp.int32, (16, per * 2 * cap), 0)
    for p in range(packs):
        qbd[p] = jnp.zeros(qbd.shape[1:], BF)
        qbd[p, pack:pack + 16, :] = jnp.where(one_row == 0, 1.0, 0.0).astype(BF)
        vt[p, pack:pack + 16, :] = jnp.ones((16, vt.shape[2]), BF)

    def project(r, c):
        rows = normed[r, c]
        row = dest[r, pl.ds(c, 1), :]
        hot = onehot(row, slots)
        values = dot(rows, w_mine[:, half:]).astype(BF)
        placed = dot(hot, values).astype(BF)
        lane = lax.broadcasted_iota(jnp.int32, (cap, 128), 1)
        place = lax.broadcasted_iota(jnp.int32, (cap, 128), 0)
        for s in range(groups):
            kv[c, s, r * cap:(r + 1) * cap, :] = placed[s * cap:(s + 1) * cap, :]
            inside = jnp.logical_and(row >= s * cap, row < (s + 1) * cap)
            count = jnp.sum(jnp.where(inside, 1, 0), axis=1, keepdims=True)
            bias = jnp.where(place < count, 0.0, MASKED)
            extra = jnp.where(lane == 0, bias, jnp.where(lane < 4, 1.0, 0.0))
            kaug[c, s, r * cap:(r + 1) * cap, :] = extra.astype(BF)
        if r < 2:
            queries = (dot(wq_t[...], rows, NT) * factor).astype(BF)
            spread = dot(queries, hot, NT).astype(BF)
            for s in range(groups):
                qt[c, s, :, r * cap:(r + 1) * cap] = spread[:, s * cap:(s + 1) * cap]

    def near_rows(c, _):
        project(0, c)
        copy_to(normed.at[0, c], normed.at[1, c], sems_in, c, sibling).wait_recv()
        project(1, c)
        return 0

    for item in to_peers:
        item.wait_recv()
    lax.fori_loop(0, cubes, near_rows, 0)

    def attend(c, s):
        for p in range(packs):
            lanes = slice(p * pack, (p + 1) * pack)
            for j in range(per):
                qbd[p, j * hd:(j + 1) * hd, j * 2 * cap:(j + 1) * 2 * cap] = qt[
                    c, s, p * pack + j * hd:p * pack + (j + 1) * hd, :]
            vt[p, :pack, :] = kv[c, s, :, half + p * pack:half + (p + 1) * pack].T
            keys = jnp.concatenate([kv[c, s, :, lanes], kaug[c, s]], axis=1)
            scores = dot(keys, qbd[p])
            top = jnp.maximum(jnp.max(scores, axis=0, keepdims=True), FLOOR)
            probs = jnp.exp2(scores - top).astype(BF)
            mixed = dot(vt[p], probs)
            total = jnp.maximum(mixed[pack:pack + 1, :], 1e-30)
            lse[c, s, p:p + 1, :] = top + jnp.log2(total)
            scale = 1.0 / total
            for j in range(per):
                cols = slice(j * 2 * cap, (j + 1) * 2 * cap)
                ot[c, s, p * pack + j * hd:p * pack + (j + 1) * hd, :] = (
                    mixed[j * hd:(j + 1) * hd, cols] * scale[:, cols]
                ).astype(BF)

    def stores(c):
        pairs = [(ot.at[c], ot_out.at[c]), (kv.at[c], kv_out.at[c]), (kaug.at[c], kaug_out.at[c]),
                 (qt.at[c], qt_out.at[c]), (normed.at[:, c], normed_out.at[:, c])]
        return [pltpu.make_async_copy(src, dst, sems_store.at[c, k]) for k, (src, dst) in enumerate(pairs)]

    def attended_copy(c):
        return copy_to(away.at[c], att.at[c, mine, :], sems_att, c, sibling)

    def cube(c, _):
        copy_to(normed.at[0, c], normed.at[2, c], sems_in, cubes + c, across).wait_recv()
        forward = copy_to(normed.at[2, c], normed.at[3, c], sems_fwd, c, sibling)
        forward.start()
        project(2, c)
        forward.wait_recv()
        project(3, c)
        for item in stores(c)[1:]:
            item.start()

        def one(s, _):
            attend(c, s)
            return 0

        lax.fori_loop(0, groups, one, 0)
        for r in (1, 0):
            hot = onehot(dest[r, pl.ds(c, 1), :], slots)
            placed = jnp.concatenate(
                [ot[c, s, :, r * cap:(r + 1) * cap] for s in range(groups)], axis=1)
            rows = dot(placed, hot).astype(BF)
            if r == 1:
                away[c] = rows
                attended_copy(c).start()
            else:
                att[c, mine, :] = rows
        stores(c)[0].start()
        return 0

    lax.fori_loop(0, cubes, cube, 0)

    def finish(c, _):
        for item in stores(c):
            item.wait()
        attended_copy(c).wait()
        copy_to(normed.at[0, c], normed.at[2, c], sems_in, cubes + c, across).wait_send()
        copy_to(normed.at[0, c], normed.at[1, c], sems_in, c, sibling).wait_send()
        copy_to(normed.at[2, c], normed.at[3, c], sems_fwd, c, sibling).wait_send()
        return 0

    lax.fori_loop(0, cubes, finish, 0)
    for item in to_peers:
        item.wait_send()


def forward_call(enc, visible, ids, gain, offset, mask_token, w_qkv, cubes, groups):
    tokens, width = enc.shape
    quarter = tokens // cubes
    cap = quarter // 3
    half = width // 2
    packs = half // 128
    wide = (128 // (width // HEADS)) * 2 * cap
    vmem = pl.BlockSpec(memory_space=pltpu.VMEM)
    far = pl.BlockSpec(memory_space=pl.ANY)
    shape = jax.ShapeDtypeStruct
    dma = pltpu.SemaphoreType.DMA
    return pl.pallas_call(
        forward_kernel,
        out_shape=(
            shape((cubes, width, quarter), BF),
            shape((groups, cubes, quarter, width), BF),
            shape((groups, 8, quarter), jnp.int32),
            shape((cubes, groups, groups * cap, width), BF),
            shape((cubes, groups, groups * cap, 128), BF),
            shape((cubes, groups, half, 2 * cap), BF),
            shape((cubes, groups, half, 2 * cap), BF),
            shape((cubes, groups, 8, wide), F32),
        ),
        in_specs=[vmem] * 6 + [far],
        out_specs=(vmem, far, vmem, far, far, far, far, vmem),
        scratch_shapes=[
            dma((3,)),
            pltpu.VMEM((groups, cubes, quarter, width), BF),
            pltpu.VMEM((cubes, groups, groups * cap, width), BF),
            pltpu.VMEM((cubes, groups, groups * cap, 128), BF),
            pltpu.VMEM((cubes, groups, half, 2 * cap), BF),
            pltpu.VMEM((cubes, groups, half, 2 * cap), BF),
            pltpu.VMEM((width, 3 * half), BF),
            pltpu.VMEM((half, width), BF),
            pltpu.VMEM((packs, 256, wide), BF),
            pltpu.VMEM((packs, 144, groups * cap), BF),
            pltpu.VMEM((cubes, half, quarter), BF),
            (dma((2 * cubes,)), dma((2 * cubes,))),
            (dma((3,)), dma((3,))),
            (dma((cubes,)), dma((cubes,))),
            (dma((cubes,)), dma((cubes,))),
            dma((cubes, 5)),
        ],
        compiler_params=pltpu.CompilerParams(
            collective_id=0, has_side_effects=True, vmem_limit_bytes=60 * 2**20),
        name="forward",
    )(enc, visible, ids, gain, offset, mask_token, w_qkv)


def pieces(values):
    high = values.astype(BF)
    rest = values - high.astype(F32)
    mid = rest.astype(BF)
    low = (rest - mid.astype(F32)).astype(BF)
    return high, mid, low


def layer_kernel(
    n_dp, n_group,
    att_in, kv_in, kaug_in, qt_in, ot_in, lse, normed_in, dest, w_qkv, enc, visible, mask_token, gain,
    cot_in, w_out_in, w_up_in, w_down_in, gain2, offset2,
    out, grad_enc, sum_ffn, sum_qkv, sum_small,
    kv_at, kaug_at, qt_at, ot_at, normed_at, grads_at, turn, sems_read, sems_turn,
    cot, w_out, w_up, w_down, att, middle, second, backs, result, grads_sum, spare, w_mine, sems_load, sems_out,
    acc, give, pair, recv, settled, sems_core, sems_ffn,
    grad_qkv, small, send_qkv, recv_qkv, settled_qkv, small_bufs, sems_qkv, sems_pair, sems_small,
    dot_slots, qbd, dobd, grad_qt, in_sib, in_fwd, in_across, sems_sib, sems_fwd, sems_across,
):
    cubes, quarter, width = middle.shape
    half = width // 2
    blocks = w_up.shape[0]
    groups = kv_at.shape[1]
    cap = qt_at.shape[3] // 2
    slots = groups * cap
    hd = width // HEADS
    pack = 128
    per = pack // hd
    packs = half // pack
    factor = hd ** -0.5
    sibling, across = peer((1,)), peer((2,))
    parity = lax.rem(lax.axis_index("group"), 2)
    mine = pl.ds(pl.multiple_of(parity * half, half), half)
    theirs = pl.ds(pl.multiple_of((1 - parity) * half, half), half)
    grad_kv, own_sum, out_fwd, out_sib, out_across = w_up, result, cot, second, backs

    core = ("group", 1)
    others = chip_bits(n_dp, n_group)
    paths = path_orders(others, PARTS)
    qkv = [
        Butterfly(grad_qkv.at[p], send_qkv.at[p], recv_qkv.at[p], settled_qkv.at[p], sum_qkv.at[parity, p],
                  (sems_qkv[0].at[p], sems_qkv[1].at[p]), order)
        for p, order in enumerate(path_orders(others, 3))]
    qkv_steps = joined(reduce_steps(qkv), gather_steps(qkv))
    smalls = [
        SmallSum(small_bufs[k], (sems_small[0].at[k], sems_small[1].at[k]), names)
        for k, names in enumerate(small_groups(n_dp, n_group))]

    def place_of(j, side):
        if j < blocks:
            return sum_ffn.at[j + side * blocks]
        return sum_ffn.at[2 * blocks, pl.ds(pl.multiple_of(side * half, half), half)]

    def rows_in(j):
        return width if j < blocks else half

    def butterflies(j):
        count = rows_in(j)
        return [
            Butterfly(acc.at[j, :count, lanes_of(p)], give.at[j, :, lanes_of(p)], recv.at[j, :, lanes_of(p)],
                      settled.at[j, :count >> halvings_of(count, len(others)), lanes_of(p)],
                      place_of(j, parity).at[:, lanes_of(p)],
                      (sems_ffn[0].at[j, p], sems_ffn[1].at[j, p]), paths[p]) for p in range(PARTS)]

    def summing(j):
        count = rows_in(j)
        inner = reduce_steps(butterflies(j))
        exchange = copy_to(give.at[j, :count], pair.at[j, :count], sems_core, j, sibling)

        def second_step():
            exchange.wait()
            acc[j, :count] += pair[j, :count].astype(F32)
            inner[0]()

        return [exchange.start, second_step] + inner[1:]

    def spreading(sets):
        steps = gather_steps([b for j in sets for b in butterflies(j)])

        def exchanges():
            return [
                copy_to(place_of(j, parity), place_of(j, parity), sems_core, blocks + 1 + j, sibling) for j in sets]

        def last_but_one():
            steps[-1]()
            for item in exchanges():
                item.start()

        def final():
            for item in exchanges():
                item.wait()

        return steps[:-1] + [last_but_one, final]

    def reads(c):
        k = lax.rem(c, 2)
        pairs = [(kv_in.at[c], kv_at.at[k]), (kaug_in.at[c], kaug_at.at[k]), (qt_in.at[c], qt_at.at[k]),
                 (ot_in.at[c], ot_at.at[k]), (normed_in.at[:, c], normed_at.at[k])]
        return [pltpu.make_async_copy(src, dst, sems_read.at[k, n]) for n, (src, dst) in enumerate(pairs)]

    loads = [(w_out_in, w_out), (att_in, att)]
    loads += [(w_up_in.at[:, j * width:(j + 1) * width], w_up.at[j]) for j in range(blocks)]
    loads += [(w_down_in.at[j * width:(j + 1) * width, :], w_down.at[j]) for j in range(blocks)]
    loads += [(cot_in.at[c * quarter:(c + 1) * quarter, :], cot.at[c]) for c in range(cubes)]
    loads += [(w_qkv.at[:, pl.ds(pl.multiple_of(p * width + parity * half, half), half)],
               w_mine.at[:, p * half:(p + 1) * half]) for p in range(3)]
    loads = [pltpu.make_async_copy(src, dst, sems_load.at[k]) for k, (src, dst) in enumerate(loads)]
    for item in loads:
        item.start()
    for c in range(min(2, cubes)):
        for item in reads(c):
            item.start()

    meets = {}
    for names in small_groups(n_dp, n_group):
        for t in range(1, 1 << len(names)):
            chosen = [name for k, name in enumerate(names) if (t >> k) & 1]
            meets[tuple(chosen)] = flip(chosen)
    for name in [core] + others:
        meets[(name,)] = flip([name])
    greet(list(meets.values()))

    one_row = lax.broadcasted_iota(jnp.int32, (16, per * 2 * cap), 0)
    for p in range(packs):
        qbd[p] = jnp.zeros(qbd.shape[1:], BF)
        dobd[p] = jnp.zeros(dobd.shape[1:], BF)
    grad_qkv[...] = jnp.zeros(grad_qkv.shape, F32)
    small[...] = jnp.zeros(small.shape, F32)

    def rows_of(c):
        return pl.ds(c * quarter, quarter)

    def start_rows(c):
        shown = visible[rows_of(c), :] == 1
        return shown, jnp.where(shown, enc[rows_of(c), :].astype(F32), mask_token[...])

    def turn_copy(c):
        return copy_to(turn.at[c], grads_at.at[c, 1], sems_turn, c, sibling)

    def out_copy(c):
        return pltpu.make_async_copy(second.at[c], out.at[rows_of(c), :], sems_out.at[0, c])

    def enc_copy(c):
        return pltpu.make_async_copy(second.at[c], grad_enc.at[rows_of(c), :], sems_out.at[1, c])

    def enter(c, _):
        value = start_rows(c)[1] + dot(att[c], w_out[...], TN)
        middle[c] = value
        normal, _ = norm_stats(value)
        second[c] = (normal * gain2[...] + offset2[...]).astype(BF)
        return 0

    def block(j, c):
        rows, cotan = second[c], cot[c]
        hidden = dot(rows, w_up[j])
        square = hidden * hidden
        tanh = jnp.tanh(hidden * (GELU_A + GELU_B * square))
        slope = 0.5 * (1.0 + tanh)
        active = (hidden * slope).astype(BF)
        slope = slope + 0.5 * hidden * (1.0 - tanh * tanh) * (GELU_A + 3.0 * GELU_B * square)
        grad_hidden = (dot(cotan, w_down[j], NT) * slope).astype(BF)
        grad_up = dot(rows, grad_hidden, TN)
        grad_down = dot(active, cotan, TN)
        kept = jnp.where(parity == 0, grad_up, grad_down)
        given = jnp.where(parity == 0, grad_down, grad_up)
        outcome = dot(active, w_down[j])
        grads = dot(grad_hidden, w_up[j], NT)
        result[c] = outcome + jnp.where(j > 0, result[c], 0.0)
        grads_sum[c] = grads + jnp.where(j > 0, grads_sum[c], 0.0)
        acc[j] = kept + jnp.where(c > 0, acc[j], 0.0)
        spare[...] = given + jnp.where(c > 0, spare[...], 0.0)

        def hand_over():
            give[j, :width] = spare[...].astype(BF)

        pl.when(c == cubes - 1)(hand_over)

    def leave(c):
        second[c] = (middle[c] + result[c]).astype(BF)
        out_copy(c).start()
        normal, recip = norm_stats(middle[c])
        grads = grads_sum[c]
        small[3:4, :] += jnp.sum(grads * normal, axis=0, keepdims=True)
        small[4:5, :] += jnp.sum(grads, axis=0, keepdims=True)
        total = cot[c].astype(F32) + norm_back(grads, normal, recip, gain2[...])
        middle[c] = total
        branch = total.astype(BF)
        back = dot(w_out[...], branch, NT).astype(BF)
        backs[c] = branch
        turn[c] = jnp.where(parity == 0, back[half:], back[:half])
        grads_at[c, 0] = jnp.where(parity == 0, back[:half], back[half:])
        turn_copy(c).start()

    def out_weights():
        total = dot(att[0], backs[0])
        for c in range(1, cubes):
            total += dot(att[c], backs[c])
        acc[blocks, :half] = jnp.where(parity == 0, total[:half], total[half:])
        give[blocks, :half] = jnp.where(parity == 0, total[half:], total[:half]).astype(BF)

    firsts = [summing(j) for j in range(blocks + 1)]
    seconds = [spreading(sets) for sets in SPREADS]
    plan = []
    for number, (steps, places) in enumerate(zip(firsts + seconds, SUM_AT + SPREAD_AT)):
        if len(places) != len(steps):
            places = [places[0] + 2 * k for k in range(len(steps))]
        stage = 0 if number < len(firsts) else len(steps)
        plan += [(place, stage + k, number, step) for k, (place, step) in enumerate(zip(places, steps))]
    plan = [(entry[0], entry[-1]) for entry in sorted(plan, key=lambda entry: entry[:3])]
    lead = blocks * cubes + cubes + 1

    def advance(place):
        for at, step in plan:
            if at == place:
                step()

    for item in loads:
        item.wait()
    lax.fori_loop(0, cubes, enter, 0)
    place = blocks * cubes

    def blocks_step(u, _):
        block(u // cubes, lax.rem(u, cubes))
        for at, step in plan:
            if at <= place:
                pl.when(u == at - 1)(step)
        return 0

    lax.fori_loop(0, place, blocks_step, 0)
    for c in range(cubes):
        leave(c)
        place += 1
        advance(place)
    out_weights()
    place += 1
    advance(place)
    for c in range(cubes):
        out_copy(c).wait()

    def extra_rows(first, values):
        high, mid, low = pieces(-values)
        rows = jnp.where(
            one_row == 0, first,
            jnp.where(one_row == 1, high.astype(F32),
                      jnp.where(one_row == 2, mid.astype(F32),
                                jnp.where(one_row == 3, low.astype(F32), 0.0))))
        return rows.astype(BF)

    def attend_back(c, s):
        slot = lax.rem(c, 2)
        for p in range(packs):
            lanes = slice(p * pack, (p + 1) * pack)
            deltas = []
            for j in range(per):
                rows = slice(p * pack + j * hd, p * pack + (j + 1) * hd)
                cols = slice(j * 2 * cap, (j + 1) * 2 * cap)
                qbd[p, j * hd:(j + 1) * hd, cols] = qt_at[slot, s, rows, :]
                grads = dot_slots[s, rows, :]
                dobd[p, j * hd:(j + 1) * hd, cols] = grads
                deltas.append(jnp.sum(
                    grads.astype(F32) * ot_at[slot, s, rows, :].astype(F32), axis=0, keepdims=True))
            qbd[p, pack:pack + 16, :] = extra_rows(1.0, lse[c, s, p:p + 1, :])
            dobd[p, pack:pack + 16, :] = extra_rows(0.0, jnp.concatenate(deltas, axis=1))
            extra = kaug_at[slot, s]
            keys = kv_at[slot, s, :, lanes]
            values = kv_at[slot, s, :, half + p * pack:half + (p + 1) * pack]
            probs = jnp.exp2(dot(jnp.concatenate([keys, extra], axis=1), qbd[p]))
            centred = dot(jnp.concatenate([values, extra], axis=1), dobd[p])
            grad_scores = (probs * centred).astype(BF)
            grad_kv[s, :, half + p * pack:half + (p + 1) * pack] = dot(
                probs.astype(BF), dobd[p, :pack, :], NT).astype(BF)
            grad_kv[s, :, lanes] = (dot(grad_scores, qbd[p, :pack, :], NT) * LN2).astype(BF)
            mixed = dot(keys.T, grad_scores) * factor
            for j in range(per):
                rows = slice(p * pack + j * hd, p * pack + (j + 1) * hd)
                cols = slice(j * 2 * cap, (j + 1) * 2 * cap)
                grad_qt[s, rows, :] = mixed[j * hd:(j + 1) * hd, cols].astype(BF)

    def back_project(r, c):
        hot = onehot(dest[r, pl.ds(c, 1), :], slots)
        placed = jnp.concatenate(
            [grad_kv[s, r * cap:(r + 1) * cap, :] for s in range(groups)], axis=0)
        grads = dot(hot, placed, TN).astype(BF)
        if r < 2:
            queries = jnp.concatenate(
                [grad_qt[s, :, r * cap:(r + 1) * cap] for s in range(groups)], axis=1)
            queries = dot(queries, hot).T.astype(BF)
            grads = jnp.concatenate([queries, grads], axis=1)
            weight = dot(normed_at[lax.rem(c, 2), r], grads, TN)
            for k in range(3):
                grad_qkv[k] += weight[:, k * half:(k + 1) * half]
            return dot(grads, w_mine[...], NT)
        weight = dot(normed_at[lax.rem(c, 2), r], grads, TN)
        for k in range(2):
            grad_qkv[k + 1] += weight[:, k * half:(k + 1) * half]
        return dot(grads, w_mine[:, half:], NT)

    def prepare(c):
        for item in reads(c):
            item.wait()
        for r in range(2):
            rows = grads_at[c, r]
            hot = onehot(dest[r, pl.ds(c, 1), :], slots)
            spread = dot(rows, hot, NT).astype(BF)
            for s in range(groups):
                dot_slots[s, :, r * cap:(r + 1) * cap] = spread[:, s * cap:(s + 1) * cap]

    def cube(c, _):
        def point(i):
            for at, step in plan:
                if at > lead and (at - lead - 1) % POINTS == i and (at - lead - 1) // POINTS < cubes:
                    pl.when(c == (at - lead - 1) // POINTS)(step)

        turn_copy(c).wait()
        prepare(c)
        point(0)

        def one(s, _):
            attend_back(c, s)
            for i in range(groups):
                pl.when(s == i)(functools.partial(point, i + 1))
            return 0

        lax.fori_loop(0, groups, one, 0)
        out_fwd[c] = back_project(3, c).astype(BF)
        forward = copy_to(out_fwd.at[c], in_fwd.at[c], sems_fwd, c, sibling)
        forward.start()
        point(5)
        partial = back_project(2, c)
        forward.wait_recv()
        out_across[c] = (partial + in_fwd[c].astype(F32)).astype(BF)
        copy_to(out_across.at[c], in_across.at[c], sems_across, c, across).start()
        point(6)
        out_sib[c] = back_project(1, c).astype(BF)
        copy_to(out_sib.at[c], in_sib.at[c], sems_sib, c, sibling).start()
        point(7)
        own_sum[c] = back_project(0, c)

        def more():
            for item in reads(c + 2):
                item.start()

        pl.when(c + 2 < cubes)(more)
        point(8)
        return 0

    lax.fori_loop(0, cubes, cube, 0)
    qkv_steps[0]()
    tail = [(at - lead - POINTS * cubes, step) for at, step in plan if at > lead + POINTS * cubes]

    def last(c):
        copy_to(out_sib.at[c], in_sib.at[c], sems_sib, c, sibling).wait()
        copy_to(out_across.at[c], in_across.at[c], sems_across, c, across).wait()
        copy_to(out_fwd.at[c], in_fwd.at[c], sems_fwd, c, sibling).wait_send()
        grads = own_sum[c] + in_sib[c].astype(F32) + in_across[c].astype(F32)
        shown, start = start_rows(c)
        normal, recip = norm_stats(start)
        small[0:1, :] += jnp.sum(grads * normal, axis=0, keepdims=True)
        small[1:2, :] += jnp.sum(grads, axis=0, keepdims=True)
        total = middle[c] + norm_back(grads, normal, recip, gain[...])
        second[c] = jnp.where(shown, total, 0.0).astype(BF)
        enc_copy(c).start()
        small[2:3, :] += jnp.sum(jnp.where(shown, 0.0, total), axis=0, keepdims=True)

    fill = list(range(cubes))
    for k in range(1, len(qkv_steps)):
        if fill:
            last(fill.pop(0))
            if not fill:
                smalls[0].start(small[...])
        qkv_steps[k]()
        while tail and tail[0][0] <= k:
            tail.pop(0)[1]()
    pair_qkv = copy_to(sum_qkv.at[parity], sum_qkv.at[parity], sems_pair, 0, sibling)
    pair_qkv.start()
    for _, step in tail:
        step()
    for k, item in enumerate(smalls):
        total = item.finish()
        if k + 1 < len(smalls):
            smalls[k + 1].start(total)
    sum_small[...] = total
    for c in range(cubes):
        enc_copy(c).wait()
    pair_qkv.wait()


POINTS = 9
PARTS = 4
SUM_AT = [
    [3, 5, 9, 12, 16, 19],
    [6, 8, 12, 16, 19, 21],
    [9, 11, 15, 19, 22, 25],
    [12, 14, 18, 20, 22, 25],
    [16, 18, 21, 25, 28, 32],
]
SPREADS = [[0], [1], [2], [3], [4]]
SPREAD_AT = [
    [19, 21, 24, 27, 30, 32],
    [21, 24, 27, 31, 35, 37],
    [25, 28, 31, 36, 39, 41],
    [25, 28, 32, 37, 41, 43],
    [32, 37, 41, 44, 46, 47],
]


def layer_call(
    att, kv, kaug, qt, ot, lse, normed, dest, w_qkv, enc, visible, mask_token, gain,
    cot, w_out, w_up, w_down, gain2, offset2, n_dp, n_group,
):
    cubes, width, quarter = att.shape
    groups = kv.shape[1]
    cap = quarter // 3
    half = width // 2
    packs = half // 128
    wide = (128 // (width // HEADS)) * 2 * cap
    blocks = w_up.shape[1] // width
    vmem = pl.BlockSpec(memory_space=pltpu.VMEM)
    far = pl.BlockSpec(memory_space=pl.ANY)
    shape = jax.ShapeDtypeStruct
    dma = pltpu.SemaphoreType.DMA
    rows = pltpu.VMEM((cubes, quarter, width), BF)
    sums = pltpu.VMEM((cubes, quarter, width), F32)
    squares = pltpu.VMEM((blocks, width, width), BF)
    pair = (dma((cubes,)), dma((cubes,)))
    stages = len(chip_bits(n_dp, n_group))
    staging = staging_rows(width, stages)
    kept = max(width >> halvings_of(width, stages), half >> halvings_of(half, stages))
    kept_qkv = width >> halvings_of(width, stages)
    small = small_groups(n_dp, n_group)
    return pl.pallas_call(
        functools.partial(layer_kernel, n_dp, n_group),
        out_shape=(
            shape(enc.shape, BF),
            shape(enc.shape, BF),
            shape((2 * blocks + 1, width, width), BF),
            shape((2, 3, width, half), BF),
            shape((8, width), F32),
        ),
        in_specs=[far] * 5 + [vmem, far, vmem, far] + [vmem] * 4 + [far] * 4 + [vmem] * 2,
        out_specs=(far, far, far, far, vmem),
        scratch_shapes=[
            pltpu.VMEM((2,) + kv.shape[1:], BF),
            pltpu.VMEM((2,) + kaug.shape[1:], BF),
            pltpu.VMEM((2,) + qt.shape[1:], BF),
            pltpu.VMEM((2,) + ot.shape[1:], BF),
            pltpu.VMEM((2, groups, quarter, width), BF),
            pltpu.VMEM((cubes, 2, half, quarter), BF),
            pltpu.VMEM((cubes, half, quarter), BF),
            dma((2, 5)),
            pair,
            rows,
            pltpu.VMEM(w_out.shape, BF),
            squares,
            squares,
            pltpu.VMEM(att.shape, BF),
            sums,
            rows,
            rows,
            sums,
            sums,
            pltpu.VMEM((width, width), F32),
            pltpu.VMEM((width, 3 * half), BF),
            dma((2 + 2 * blocks + cubes + 3,)),
            dma((2, cubes)),
            pltpu.VMEM((blocks + 1, width, width), F32),
            pltpu.VMEM((blocks + 1, max(width, staging), width), BF),
            pltpu.VMEM((blocks + 1, width, width), BF),
            pltpu.VMEM((blocks + 1, staging, width), BF),
            pltpu.VMEM((blocks + 1, kept, width), BF),
            (dma((2 * blocks + 2,)), dma((2 * blocks + 2,))),
            (dma((blocks + 1, PARTS, 2 * stages + 1)), dma((blocks + 1, PARTS, 2 * stages + 1))),
            pltpu.VMEM((3, width, half), F32),
            pltpu.VMEM((8, width), F32),
            pltpu.VMEM((3, staging, half), BF),
            pltpu.VMEM((3, staging, half), BF),
            pltpu.VMEM((3, kept_qkv, half), BF),
            tuple(pltpu.VMEM((1 << len(names), 8, width), F32) for names in small),
            (dma((3, 2 * stages + 1)), dma((3, 2 * stages + 1))),
            (dma((1,)), dma((1,))),
            (dma((len(small), 8)), dma((len(small), 8))),
            pltpu.VMEM((groups, half, 2 * cap), BF),
            pltpu.VMEM((packs, 256, wide), BF),
            pltpu.VMEM((packs, 256, wide), BF),
            pltpu.VMEM((groups, half, 2 * cap), BF),
            rows, rows, rows,
            pair, pair, pair,
        ],
        compiler_params=pltpu.CompilerParams(
            collective_id=1, has_side_effects=True, vmem_limit_bytes=63 * 2**20),
        name="layer",
    )(att, kv, kaug, qt, ot, lse, normed, dest, w_qkv, enc, visible, mask_token, gain,
      cot, w_out, w_up, w_down, gain2, offset2)


def cast_kernel(ups, downs, outs, qkvs, up, down, out, qkv):
    width, half = outs.shape[1], qkvs.shape[3]
    for k in range(ups.shape[0]):
        up[:, k * width:(k + 1) * width] = ups[k].astype(F32)
    down[...] = downs[...].astype(F32)
    out[...] = outs[...].astype(F32)
    for part in range(3):
        for side in range(2):
            at = part * width + side * half
            qkv[:, at:at + half] = qkvs[side, part].astype(F32)


def cast_call(ffn, qkv):
    width = qkv.shape[2]
    blocks = ffn.shape[0] // (2 * width)
    steps = 8
    rows = width // steps
    tall = blocks * rows
    shape = jax.ShapeDtypeStruct
    return pl.pallas_call(
        cast_kernel,
        grid=(steps,),
        in_specs=[
            pl.BlockSpec((blocks, rows, width), lambda i: (0, i, 0)),
            pl.BlockSpec((tall, width), lambda i: (steps + i, 0)),
            pl.BlockSpec((rows, width), lambda i: (2 * blocks * steps + i, 0)),
            pl.BlockSpec((2, 3, rows, width // 2), lambda i: (0, 0, i, 0)),
        ],
        out_specs=[
            pl.BlockSpec((rows, blocks * width), lambda i: (i, 0)),
            pl.BlockSpec((tall, width), lambda i: (i, 0)),
            pl.BlockSpec((rows, width), lambda i: (i, 0)),
            pl.BlockSpec((rows, 3 * width), lambda i: (i, 0)),
        ],
        out_shape=(
            shape((width, blocks * width), F32),
            shape((blocks * width, width), F32),
            shape((width, width), F32),
            shape((width, 3 * width), F32),
        ),
        name="cast",
    )(ffn.reshape(2 * blocks + 1, width, width), ffn, ffn, qkv)


def on_device(
    enc, visible, band_group, cotangent, ln1_gain, ln1_bias, w_qkv, w_out,
    ln2_gain, ln2_bias, w_up, w_down, mask_token,
):
    groups = lax.axis_size("group")
    tok_dev, width = enc.shape
    quarter = CUBE_TOK // groups
    cubes = tok_dev // quarter
    column = visible.reshape(tok_dev, 1)
    ids = jnp.pad(band_group.reshape(cubes, quarter), ((0, 8 - cubes), (0, 0)), constant_values=-1)
    gain1, mask_row = ln1_gain[None, :], mask_token[None, :]
    att, normed, dest, kv, kaug, qt, ot, lse = forward_call(
        enc, column, ids, gain1, ln1_bias[None, :], mask_row, w_qkv, cubes, groups)
    out, grad_enc, sum_ffn, sum_qkv, small = layer_call(
        att, kv, kaug, qt, ot, lse, normed, dest, w_qkv, enc, column, mask_row, gain1, cotangent, w_out, w_up,
        w_down, ln2_gain[None, :], ln2_bias[None, :], lax.axis_size("dp"), groups)
    sum_up, sum_down, sum_out, sum_w_qkv = cast_call(sum_ffn.reshape(9 * width, width), sum_qkv)
    return (
        out, grad_enc, small[0], small[1], sum_w_qkv, sum_out, small[3], small[4], sum_up, sum_down, small[2])


def solution(mesh):
    rows, line = P(("dp", "group"), None), P(("dp", "group"))
    return jax.shard_map(
        on_device, mesh=mesh, in_specs=(rows, line, line, rows) + (P(),) * 9,
        out_specs=(rows, rows) + (P(),) * 9, check_vma=False)
```

```python
import functools
import jax
import jax.numpy as jnp
from jax import lax
from jax.experimental import pallas as pl
from jax.experimental.pallas import tpu as pltpu
from jax.sharding import PartitionSpec as P

HEADS = 16
CUBE_TOK = 1536
EPS = 1e-05
LOG2E = 1.4426950408889634
LN2 = 0.6931471805599453
GELU_A = 0.7978845608028654
GELU_B = 0.7978845608028654 * 0.044715
FLOOR = -1e20
MASKED = -1e30

NN = (((1,), (0,)), ((), ()))
NT = (((1,), (1,)), ((), ()))
TN = (((0,), (0,)), ((), ()))
MESH = pl.DeviceIdType.MESH
BF = jnp.bfloat16
F32 = jnp.float32


def dot(left, right, dims=NN):
    return lax.dot_general(left, right, dims, preferred_element_type=F32)


def norm_stats(values):
    centre = values - jnp.mean(values, axis=-1, keepdims=True)
    spread = jnp.mean(centre * centre, axis=-1, keepdims=True)
    recip = lax.rsqrt(spread + EPS)
    return centre * recip, recip


def norm_back(grad_rows, normal, recip, gain):
    scaled = grad_rows * gain
    return recip * (
        scaled
        - jnp.mean(scaled, axis=-1, keepdims=True)
        - normal * jnp.mean(scaled * normal, axis=-1, keepdims=True)
    )


def onehot(dest_row, slots):
    rows = lax.broadcasted_iota(jnp.int32, (slots, dest_row.shape[1]), 0)
    return jnp.where(rows == dest_row, 1.0, 0.0).astype(BF)


def peer(bits):
    me = lax.axis_index("group")
    for bit in bits:
        me = me + (1 - 2 * (lax.rem(me // bit, 2))) * bit
    return (lax.axis_index("dp"), me)


def copy_to(src, dst, sems, index, device):
    return pltpu.make_async_remote_copy(
        src_ref=src, dst_ref=dst, send_sem=sems[0].at[index], recv_sem=sems[1].at[index],
        device_id=device, device_id_type=MESH,
    )


def greet(devices):
    barrier = pltpu.get_barrier_semaphore()
    for device in devices:
        pl.semaphore_signal(barrier, inc=1, device_id=device, device_id_type=MESH)
    pl.semaphore_wait(barrier, len(devices))


def own_dest(ids, capacity, groups):
    tokens = ids.shape[1]
    upper = (
        lax.broadcasted_iota(jnp.int32, (tokens, tokens), 0)
        < lax.broadcasted_iota(jnp.int32, (tokens, tokens), 1)
    )
    upper = jnp.where(upper, 1.0, 0.0).astype(BF)
    total = jnp.zeros(ids.shape, F32)
    for group in range(groups):
        hit = jnp.where(ids == group, 1.0, 0.0)
        ranks = dot(hit.astype(BF), upper)
        total = total + hit * (ranks + float(group * capacity))
    return total.astype(jnp.int32)


def bits_of(size):
    return [1 << k for k in range(size.bit_length() - 1)]


def bit_value(name):
    axis, bit = name
    return lax.rem(lax.axis_index(axis) // bit, 2)


def flip(names):
    place = {axis: lax.axis_index(axis) for axis in ("dp", "group")}
    for axis, bit in names:
        place[axis] = place[axis] + (1 - 2 * bit_value((axis, bit))) * bit
    return (place["dp"], place["group"])


class Butterfly:
    def __init__(self, acc, send, recv, settled, out, sems, names):
        self.acc, self.send, self.recv, self.settled, self.out = acc, send, recv, settled, out
        self.sems, self.names = sems, names
        self.rows = acc.shape[0]
        self.halvings = halvings_of(self.rows, len(names))
        self.groups = [[name] for name in names]
        if self.halvings >= 4:
            last = names[self.halvings - 2:self.halvings]
            self.groups[self.halvings - 2:self.halvings] = [last]
        self.legs = sum((1 << len(group)) - 1 for group in self.groups)
        self.halving_groups = [
            g for g in range(len(self.groups)) if self.done(g) < self.halvings]

    def done(self, g):
        return sum(len(group) for group in self.groups[:g])

    def start_row(self, k):
        low = 0
        for j in range(min(k, self.halvings)):
            low = low + bit_value(self.names[j]) * (self.rows >> (j + 1))
        return low

    def span(self, low, count):
        return pl.ds(pl.multiple_of(low, 16), count)

    def partners(self, g):
        names, done = self.groups[g], self.done(g)
        number = sum((1 << len(group)) - 1 for group in self.groups[:g])
        found = []
        for t in range(1, 1 << len(names)):
            low = self.start_row(done)
            if done < self.halvings:
                for k, name in enumerate(names):
                    value = 1 - bit_value(name) if (t >> k) & 1 else bit_value(name)
                    low = low + value * (self.rows >> (done + k + 1))
            found.append(([name for k, name in enumerate(names) if (t >> k) & 1], number + t - 1, low))
        return found

    def hops(self, g):
        done, size = self.done(g), len(self.groups[g])
        if done < self.halvings:
            count = self.rows >> (done + size)
            at = self.rows - (self.rows >> done)
        else:
            count = self.rows >> self.halvings
            at = self.rows + (done - self.halvings - 1) * count
        found = []
        for n, (names, number, low) in enumerate(self.partners(g)):
            where = pl.ds(at + n * count, count)
            item = copy_to(self.send.at[where], self.recv.at[where], self.sems, number, flip(names))
            found.append((item, where, self.span(low, count)))
        return found, count

    def reduce_start(self, g):
        for item, where, rows in self.hops(g)[0]:
            self.send[where, :] = self.acc[rows, :].astype(BF)
            item.start()

    def reduce_finish(self, g):
        found, count = self.hops(g)
        rows = self.span(self.start_row(self.done(g) + len(self.groups[g])), count)
        for item, where, _ in found:
            item.wait()
        for _, where, _ in found:
            if self.done(g) < self.halvings:
                self.acc[rows, :] += self.recv[where, :].astype(F32)
            else:
                self.acc[rows, :] = self.send[where, :].astype(F32) + self.recv[where, :].astype(F32)

    def own_piece(self):
        return self.span(self.start_row(self.halvings), self.rows >> self.halvings)

    def keep(self):
        return pltpu.make_async_copy(
            self.settled, self.out.at[self.own_piece(), :], self.sems[0].at[2 * self.legs])

    def settle(self):
        self.settled[...] = self.acc[self.own_piece(), :].astype(BF)
        self.keep().start()

    def gather(self, g):
        done = self.done(g) + len(self.groups[g])
        rows = self.span(self.start_row(done), self.rows >> done)
        src = self.settled if done == self.halvings else self.out.at[rows, :]
        return [
            copy_to(src, self.out.at[rows, :], self.sems, self.legs + number, flip(names))
            for names, number, _ in self.partners(g)]


def halvings_of(rows, stages):
    count = 0
    while count < stages and (rows >> (count + 1)) % 16 == 0:
        count += 1
    return count


def staging_rows(rows, stages):
    count = halvings_of(rows, stages)
    return rows + (stages - count - 1) * (rows >> count)


def reduce_steps(butterflies):
    stages = len(butterflies[0].groups)

    def first():
        for b in butterflies:
            b.reduce_start(0)

    steps = [first]
    for g in range(stages):
        def step(g=g):
            for b in butterflies:
                b.reduce_finish(g)
                if g + 1 < stages:
                    b.reduce_start(g + 1)
                else:
                    b.settle()
        steps.append(step)
    return steps


def gather_steps(butterflies):
    last = butterflies[0].halving_groups[-1]

    def start(b, g):
        for item in b.gather(g):
            item.start()

    def first():
        for b in butterflies:
            start(b, last)

    steps = [first]
    for g in range(last, -1, -1):
        def step(g=g):
            for b in butterflies:
                for item in b.gather(g):
                    item.wait()
                if g == last:
                    b.keep().wait()
                if g > 0:
                    start(b, g - 1)
        steps.append(step)
    return steps


def joined(before, after):
    def both():
        before[-1]()
        after[0]()

    return before[:-1] + [both] + after[1:]


def path_orders(names, count):
    head, tail = names[:count], names[count:]
    return [head[k:] + head[:k] + tail for k in range(count)]


def balanced_orders(names):
    first, second, third, tail = names[0], names[1], names[2], names[3:]
    return [[second, first, third] + tail, [second, third, first] + tail] + [[third, second, first] + tail] * 2


def chip_bits(n_dp, n_group):
    return [("group", b) for b in bits_of(n_group) if b > 1] + [("dp", b) for b in bits_of(n_dp)]


def lanes_of(p):
    return slice(p * 128, (p + 1) * 128)


PARTS = 4

def small_groups(n_dp, n_group):
    names = [("group", b) for b in bits_of(n_group)] + [("dp", b) for b in bits_of(n_dp)]
    groups = [names[:3]]
    rest = names[3:]
    while rest:
        groups.append(rest[:2])
        rest = rest[2:]
    return groups


class SmallSum:
    def __init__(self, buf, sems, names):
        self.buf, self.sems, self.names = buf, sems, names
        self.count = 1 << len(names)

    def copies(self):
        place = 0
        for k, name in enumerate(self.names):
            place = place + bit_value(name) * (1 << k)
        items = []
        for t in range(1, self.count):
            others = [name for k, name in enumerate(self.names) if (t >> k) & 1]
            items.append(copy_to(self.buf.at[place], self.buf.at[place], self.sems, t, flip(others)))
        return place, items

    def start(self, values):
        place, items = self.copies()
        self.buf[place] = values
        for item in items:
            item.start()

    def finish(self):
        _, items = self.copies()
        for item in items:
            item.wait()
        total = self.buf[0]
        for j in range(1, self.count):
            total = total + self.buf[j]
        return total


def as_columns(codes, columns):
    shown = jnp.where(codes[...] >= 8, 1.0, 0.0)
    shown = jnp.concatenate([shown, jnp.zeros((8 - shown.shape[0], shown.shape[1]), F32)], axis=0).T
    for c in range(codes.shape[0]):
        columns[c] = shown[:, c:c + 1]


def forward_kernel(
    enc, codes, gain, offset, mask_token, w_qkv,
    att, normed_out, dest, kv_out, kaug_out, qt_out, ot_out, lse,
    sems_load,
    normed, kv, kaug, qt, ot, columns, w_mine, wq_t, qbd, vt, away, sems_in, sems_dest, sems_fwd, sems_att, sems_store,
):
    cubes, quarter = normed.shape[1], normed.shape[2]
    width = enc.shape[1]
    half = width // 2
    groups = kv.shape[1]
    cap = qt.shape[3] // 2
    slots = groups * cap
    hd = width // HEADS
    pack = 128
    per = pack // hd
    packs = half // pack
    factor = LOG2E * hd ** -0.5
    sibling, across, cross = peer((1,)), peer((2,)), peer((1, 2))
    parity = lax.rem(lax.axis_index("group"), 2)

    mine = pl.ds(pl.multiple_of(parity * half, half), half)

    loads = [pltpu.make_async_copy(w_qkv.at[:, pl.ds(pl.multiple_of(p * width + parity * half, half), half)],
                                   w_mine.at[:, p * half:(p + 1) * half], sems_load.at[p]) for p in range(3)]
    for item in loads:
        item.start()

    greet([sibling, across, cross])

    dest[0] = jnp.zeros(dest.shape[1:], jnp.int32)
    dest[0, :cubes] = own_dest(codes[...] & 7, cap, groups)
    as_columns(codes, columns)
    to_peers = []
    for index, device in enumerate((sibling, across, cross)):
        item = copy_to(dest.at[0], dest.at[index + 1], sems_dest, index, device)
        item.start()
        to_peers.append(item)

    def start_rows(c):
        rows = enc[pl.ds(c * quarter, quarter), :].astype(F32)
        return jnp.where(columns[c] == 1.0, rows, mask_token[...])

    def own_rows(c, _):
        normal, _ = norm_stats(start_rows(c))
        normed[0, c] = (normal * gain[...] + offset[...]).astype(BF)
        copy_to(normed.at[0, c], normed.at[2, c], sems_in, cubes + c, across).start()
        copy_to(normed.at[0, c], normed.at[1, c], sems_in, c, sibling).start()
        return 0

    lax.fori_loop(0, cubes, own_rows, 0)

    for item in loads:
        item.wait()
    wq_t[...] = w_mine[:, :half].T

    one_row = lax.broadcasted_iota(jnp.int32, (16, per * 2 * cap), 0)
    for p in range(packs):
        qbd[p] = jnp.zeros(qbd.shape[1:], BF)
        qbd[p, pack:pack + 16, :] = jnp.where(one_row == 0, 1.0, 0.0).astype(BF)
        vt[p, pack:pack + 16, :] = jnp.ones((16, vt.shape[2]), BF)

    def project(r, c):
        rows = normed[r, c]
        row = dest[r, pl.ds(c, 1), :]
        hot = onehot(row, slots)
        values = dot(rows, w_mine[:, half:]).astype(BF)
        placed = dot(hot, values).astype(BF)
        lane = lax.broadcasted_iota(jnp.int32, (cap, 128), 1)
        place = lax.broadcasted_iota(jnp.int32, (cap, 128), 0)
        for s in range(groups):
            kv[c, s, r * cap:(r + 1) * cap, :] = placed[s * cap:(s + 1) * cap, :]
            inside = jnp.logical_and(row >= s * cap, row < (s + 1) * cap)
            count = jnp.sum(jnp.where(inside, 1, 0), axis=1, keepdims=True)
            bias = jnp.where(place < count, 0.0, MASKED)
            extra = jnp.where(lane == 0, bias, jnp.where(lane < 4, 1.0, 0.0))
            kaug[c, s, r * cap:(r + 1) * cap, :] = extra.astype(BF)
        if r < 2:
            queries = (dot(wq_t[...], rows, NT) * factor).astype(BF)
            spread = dot(queries, hot, NT).astype(BF)
            for s in range(groups):
                qt[c, s, :, r * cap:(r + 1) * cap] = spread[:, s * cap:(s + 1) * cap]

    def near_rows(c, _):
        project(0, c)
        copy_to(normed.at[0, c], normed.at[1, c], sems_in, c, sibling).wait_recv()
        project(1, c)
        return 0

    for item in to_peers:
        item.wait_recv()
    lax.fori_loop(0, cubes, near_rows, 0)

    def attend(c, s):
        for p in range(packs):
            lanes = slice(p * pack, (p + 1) * pack)
            for j in range(per):
                qbd[p, j * hd:(j + 1) * hd, j * 2 * cap:(j + 1) * 2 * cap] = qt[
                    c, s, p * pack + j * hd:p * pack + (j + 1) * hd, :]
            vt[p, :pack, :] = kv[c, s, :, half + p * pack:half + (p + 1) * pack].T
            keys = jnp.concatenate([kv[c, s, :, lanes], kaug[c, s]], axis=1)
            scores = dot(keys, qbd[p])
            top = jnp.maximum(jnp.max(scores, axis=0, keepdims=True), FLOOR)
            probs = jnp.exp2(scores - top).astype(BF)
            mixed = dot(vt[p], probs)
            total = jnp.maximum(mixed[pack:pack + 1, :], 1e-30)
            lse[c, s, p:p + 1, :] = top + jnp.log2(total)
            scale = 1.0 / total
            for j in range(per):
                cols = slice(j * 2 * cap, (j + 1) * 2 * cap)
                ot[c, s, p * pack + j * hd:p * pack + (j + 1) * hd, :] = (
                    mixed[j * hd:(j + 1) * hd, cols] * scale[:, cols]
                ).astype(BF)

    def stores(c):
        pairs = [(ot.at[c], ot_out.at[c]), (kv.at[c], kv_out.at[c]), (kaug.at[c], kaug_out.at[c]),
                 (qt.at[c], qt_out.at[c]), (normed.at[:, c], normed_out.at[:, c])]
        return [pltpu.make_async_copy(src, dst, sems_store.at[c, k]) for k, (src, dst) in enumerate(pairs)]

    def attended_copy(c):
        return copy_to(away.at[c], att.at[c, mine, :], sems_att, c, sibling)

    def cube(c, _):
        copy_to(normed.at[0, c], normed.at[2, c], sems_in, cubes + c, across).wait_recv()
        forward = copy_to(normed.at[2, c], normed.at[3, c], sems_fwd, c, sibling)
        forward.start()
        project(2, c)
        forward.wait_recv()
        project(3, c)
        for item in stores(c)[1:]:
            item.start()

        def one(s, _):
            attend(c, s)
            return 0

        lax.fori_loop(0, groups, one, 0)
        for r in (1, 0):
            hot = onehot(dest[r, pl.ds(c, 1), :], slots)
            placed = jnp.concatenate(
                [ot[c, s, :, r * cap:(r + 1) * cap] for s in range(groups)], axis=1)
            rows = dot(placed, hot).astype(BF)
            if r == 1:
                away[c] = rows
                attended_copy(c).start()
            else:
                att[c, mine, :] = rows
        stores(c)[0].start()
        return 0

    lax.fori_loop(0, cubes, cube, 0)

    def finish(c, _):
        for item in stores(c):
            item.wait()
        attended_copy(c).wait()
        copy_to(normed.at[0, c], normed.at[2, c], sems_in, cubes + c, across).wait_send()
        copy_to(normed.at[0, c], normed.at[1, c], sems_in, c, sibling).wait_send()
        copy_to(normed.at[2, c], normed.at[3, c], sems_fwd, c, sibling).wait_send()
        return 0

    lax.fori_loop(0, cubes, finish, 0)
    for item in to_peers:
        item.wait_send()


def forward_call(enc, codes, gain, offset, mask_token, w_qkv, cubes, groups):
    tokens, width = enc.shape
    quarter = tokens // cubes
    cap = quarter // 3
    half = width // 2
    packs = half // 128
    wide = (128 // (width // HEADS)) * 2 * cap
    vmem = pl.BlockSpec(memory_space=pltpu.VMEM)
    far = pl.BlockSpec(memory_space=pl.ANY)
    shape = jax.ShapeDtypeStruct
    dma = pltpu.SemaphoreType.DMA
    return pl.pallas_call(
        forward_kernel,
        out_shape=(
            shape((cubes, width, quarter), BF),
            shape((groups, cubes, quarter, width), BF),
            shape((groups, 8, quarter), jnp.int32),
            shape((cubes, groups, groups * cap, width), BF),
            shape((cubes, groups, groups * cap, 128), BF),
            shape((cubes, groups, half, 2 * cap), BF),
            shape((cubes, groups, half, 2 * cap), BF),
            shape((cubes, groups, 8, wide), F32),
        ),
        in_specs=[vmem] * 5 + [far],
        out_specs=(vmem, far, vmem, far, far, far, far, vmem),
        scratch_shapes=[
            dma((3,)),
            pltpu.VMEM((groups, cubes, quarter, width), BF),
            pltpu.VMEM((cubes, groups, groups * cap, width), BF),
            pltpu.VMEM((cubes, groups, groups * cap, 128), BF),
            pltpu.VMEM((cubes, groups, half, 2 * cap), BF),
            pltpu.VMEM((cubes, groups, half, 2 * cap), BF),
            pltpu.VMEM((cubes, quarter, 1), F32),
            pltpu.VMEM((width, 3 * half), BF),
            pltpu.VMEM((half, width), BF),
            pltpu.VMEM((packs, 256, wide), BF),
            pltpu.VMEM((packs, 144, groups * cap), BF),
            pltpu.VMEM((cubes, half, quarter), BF),
            (dma((2 * cubes,)), dma((2 * cubes,))),
            (dma((3,)), dma((3,))),
            (dma((cubes,)), dma((cubes,))),
            (dma((cubes,)), dma((cubes,))),
            dma((cubes, 5)),
        ],
        compiler_params=pltpu.CompilerParams(
            collective_id=0, has_side_effects=True, vmem_limit_bytes=60 * 2**20),
        name="forward",
    )(enc, codes, gain, offset, mask_token, w_qkv)


def pieces(values):
    high = values.astype(BF)
    rest = values - high.astype(F32)
    mid = rest.astype(BF)
    low = (rest - mid.astype(F32)).astype(BF)
    return high, mid, low


def layer_kernel(
    n_dp, n_group,
    att_in, kv_in, kaug_in, qt_in, ot_in, lse, normed_in, dest, w_qkv, enc, visible, mask_token, gain,
    cot_in, w_out_in, w_up_in, w_down_in, gain2, offset2,
    out, grad_enc, sum_ffn, sum_qkv, sum_small,
    kv_at, kaug_at, qt_at, ot_at, normed_at, grads_at, turn, sems_read, sems_turn,
    cot, w_out, w_up, w_down, att, middle, second, backs, result, grads_sum, spare, w_mine, sems_load, sems_out,
    acc, give, pair, recv, settled, sems_core, sems_ffn,
    grad_qkv, small, send_qkv, recv_qkv, settled_qkv, small_bufs, sems_qkv, sems_pair, sems_small,
    columns, dot_slots, qbd, dobd, grad_qt, in_sib, in_fwd, in_across, sems_sib, sems_fwd, sems_across,
):
    cubes, quarter, width = middle.shape
    half = width // 2
    blocks = w_up.shape[0]
    groups = kv_at.shape[1]
    cap = qt_at.shape[3] // 2
    slots = groups * cap
    hd = width // HEADS
    pack = 128
    per = pack // hd
    packs = half // pack
    factor = hd ** -0.5
    sibling, across = peer((1,)), peer((2,))
    parity = lax.rem(lax.axis_index("group"), 2)
    mine = pl.ds(pl.multiple_of(parity * half, half), half)
    theirs = pl.ds(pl.multiple_of((1 - parity) * half, half), half)
    grad_kv, own_sum, out_fwd, out_sib, out_across = w_up, result, cot, second, backs

    core = ("group", 1)
    others = chip_bits(n_dp, n_group)
    paths = balanced_orders(others)
    qkv = [
        Butterfly(grad_qkv.at[p], send_qkv.at[p], recv_qkv.at[p], settled_qkv.at[p], sum_qkv.at[parity, p],
                  (sems_qkv[0].at[p], sems_qkv[1].at[p]), order)
        for p, order in enumerate(path_orders(others, 3))]
    qkv_steps = joined(reduce_steps(qkv), gather_steps(qkv))
    smalls = [
        SmallSum(small_bufs[k], (sems_small[0].at[k], sems_small[1].at[k]), names)
        for k, names in enumerate(small_groups(n_dp, n_group))]

    def place_of(j, side):
        if j < blocks:
            return sum_ffn.at[j + side * blocks]
        return sum_ffn.at[2 * blocks, pl.ds(pl.multiple_of(side * half, half), half)]

    def rows_in(j):
        return width if j < blocks else half

    def butterflies(j):
        count = rows_in(j)
        return [
            Butterfly(acc.at[j, :count, lanes_of(p)], give.at[j, :, lanes_of(p)], recv.at[j, :, lanes_of(p)],
                      settled.at[j, :count >> halvings_of(count, len(others)), lanes_of(p)],
                      place_of(j, parity).at[:, lanes_of(p)],
                      (sems_ffn[0].at[j, p], sems_ffn[1].at[j, p]), paths[p]) for p in range(PARTS)]

    def summing(j):
        count = rows_in(j)
        inner = reduce_steps(butterflies(j))
        exchange = copy_to(give.at[j, :count], pair.at[j, :count], sems_core, j, sibling)

        def second_step():
            exchange.wait()
            acc[j, :count] += pair[j, :count].astype(F32)
            inner[0]()

        return [exchange.start, second_step] + inner[1:]

    def spreading(sets):
        steps = gather_steps([b for j in sets for b in butterflies(j)])

        def exchanges():
            return [
                copy_to(place_of(j, parity), place_of(j, parity), sems_core, blocks + 1 + j, sibling) for j in sets]

        def last_but_one():
            steps[-1]()
            for item in exchanges():
                item.start()

        def final():
            for item in exchanges():
                item.wait()

        return steps[:-1] + [last_but_one, final]

    def reads(c):
        k = lax.rem(c, 2)
        pairs = [(kv_in.at[c], kv_at.at[k]), (kaug_in.at[c], kaug_at.at[k]), (qt_in.at[c], qt_at.at[k]),
                 (ot_in.at[c], ot_at.at[k]), (normed_in.at[:, c], normed_at.at[k])]
        return [pltpu.make_async_copy(src, dst, sems_read.at[k, n]) for n, (src, dst) in enumerate(pairs)]

    loads = [(w_out_in, w_out), (att_in, att)]
    loads += [(w_up_in.at[:, j * width:(j + 1) * width], w_up.at[j]) for j in range(blocks)]
    loads += [(w_down_in.at[j * width:(j + 1) * width, :], w_down.at[j]) for j in range(blocks)]
    loads += [(cot_in.at[c * quarter:(c + 1) * quarter, :], cot.at[c]) for c in range(cubes)]
    loads += [(w_qkv.at[:, pl.ds(pl.multiple_of(p * width + parity * half, half), half)],
               w_mine.at[:, p * half:(p + 1) * half]) for p in range(3)]
    loads = [pltpu.make_async_copy(src, dst, sems_load.at[k]) for k, (src, dst) in enumerate(loads)]
    for item in loads:
        item.start()
    for c in range(min(2, cubes)):
        for item in reads(c):
            item.start()

    meets = {}
    for names in small_groups(n_dp, n_group):
        for t in range(1, 1 << len(names)):
            chosen = [name for k, name in enumerate(names) if (t >> k) & 1]
            meets[tuple(sorted(chosen))] = flip(chosen)
    for chosen in [[core]] + [[name] for name in others] + [
            list(pair) for i, first in enumerate(others) for pair in ((first, other) for other in others[i + 1:])]:
        meets[tuple(sorted(chosen))] = flip(chosen)
    greet(list(meets.values()))

    one_row = lax.broadcasted_iota(jnp.int32, (16, per * 2 * cap), 0)
    for p in range(packs):
        qbd[p] = jnp.zeros(qbd.shape[1:], BF)
        dobd[p] = jnp.zeros(dobd.shape[1:], BF)
    as_columns(visible, columns)
    grad_qkv[...] = jnp.zeros(grad_qkv.shape, F32)
    small[...] = jnp.zeros(small.shape, F32)

    def rows_of(c):
        return pl.ds(c * quarter, quarter)

    def start_rows(c):
        shown = columns[c] == 1.0
        return shown, jnp.where(shown, enc[rows_of(c), :].astype(F32), mask_token[...])

    def turn_copy(c):
        return copy_to(turn.at[c], grads_at.at[c, 1], sems_turn, c, sibling)

    def out_copy(c):
        return pltpu.make_async_copy(second.at[c], out.at[rows_of(c), :], sems_out.at[0, c])

    def enc_copy(c):
        return pltpu.make_async_copy(second.at[c], grad_enc.at[rows_of(c), :], sems_out.at[1, c])

    def enter(c, _):
        value = start_rows(c)[1] + dot(att[c], w_out[...], TN)
        middle[c] = value
        normal, _ = norm_stats(value)
        second[c] = (normal * gain2[...] + offset2[...]).astype(BF)
        return 0

    def block(j, c):
        rows, cotan = second[c], cot[c]
        hidden = dot(rows, w_up[j])
        square = hidden * hidden
        tanh = jnp.tanh(hidden * (GELU_A + GELU_B * square))
        slope = 0.5 * (1.0 + tanh)
        active = (hidden * slope).astype(BF)
        slope = slope + 0.5 * hidden * (1.0 - tanh * tanh) * (GELU_A + 3.0 * GELU_B * square)
        grad_hidden = (dot(cotan, w_down[j], NT) * slope).astype(BF)
        grad_up = dot(rows, grad_hidden, TN)
        grad_down = dot(active, cotan, TN)
        kept = jnp.where(parity == 0, grad_up, grad_down)
        given = jnp.where(parity == 0, grad_down, grad_up)
        outcome = dot(active, w_down[j])
        grads = dot(grad_hidden, w_up[j], NT)
        result[c] = outcome + jnp.where(j > 0, result[c], 0.0)
        grads_sum[c] = grads + jnp.where(j > 0, grads_sum[c], 0.0)
        acc[j] = kept + jnp.where(c > 0, acc[j], 0.0)
        spare[...] = given + jnp.where(c > 0, spare[...], 0.0)

        def hand_over():
            give[j, :width] = spare[...].astype(BF)

        pl.when(c == cubes - 1)(hand_over)

    def leave(c):
        second[c] = (middle[c] + result[c]).astype(BF)
        out_copy(c).start()
        normal, recip = norm_stats(middle[c])
        grads = grads_sum[c]
        small[3:4, :] += jnp.sum(grads * normal, axis=0, keepdims=True)
        small[4:5, :] += jnp.sum(grads, axis=0, keepdims=True)
        total = cot[c].astype(F32) + norm_back(grads, normal, recip, gain2[...])
        middle[c] = total
        branch = total.astype(BF)
        back = dot(w_out[...], branch, NT).astype(BF)
        backs[c] = branch
        turn[c] = jnp.where(parity == 0, back[half:], back[:half])
        grads_at[c, 0] = jnp.where(parity == 0, back[:half], back[half:])
        turn_copy(c).start()

    def out_weights():
        total = dot(att[0], backs[0])
        for c in range(1, cubes):
            total += dot(att[c], backs[c])
        acc[blocks, :half] = jnp.where(parity == 0, total[:half], total[half:])
        give[blocks, :half] = jnp.where(parity == 0, total[half:], total[:half]).astype(BF)

    firsts = [summing(j) for j in range(blocks + 1)]
    seconds = [spreading(sets) for sets in SPREADS]
    plan = []
    for number, (steps, places) in enumerate(zip(firsts + seconds, SUM_AT + SPREAD_AT)):
        if len(places) != len(steps):
            places = [places[0] + 2 * k for k in range(len(steps))]
        stage = 0 if number < len(firsts) else len(steps)
        plan += [(place, stage + k, number, step) for k, (place, step) in enumerate(zip(places, steps))]
    plan = [(entry[0], entry[-1]) for entry in sorted(plan, key=lambda entry: entry[:3])]
    lead = blocks * cubes + cubes + 1

    def advance(place):
        for at, step in plan:
            if at == place:
                step()

    for item in loads[:2]:
        item.wait()
    lax.fori_loop(0, cubes, enter, 0)
    for item in loads[2:]:
        item.wait()
    place = blocks * cubes

    def blocks_step(u, _):
        block(u // cubes, lax.rem(u, cubes))
        for at, step in plan:
            if at <= place:
                pl.when(u == at - 1)(step)
        return 0

    lax.fori_loop(0, place, blocks_step, 0)
    for c in range(cubes):
        leave(c)
        place += 1
        advance(place)
    out_weights()
    place += 1
    advance(place)
    for c in range(cubes):
        out_copy(c).wait()

    def extra_rows(first, values):
        high, mid, low = pieces(-values)
        rows = jnp.where(
            one_row == 0, first,
            jnp.where(one_row == 1, high.astype(F32),
                      jnp.where(one_row == 2, mid.astype(F32),
                                jnp.where(one_row == 3, low.astype(F32), 0.0))))
        return rows.astype(BF)

    def attend_back(c, s):
        slot = lax.rem(c, 2)
        for p in range(packs):
            lanes = slice(p * pack, (p + 1) * pack)
            deltas = []
            for j in range(per):
                rows = slice(p * pack + j * hd, p * pack + (j + 1) * hd)
                cols = slice(j * 2 * cap, (j + 1) * 2 * cap)
                qbd[p, j * hd:(j + 1) * hd, cols] = qt_at[slot, s, rows, :]
                grads = dot_slots[s, rows, :]
                dobd[p, j * hd:(j + 1) * hd, cols] = grads
                deltas.append(jnp.sum(
                    grads.astype(F32) * ot_at[slot, s, rows, :].astype(F32), axis=0, keepdims=True))
            qbd[p, pack:pack + 16, :] = extra_rows(1.0, lse[c, s, p:p + 1, :])
            dobd[p, pack:pack + 16, :] = extra_rows(0.0, jnp.concatenate(deltas, axis=1))
            extra = kaug_at[slot, s]
            keys = kv_at[slot, s, :, lanes]
            values = kv_at[slot, s, :, half + p * pack:half + (p + 1) * pack]
            probs = jnp.exp2(dot(jnp.concatenate([keys, extra], axis=1), qbd[p]))
            centred = dot(jnp.concatenate([values, extra], axis=1), dobd[p])
            grad_scores = (probs * centred).astype(BF)
            grad_kv[s, :, half + p * pack:half + (p + 1) * pack] = dot(
                probs.astype(BF), dobd[p, :pack, :], NT).astype(BF)
            grad_kv[s, :, lanes] = (dot(grad_scores, qbd[p, :pack, :], NT) * LN2).astype(BF)
            mixed = dot(keys.T, grad_scores) * factor
            for j in range(per):
                rows = slice(p * pack + j * hd, p * pack + (j + 1) * hd)
                cols = slice(j * 2 * cap, (j + 1) * 2 * cap)
                grad_qt[s, rows, :] = mixed[j * hd:(j + 1) * hd, cols].astype(BF)

    def back_rows(r, c):
        hot = onehot(dest[r, pl.ds(c, 1), :], slots)
        placed = jnp.concatenate(
            [grad_kv[s, r * cap:(r + 1) * cap, :] for s in range(groups)], axis=0)
        grads = dot(hot, placed, TN).astype(BF)
        if r < 2:
            queries = jnp.concatenate(
                [grad_qt[s, :, r * cap:(r + 1) * cap] for s in range(groups)], axis=1)
            queries = dot(queries, hot).T.astype(BF)
            grads = jnp.concatenate([queries, grads], axis=1)
        weight = dot(normed_at[lax.rem(c, 2), r], grads, TN)
        first = 3 - weight.shape[1] // half
        for k in range(first, 3):
            grad_qkv[k] += weight[:, (k - first) * half:(k - first + 1) * half]
        return grads

    def back_project(r, c):
        grads = back_rows(r, c)
        return dot(grads, w_mine[:, 3 * half - grads.shape[1]:], NT)

    def prepare(c):
        for item in reads(c):
            item.wait()
        for r in range(2):
            rows = grads_at[c, r]
            hot = onehot(dest[r, pl.ds(c, 1), :], slots)
            spread = dot(rows, hot, NT).astype(BF)
            for s in range(groups):
                dot_slots[s, :, r * cap:(r + 1) * cap] = spread[:, s * cap:(s + 1) * cap]

    def cube(c, _):
        def point(i):
            for at, step in plan:
                if at > lead and (at - lead - 1) % POINTS == i and (at - lead - 1) // POINTS < cubes:
                    pl.when(c == (at - lead - 1) // POINTS)(step)

        turn_copy(c).wait()
        prepare(c)
        point(0)

        def one(s, _):
            attend_back(c, s)
            for i in range(groups):
                pl.when(s == i)(functools.partial(point, i + 1))
            return 0

        lax.fori_loop(0, groups, one, 0)
        out_fwd[c] = back_project(3, c).astype(BF)
        forward = copy_to(out_fwd.at[c], in_fwd.at[c], sems_fwd, c, sibling)
        forward.start()
        point(5)
        partial = back_project(2, c)
        forward.wait_recv()
        out_across[c] = (partial + in_fwd[c].astype(F32)).astype(BF)
        copy_to(out_across.at[c], in_across.at[c], sems_across, c, across).start()
        point(6)
        near_rows = back_rows(1, c)
        own_rows = back_rows(0, c)
        pl.when(c == cubes - 1)(qkv_steps[0])
        point(7)
        out_sib[c] = dot(near_rows, w_mine[...], NT).astype(BF)
        copy_to(out_sib.at[c], in_sib.at[c], sems_sib, c, sibling).start()
        own_sum[c] = dot(own_rows, w_mine[...], NT)

        def more():
            for item in reads(c + 2):
                item.start()

        pl.when(c + 2 < cubes)(more)
        point(8)
        return 0

    lax.fori_loop(0, cubes, cube, 0)
    tail = [(at - lead - POINTS * cubes, step) for at, step in plan if at > lead + POINTS * cubes]

    def last(c):
        copy_to(out_sib.at[c], in_sib.at[c], sems_sib, c, sibling).wait()
        copy_to(out_across.at[c], in_across.at[c], sems_across, c, across).wait()
        copy_to(out_fwd.at[c], in_fwd.at[c], sems_fwd, c, sibling).wait_send()
        grads = own_sum[c] + in_sib[c].astype(F32) + in_across[c].astype(F32)
        shown, start = start_rows(c)
        normal, recip = norm_stats(start)
        small[0:1, :] += jnp.sum(grads * normal, axis=0, keepdims=True)
        small[1:2, :] += jnp.sum(grads, axis=0, keepdims=True)
        total = middle[c] + norm_back(grads, normal, recip, gain[...])
        second[c] = jnp.where(shown, total, 0.0).astype(BF)
        enc_copy(c).start()
        small[2:3, :] += jnp.sum(jnp.where(shown, 0.0, total), axis=0, keepdims=True)

    fill = list(range(cubes))
    pending = []

    def small_step():
        total = smalls[pending[0]].finish()
        pending.append(pending.pop(0) + 1)
        if pending[0] < len(smalls):
            smalls[pending[0]].start(total)
        else:
            pending.clear()
            sum_small[...] = total

    for k in range(1, len(qkv_steps)):
        if fill:
            last(fill.pop(0))
            if not fill:
                smalls[0].start(small[...])
                pending.append(0)
            qkv_steps[k]()
        else:
            qkv_steps[k]()
            if pending:
                small_step()
        while tail and tail[0][0] <= k:
            tail.pop(0)[1]()
    pair_qkv = copy_to(sum_qkv.at[parity], sum_qkv.at[parity], sems_pair, 0, sibling)
    pair_qkv.start()
    for _, step in tail:
        step()
    while pending:
        small_step()
    for c in range(cubes):
        enc_copy(c).wait()
    pair_qkv.wait()


POINTS = 9
PARTS = 4
SUM_AT = [
    [3, 5, 9, 12, 16],
    [6, 8, 12, 17, 20],
    [9, 11, 15, 19, 22],
    [12, 14, 18, 21, 25],
    [16, 18, 21, 26, 29],
]
SPREADS = [[0], [1], [2], [3], [4]]
SPREAD_AT = [
    [16, 20, 23, 28, 30],
    [20, 24, 28, 32, 34],
    [22, 27, 30, 35, 37],
    [25, 29, 33, 37, 39],
    [29, 33, 37, 39, 41],
]


def layer_call(
    att, kv, kaug, qt, ot, lse, normed, dest, w_qkv, enc, visible, mask_token, gain,
    cot, w_out, w_up, w_down, gain2, offset2, n_dp, n_group,
):
    cubes, width, quarter = att.shape
    groups = kv.shape[1]
    cap = quarter // 3
    half = width // 2
    packs = half // 128
    wide = (128 // (width // HEADS)) * 2 * cap
    blocks = w_up.shape[1] // width
    vmem = pl.BlockSpec(memory_space=pltpu.VMEM)
    far = pl.BlockSpec(memory_space=pl.ANY)
    shape = jax.ShapeDtypeStruct
    dma = pltpu.SemaphoreType.DMA
    rows = pltpu.VMEM((cubes, quarter, width), BF)
    sums = pltpu.VMEM((cubes, quarter, width), F32)
    squares = pltpu.VMEM((blocks, width, width), BF)
    pair = (dma((cubes,)), dma((cubes,)))
    stages = len(chip_bits(n_dp, n_group))
    staging = staging_rows(width, stages)
    kept = max(width >> halvings_of(width, stages), half >> halvings_of(half, stages))
    kept_qkv = width >> halvings_of(width, stages)
    small = small_groups(n_dp, n_group)
    return pl.pallas_call(
        functools.partial(layer_kernel, n_dp, n_group),
        out_shape=(
            shape(enc.shape, BF),
            shape(enc.shape, BF),
            shape((2 * blocks + 1, width, width), BF),
            shape((2, 3, width, half), BF),
            shape((8, width), F32),
        ),
        in_specs=[far] * 5 + [vmem, far, vmem, far] + [vmem] * 4 + [far] * 4 + [vmem] * 2,
        out_specs=(far, far, far, far, vmem),
        scratch_shapes=[
            pltpu.VMEM((2,) + kv.shape[1:], BF),
            pltpu.VMEM((2,) + kaug.shape[1:], BF),
            pltpu.VMEM((2,) + qt.shape[1:], BF),
            pltpu.VMEM((2,) + ot.shape[1:], BF),
            pltpu.VMEM((2, groups, quarter, width), BF),
            pltpu.VMEM((cubes, 2, half, quarter), BF),
            pltpu.VMEM((cubes, half, quarter), BF),
            dma((2, 5)),
            pair,
            rows,
            pltpu.VMEM(w_out.shape, BF),
            squares,
            squares,
            pltpu.VMEM(att.shape, BF),
            sums,
            rows,
            rows,
            sums,
            sums,
            pltpu.VMEM((width, width), F32),
            pltpu.VMEM((width, 3 * half), BF),
            dma((2 + 2 * blocks + cubes + 3,)),
            dma((2, cubes)),
            pltpu.VMEM((blocks + 1, width, width), F32),
            pltpu.VMEM((blocks + 1, max(width, staging), width), BF),
            pltpu.VMEM((blocks + 1, width, width), BF),
            pltpu.VMEM((blocks + 1, staging, width), BF),
            pltpu.VMEM((blocks + 1, kept, width), BF),
            (dma((2 * blocks + 2,)), dma((2 * blocks + 2,))),
            (dma((blocks + 1, PARTS, 2 * stages + 3)), dma((blocks + 1, PARTS, 2 * stages + 3))),
            pltpu.VMEM((3, width, half), F32),
            pltpu.VMEM((8, width), F32),
            pltpu.VMEM((3, staging, half), BF),
            pltpu.VMEM((3, staging, half), BF),
            pltpu.VMEM((3, kept_qkv, half), BF),
            tuple(pltpu.VMEM((1 << len(names), 8, width), F32) for names in small),
            (dma((3, 2 * stages + 3)), dma((3, 2 * stages + 3))),
            (dma((1,)), dma((1,))),
            (dma((len(small), 8)), dma((len(small), 8))),
            pltpu.VMEM((cubes, quarter, 1), F32),
            pltpu.VMEM((groups, half, 2 * cap), BF),
            pltpu.VMEM((packs, 256, wide), BF),
            pltpu.VMEM((packs, 256, wide), BF),
            pltpu.VMEM((groups, half, 2 * cap), BF),
            rows, rows, rows,
            pair, pair, pair,
        ],
        compiler_params=pltpu.CompilerParams(
            collective_id=1, has_side_effects=True, vmem_limit_bytes=63 * 2**20),
        name="layer",
    )(att, kv, kaug, qt, ot, lse, normed, dest, w_qkv, enc, visible, mask_token, gain,
      cot, w_out, w_up, w_down, gain2, offset2)


def cast_kernel(ups, downs, outs, qkvs, up, down, out, qkv):
    width, half = outs.shape[1], qkvs.shape[3]
    for k in range(ups.shape[0]):
        up[:, k * width:(k + 1) * width] = ups[k].astype(F32)
    down[...] = downs[...].astype(F32)
    out[...] = outs[...].astype(F32)
    for part in range(3):
        for side in range(2):
            at = part * width + side * half
            qkv[:, at:at + half] = qkvs[side, part].astype(F32)


def cast_call(ffn, qkv):
    width = qkv.shape[2]
    blocks = ffn.shape[0] // (2 * width)
    steps = 2
    rows = width // steps
    tall = blocks * rows
    shape = jax.ShapeDtypeStruct
    return pl.pallas_call(
        cast_kernel,
        grid=(steps,),
        in_specs=[
            pl.BlockSpec((blocks, rows, width), lambda i: (0, i, 0)),
            pl.BlockSpec((tall, width), lambda i: (steps + i, 0)),
            pl.BlockSpec((rows, width), lambda i: (2 * blocks * steps + i, 0)),
            pl.BlockSpec((2, 3, rows, width // 2), lambda i: (0, 0, i, 0)),
        ],
        out_specs=[
            pl.BlockSpec((rows, blocks * width), lambda i: (i, 0)),
            pl.BlockSpec((tall, width), lambda i: (i, 0)),
            pl.BlockSpec((rows, width), lambda i: (i, 0)),
            pl.BlockSpec((rows, 3 * width), lambda i: (i, 0)),
        ],
        out_shape=(
            shape((width, blocks * width), F32),
            shape((blocks * width, width), F32),
            shape((width, width), F32),
            shape((width, 3 * width), F32),
        ),
        name="cast",
    )(ffn.reshape(2 * blocks + 1, width, width), ffn, ffn, qkv)


def on_device(
    enc, visible, band_group, cotangent, ln1_gain, ln1_bias, w_qkv, w_out,
    ln2_gain, ln2_bias, w_up, w_down, mask_token,
):
    groups = lax.axis_size("group")
    tok_dev, width = enc.shape
    quarter = CUBE_TOK // groups
    cubes = tok_dev // quarter
    codes = (visible * 8 + band_group).reshape(cubes, quarter)
    gain1, mask_row = ln1_gain[None, :], mask_token[None, :]
    att, normed, dest, kv, kaug, qt, ot, lse = forward_call(
        enc, codes, gain1, ln1_bias[None, :], mask_row, w_qkv, cubes, groups)
    out, grad_enc, sum_ffn, sum_qkv, small = layer_call(
        att, kv, kaug, qt, ot, lse, normed, dest, w_qkv, enc, codes, mask_row, gain1, cotangent, w_out, w_up,
        w_down, ln2_gain[None, :], ln2_bias[None, :], lax.axis_size("dp"), groups)
    sum_up, sum_down, sum_out, sum_w_qkv = cast_call(sum_ffn.reshape(9 * width, width), sum_qkv)
    return (
        out, grad_enc, small[0], small[1], sum_w_qkv, sum_out, small[3], small[4], sum_up, sum_down, small[2])


def solution(mesh):
    rows, line = P(("dp", "group"), None), P(("dp", "group"))
    return jax.shard_map(
        on_device, mesh=mesh, in_specs=(rows, line, line, rows) + (P(),) * 9,
        out_specs=(rows, rows) + (P(),) * 9, check_vma=False)
```

```python
import functools
import jax
import jax.numpy as jnp
from jax import lax
from jax.experimental import pallas as pl
from jax.experimental.pallas import tpu as pltpu
from jax.sharding import PartitionSpec as P

HEADS = 16
CUBE_TOK = 1536
EPS = 1e-05
LOG2E = 1.4426950408889634
LN2 = 0.6931471805599453
GELU_A = 0.7978845608028654
GELU_B = 0.7978845608028654 * 0.044715
FLOOR = -1e20
MASKED = -1e30

NN = (((1,), (0,)), ((), ()))
NT = (((1,), (1,)), ((), ()))
TN = (((0,), (0,)), ((), ()))
MESH = pl.DeviceIdType.MESH
BF = jnp.bfloat16
F32 = jnp.float32


def dot(left, right, dims=NN):
    return lax.dot_general(left, right, dims, preferred_element_type=F32)


def norm_stats(values):
    centre = values - jnp.mean(values, axis=-1, keepdims=True)
    spread = jnp.mean(centre * centre, axis=-1, keepdims=True)
    recip = lax.rsqrt(spread + EPS)
    return centre * recip, recip


def norm_back(grad_rows, normal, recip, gain):
    scaled = grad_rows * gain
    return recip * (
        scaled
        - jnp.mean(scaled, axis=-1, keepdims=True)
        - normal * jnp.mean(scaled * normal, axis=-1, keepdims=True)
    )


def onehot(dest_row, slots):
    rows = lax.broadcasted_iota(jnp.int32, (slots, dest_row.shape[1]), 0)
    return jnp.where(rows == dest_row, 1.0, 0.0).astype(BF)


def peer(bits):
    me = lax.axis_index("group")
    for bit in bits:
        me = me + (1 - 2 * (lax.rem(me // bit, 2))) * bit
    return (lax.axis_index("dp"), me)


def copy_to(src, dst, sems, index, device):
    return pltpu.make_async_remote_copy(
        src_ref=src, dst_ref=dst, send_sem=sems[0].at[index], recv_sem=sems[1].at[index],
        device_id=device, device_id_type=MESH,
    )


def greet(devices):
    barrier = pltpu.get_barrier_semaphore()
    for device in devices:
        pl.semaphore_signal(barrier, inc=1, device_id=device, device_id_type=MESH)
    pl.semaphore_wait(barrier, len(devices))


def own_dest(ids, capacity, groups):
    tokens = ids.shape[1]
    upper = (
        lax.broadcasted_iota(jnp.int32, (tokens, tokens), 0)
        < lax.broadcasted_iota(jnp.int32, (tokens, tokens), 1)
    )
    upper = jnp.where(upper, 1.0, 0.0).astype(BF)
    total = jnp.zeros(ids.shape, F32)
    for group in range(groups):
        hit = jnp.where(ids == group, 1.0, 0.0)
        ranks = dot(hit.astype(BF), upper)
        total = total + hit * (ranks + float(group * capacity))
    return total.astype(jnp.int32)


def bits_of(size):
    return [1 << k for k in range(size.bit_length() - 1)]


def bit_value(name):
    axis, bit = name
    return lax.rem(lax.axis_index(axis) // bit, 2)


def flip(names):
    place = {axis: lax.axis_index(axis) for axis in ("dp", "group")}
    for axis, bit in names:
        place[axis] = place[axis] + (1 - 2 * bit_value((axis, bit))) * bit
    return (place["dp"], place["group"])


class Butterfly:
    def __init__(self, acc, send, recv, settled, out, sems, names):
        self.acc, self.send, self.recv, self.settled, self.out = acc, send, recv, settled, out
        self.sems, self.names = sems, names
        self.rows = acc.shape[0]
        self.halvings = halvings_of(self.rows, len(names))
        self.groups = [[name] for name in names]
        if self.halvings >= 4:
            last = names[self.halvings - 2:self.halvings]
            self.groups[self.halvings - 2:self.halvings] = [last]
        self.legs = sum((1 << len(group)) - 1 for group in self.groups)
        self.halving_groups = [
            g for g in range(len(self.groups)) if self.done(g) < self.halvings]

    def done(self, g):
        return sum(len(group) for group in self.groups[:g])

    def start_row(self, k):
        low = 0
        for j in range(min(k, self.halvings)):
            low = low + bit_value(self.names[j]) * (self.rows >> (j + 1))
        return low

    def span(self, low, count):
        return pl.ds(pl.multiple_of(low, 16), count)

    def partners(self, g):
        names, done = self.groups[g], self.done(g)
        number = sum((1 << len(group)) - 1 for group in self.groups[:g])
        found = []
        for t in range(1, 1 << len(names)):
            low = self.start_row(done)
            if done < self.halvings:
                for k, name in enumerate(names):
                    value = 1 - bit_value(name) if (t >> k) & 1 else bit_value(name)
                    low = low + value * (self.rows >> (done + k + 1))
            found.append(([name for k, name in enumerate(names) if (t >> k) & 1], number + t - 1, low))
        return found

    def hops(self, g):
        done, size = self.done(g), len(self.groups[g])
        if done < self.halvings:
            count = self.rows >> (done + size)
            at = self.rows - (self.rows >> done)
        else:
            count = self.rows >> self.halvings
            at = self.rows + (done - self.halvings - 1) * count
        found = []
        for n, (names, number, low) in enumerate(self.partners(g)):
            where = pl.ds(at + n * count, count)
            item = copy_to(self.send.at[where], self.recv.at[where], self.sems, number, flip(names))
            found.append((item, where, self.span(low, count)))
        return found, count

    def reduce_start(self, g):
        for item, where, rows in self.hops(g)[0]:
            self.send[where, :] = self.acc[rows, :].astype(BF)
            item.start()

    def reduce_finish(self, g):
        found, count = self.hops(g)
        rows = self.span(self.start_row(self.done(g) + len(self.groups[g])), count)
        for item, where, _ in found:
            item.wait()
        for _, where, _ in found:
            if self.done(g) < self.halvings:
                self.acc[rows, :] += self.recv[where, :].astype(F32)
            else:
                self.acc[rows, :] = self.send[where, :].astype(F32) + self.recv[where, :].astype(F32)

    def own_piece(self):
        return self.span(self.start_row(self.halvings), self.rows >> self.halvings)

    def keep(self):
        return pltpu.make_async_copy(
            self.settled, self.out.at[self.own_piece(), :], self.sems[0].at[2 * self.legs])

    def settle(self):
        self.settled[...] = self.acc[self.own_piece(), :].astype(BF)
        self.keep().start()

    def gather(self, g):
        done = self.done(g) + len(self.groups[g])
        rows = self.span(self.start_row(done), self.rows >> done)
        src = self.settled if done == self.halvings else self.out.at[rows, :]
        return [
            copy_to(src, self.out.at[rows, :], self.sems, self.legs + number, flip(names))
            for names, number, _ in self.partners(g)]


def halvings_of(rows, stages):
    count = 0
    while count < stages and (rows >> (count + 1)) % 16 == 0:
        count += 1
    return count


def staging_rows(rows, stages):
    count = halvings_of(rows, stages)
    return rows + (stages - count - 1) * (rows >> count)


def reduce_steps(butterflies):
    stages = len(butterflies[0].groups)

    def first():
        for b in butterflies:
            b.reduce_start(0)

    steps = [first]
    for g in range(stages):
        def step(g=g):
            for b in butterflies:
                b.reduce_finish(g)
                if g + 1 < stages:
                    b.reduce_start(g + 1)
                else:
                    b.settle()
        steps.append(step)
    return steps


def gather_steps(butterflies):
    last = butterflies[0].halving_groups[-1]

    def start(b, g):
        for item in b.gather(g):
            item.start()

    def first():
        for b in butterflies:
            start(b, last)

    steps = [first]
    for g in range(last, -1, -1):
        def step(g=g):
            for b in butterflies:
                for item in b.gather(g):
                    item.wait()
                if g == last:
                    b.keep().wait()
                if g > 0:
                    start(b, g - 1)
        steps.append(step)
    return steps


def joined(before, after):
    def both():
        before[-1]()
        after[0]()

    return before[:-1] + [both] + after[1:]


def path_orders(names, count):
    head, tail = names[:count], names[count:]
    return [head[k:] + head[:k] + tail for k in range(count)]


def balanced_orders(names):
    first, second, third, tail = names[0], names[1], names[2], names[3:]
    return [[second, first, third] + tail, [second, third, first] + tail] + [[third, second, first] + tail] * 2


def chip_bits(n_dp, n_group):
    return [("group", b) for b in bits_of(n_group) if b > 1] + [("dp", b) for b in bits_of(n_dp)]


def lanes_of(p):
    return slice(p * 128, (p + 1) * 128)


PARTS = 4

def small_groups(n_dp, n_group):
    names = [("group", b) for b in bits_of(n_group)] + [("dp", b) for b in bits_of(n_dp)]
    groups = [names[:3]]
    rest = names[3:]
    while rest:
        groups.append(rest[:2])
        rest = rest[2:]
    return groups


class SmallSum:
    def __init__(self, buf, sems, names):
        self.buf, self.sems, self.names = buf, sems, names
        self.count = 1 << len(names)

    def copies(self):
        place = 0
        for k, name in enumerate(self.names):
            place = place + bit_value(name) * (1 << k)
        items = []
        for t in range(1, self.count):
            others = [name for k, name in enumerate(self.names) if (t >> k) & 1]
            items.append(copy_to(self.buf.at[place], self.buf.at[place], self.sems, t, flip(others)))
        return place, items

    def start(self, values):
        place, items = self.copies()
        self.buf[place] = values
        for item in items:
            item.start()

    def finish(self):
        _, items = self.copies()
        for item in items:
            item.wait()
        total = self.buf[0]
        for j in range(1, self.count):
            total = total + self.buf[j]
        return total


def as_columns(codes, columns):
    shown = jnp.where(codes[...] >= 8, 1.0, 0.0)
    shown = jnp.concatenate([shown, jnp.zeros((8 - shown.shape[0], shown.shape[1]), F32)], axis=0).T
    for c in range(codes.shape[0]):
        columns[c] = shown[:, c:c + 1]


def forward_kernel(
    enc, codes, gain, offset, mask_token, w_qkv,
    att, normed_out, dest, kv_out, kaug_out, qt_out, ot_out, lse,
    sems_load,
    normed, kv, kaug, qt, ot, columns, w_mine, wq_t, qbd, vt, away, sems_in, sems_dest, sems_fwd, sems_att, sems_store,
):
    cubes, quarter = normed.shape[1], normed.shape[2]
    width = enc.shape[1]
    half = width // 2
    groups = kv.shape[1]
    cap = qt.shape[3] // 2
    slots = groups * cap
    hd = width // HEADS
    pack = 128
    per = pack // hd
    packs = half // pack
    factor = LOG2E * hd ** -0.5
    sibling, across, cross = peer((1,)), peer((2,)), peer((1, 2))
    parity = lax.rem(lax.axis_index("group"), 2)

    mine = pl.ds(pl.multiple_of(parity * half, half), half)

    loads = [pltpu.make_async_copy(w_qkv.at[:, pl.ds(pl.multiple_of(p * width + parity * half, half), half)],
                                   w_mine.at[:, p * half:(p + 1) * half], sems_load.at[p]) for p in range(3)]
    for item in loads:
        item.start()

    greet([sibling, across, cross])

    dest[0] = jnp.zeros(dest.shape[1:], jnp.int32)
    dest[0, :cubes] = own_dest(codes[...] & 7, cap, groups)
    as_columns(codes, columns)
    to_peers = []
    for index, device in enumerate((sibling, across, cross)):
        item = copy_to(dest.at[0], dest.at[index + 1], sems_dest, index, device)
        item.start()
        to_peers.append(item)

    def start_rows(c):
        rows = enc[pl.ds(c * quarter, quarter), :].astype(F32)
        return jnp.where(columns[c] == 1.0, rows, mask_token[...])

    def own_rows(c, _):
        normal, _ = norm_stats(start_rows(c))
        normed[0, c] = (normal * gain[...] + offset[...]).astype(BF)
        copy_to(normed.at[0, c], normed.at[2, c], sems_in, cubes + c, across).start()
        copy_to(normed.at[0, c], normed.at[1, c], sems_in, c, sibling).start()
        return 0

    lax.fori_loop(0, cubes, own_rows, 0)

    for item in loads:
        item.wait()
    wq_t[...] = w_mine[:, :half].T

    one_row = lax.broadcasted_iota(jnp.int32, (16, per * 2 * cap), 0)
    for p in range(packs):
        qbd[p] = jnp.zeros(qbd.shape[1:], BF)
        qbd[p, pack:pack + 16, :] = jnp.where(one_row == 0, 1.0, 0.0).astype(BF)
        vt[p, pack:pack + 16, :] = jnp.ones((16, vt.shape[2]), BF)

    def project(r, c):
        rows = normed[r, c]
        row = dest[r, pl.ds(c, 1), :]
        hot = onehot(row, slots)
        values = dot(rows, w_mine[:, half:]).astype(BF)
        placed = dot(hot, values).astype(BF)
        lane = lax.broadcasted_iota(jnp.int32, (cap, 128), 1)
        place = lax.broadcasted_iota(jnp.int32, (cap, 128), 0)
        for s in range(groups):
            kv[c, s, r * cap:(r + 1) * cap, :] = placed[s * cap:(s + 1) * cap, :]
            inside = jnp.logical_and(row >= s * cap, row < (s + 1) * cap)
            count = jnp.sum(jnp.where(inside, 1, 0), axis=1, keepdims=True)
            bias = jnp.where(place < count, 0.0, MASKED)
            extra = jnp.where(lane == 0, bias, jnp.where(lane < 4, 1.0, 0.0))
            kaug[c, s, r * cap:(r + 1) * cap, :] = extra.astype(BF)
        if r < 2:
            queries = (dot(wq_t[...], rows, NT) * factor).astype(BF)
            spread = dot(queries, hot, NT).astype(BF)
            for s in range(groups):
                qt[c, s, :, r * cap:(r + 1) * cap] = spread[:, s * cap:(s + 1) * cap]

    def near_rows(c, _):
        project(0, c)
        copy_to(normed.at[0, c], normed.at[1, c], sems_in, c, sibling).wait_recv()
        project(1, c)
        return 0

    for item in to_peers:
        item.wait_recv()
    lax.fori_loop(0, cubes, near_rows, 0)

    def attend(c, s):
        for p in range(packs):
            lanes = slice(p * pack, (p + 1) * pack)
            for j in range(per):
                qbd[p, j * hd:(j + 1) * hd, j * 2 * cap:(j + 1) * 2 * cap] = qt[
                    c, s, p * pack + j * hd:p * pack + (j + 1) * hd, :]
            vt[p, :pack, :] = kv[c, s, :, half + p * pack:half + (p + 1) * pack].T
            keys = jnp.concatenate([kv[c, s, :, lanes], kaug[c, s]], axis=1)
            scores = dot(keys, qbd[p])
            top = jnp.maximum(jnp.max(scores, axis=0, keepdims=True), FLOOR)
            probs = jnp.exp2(scores - top).astype(BF)
            mixed = dot(vt[p], probs)
            total = jnp.maximum(mixed[pack:pack + 1, :], 1e-30)
            lse[c, s, p:p + 1, :] = top + jnp.log2(total)
            scale = 1.0 / total
            for j in range(per):
                cols = slice(j * 2 * cap, (j + 1) * 2 * cap)
                ot[c, s, p * pack + j * hd:p * pack + (j + 1) * hd, :] = (
                    mixed[j * hd:(j + 1) * hd, cols] * scale[:, cols]
                ).astype(BF)

    def stores(c):
        pairs = [(ot.at[c], ot_out.at[c]), (kv.at[c], kv_out.at[c]), (kaug.at[c], kaug_out.at[c]),
                 (qt.at[c], qt_out.at[c]), (normed.at[:, c], normed_out.at[:, c])]
        return [pltpu.make_async_copy(src, dst, sems_store.at[c, k]) for k, (src, dst) in enumerate(pairs)]

    def attended_copy(c):
        return copy_to(away.at[c], att.at[c, mine, :], sems_att, c, sibling)

    def cube(c, _):
        copy_to(normed.at[0, c], normed.at[2, c], sems_in, cubes + c, across).wait_recv()
        forward = copy_to(normed.at[2, c], normed.at[3, c], sems_fwd, c, sibling)
        forward.start()
        project(2, c)
        forward.wait_recv()
        project(3, c)
        for item in stores(c)[1:]:
            item.start()

        def one(s, _):
            attend(c, s)
            return 0

        lax.fori_loop(0, groups, one, 0)
        for r in (1, 0):
            hot = onehot(dest[r, pl.ds(c, 1), :], slots)
            placed = jnp.concatenate(
                [ot[c, s, :, r * cap:(r + 1) * cap] for s in range(groups)], axis=1)
            rows = dot(placed, hot).astype(BF)
            if r == 1:
                away[c] = rows
                attended_copy(c).start()
            else:
                att[c, mine, :] = rows
        stores(c)[0].start()
        return 0

    lax.fori_loop(0, cubes, cube, 0)

    def finish(c, _):
        for item in stores(c):
            item.wait()
        attended_copy(c).wait()
        copy_to(normed.at[0, c], normed.at[2, c], sems_in, cubes + c, across).wait_send()
        copy_to(normed.at[0, c], normed.at[1, c], sems_in, c, sibling).wait_send()
        copy_to(normed.at[2, c], normed.at[3, c], sems_fwd, c, sibling).wait_send()
        return 0

    lax.fori_loop(0, cubes, finish, 0)
    for item in to_peers:
        item.wait_send()


def forward_call(enc, codes, gain, offset, mask_token, w_qkv, cubes, groups):
    tokens, width = enc.shape
    quarter = tokens // cubes
    cap = quarter // 3
    half = width // 2
    packs = half // 128
    wide = (128 // (width // HEADS)) * 2 * cap
    vmem = pl.BlockSpec(memory_space=pltpu.VMEM)
    far = pl.BlockSpec(memory_space=pl.ANY)
    shape = jax.ShapeDtypeStruct
    dma = pltpu.SemaphoreType.DMA
    return pl.pallas_call(
        forward_kernel,
        out_shape=(
            shape((cubes, width, quarter), BF),
            shape((groups, cubes, quarter, width), BF),
            shape((groups, 8, quarter), jnp.int32),
            shape((cubes, groups, groups * cap, width), BF),
            shape((cubes, groups, groups * cap, 128), BF),
            shape((cubes, groups, half, 2 * cap), BF),
            shape((cubes, groups, half, 2 * cap), BF),
            shape((cubes, groups, 8, wide), F32),
        ),
        in_specs=[vmem] * 5 + [far],
        out_specs=(vmem, far, vmem, far, far, far, far, vmem),
        scratch_shapes=[
            dma((3,)),
            pltpu.VMEM((groups, cubes, quarter, width), BF),
            pltpu.VMEM((cubes, groups, groups * cap, width), BF),
            pltpu.VMEM((cubes, groups, groups * cap, 128), BF),
            pltpu.VMEM((cubes, groups, half, 2 * cap), BF),
            pltpu.VMEM((cubes, groups, half, 2 * cap), BF),
            pltpu.VMEM((cubes, quarter, 1), F32),
            pltpu.VMEM((width, 3 * half), BF),
            pltpu.VMEM((half, width), BF),
            pltpu.VMEM((packs, 256, wide), BF),
            pltpu.VMEM((packs, 144, groups * cap), BF),
            pltpu.VMEM((cubes, half, quarter), BF),
            (dma((2 * cubes,)), dma((2 * cubes,))),
            (dma((3,)), dma((3,))),
            (dma((cubes,)), dma((cubes,))),
            (dma((cubes,)), dma((cubes,))),
            dma((cubes, 5)),
        ],
        compiler_params=pltpu.CompilerParams(
            collective_id=0, has_side_effects=True, vmem_limit_bytes=60 * 2**20),
        name="forward",
    )(enc, codes, gain, offset, mask_token, w_qkv)


def pieces(values):
    high = values.astype(BF)
    rest = values - high.astype(F32)
    mid = rest.astype(BF)
    low = (rest - mid.astype(F32)).astype(BF)
    return high, mid, low


def layer_kernel(
    n_dp, n_group,
    att_in, kv_in, kaug_in, qt_in, ot_in, lse, normed_in, dest, w_qkv, enc, visible, mask_token, gain,
    cot_in, w_out_in, w_up_in, w_down_in, gain2, offset2,
    out, grad_enc, sum_ffn, sum_qkv, sum_small,
    kv_at, kaug_at, qt_at, ot_at, normed_at, grads_at, turn, sems_read, sems_turn,
    cot, w_out, w_up, w_down, att, middle, second, backs, result, grads_sum, spare, w_mine, sems_load, sems_out,
    acc, give, pair, recv, settled, sems_core, sems_ffn,
    grad_qkv, small, send_qkv, recv_qkv, settled_qkv, small_bufs, sems_qkv, sems_pair, sems_small,
    columns, dot_slots, qbd, dobd, grad_qt, in_sib, in_fwd, in_across, sems_sib, sems_fwd, sems_across,
):
    cubes, quarter, width = middle.shape
    half = width // 2
    blocks = w_up.shape[0]
    groups = kv_at.shape[1]
    cap = qt_at.shape[3] // 2
    slots = groups * cap
    hd = width // HEADS
    pack = 128
    per = pack // hd
    packs = half // pack
    factor = hd ** -0.5
    sibling, across = peer((1,)), peer((2,))
    parity = lax.rem(lax.axis_index("group"), 2)
    mine = pl.ds(pl.multiple_of(parity * half, half), half)
    theirs = pl.ds(pl.multiple_of((1 - parity) * half, half), half)
    grad_kv, own_sum, out_fwd, out_sib, out_across = w_up, result, cot, second, backs

    core = ("group", 1)
    others = chip_bits(n_dp, n_group)
    paths = balanced_orders(others)
    qkv = [
        Butterfly(grad_qkv.at[p], send_qkv.at[p], recv_qkv.at[p], settled_qkv.at[p], sum_qkv.at[parity, p],
                  (sems_qkv[0].at[p], sems_qkv[1].at[p]), order)
        for p, order in enumerate([balanced_orders(others)[k] for k in (0, 2, 1)])]
    qkv_steps = joined(reduce_steps(qkv), gather_steps(qkv))

    def swap_copies(side):
        items = []
        for p, b in enumerate(qkv):
            count = b.rows // 2
            value = bit_value(b.names[0])
            rows = b.out.at[b.span((value if side == 0 else 1 - value) * count, count), :]
            items.append(copy_to(rows, rows, sems_pair, 3 * side + p, sibling))
        return items
    smalls = [
        SmallSum(small_bufs[k], (sems_small[0].at[k], sems_small[1].at[k]), names)
        for k, names in enumerate(small_groups(n_dp, n_group))]

    def place_of(j, side):
        if j < blocks:
            return sum_ffn.at[j + side * blocks]
        return sum_ffn.at[2 * blocks, pl.ds(pl.multiple_of(side * half, half), half)]

    def rows_in(j):
        return width if j < blocks else half

    def butterflies(j):
        count = rows_in(j)
        return [
            Butterfly(acc.at[j, :count, lanes_of(p)], give.at[j, :, lanes_of(p)], recv.at[j, :, lanes_of(p)],
                      settled.at[j, :count >> halvings_of(count, len(others)), lanes_of(p)],
                      place_of(j, parity).at[:, lanes_of(p)],
                      (sems_ffn[0].at[j, p], sems_ffn[1].at[j, p]), paths[p]) for p in range(PARTS)]

    def summing(j):
        count = rows_in(j)
        inner = reduce_steps(butterflies(j))
        exchange = copy_to(give.at[j, :count], pair.at[j, :count], sems_core, j, sibling)

        def second_step():
            exchange.wait()
            acc[j, :count] += pair[j, :count].astype(F32)
            inner[0]()

        return [exchange.start, second_step] + inner[1:]

    def spreading(sets):
        steps = gather_steps([b for j in sets for b in butterflies(j)])

        def exchanges():
            return [
                copy_to(place_of(j, parity), place_of(j, parity), sems_core, blocks + 1 + j, sibling) for j in sets]

        def last_but_one():
            steps[-1]()
            for item in exchanges():
                item.start()

        def final():
            for item in exchanges():
                item.wait()

        return steps[:-1] + [last_but_one, final]

    def reads(c):
        k = lax.rem(c, 2)
        pairs = [(kv_in.at[c], kv_at.at[k]), (kaug_in.at[c], kaug_at.at[k]), (qt_in.at[c], qt_at.at[k]),
                 (ot_in.at[c], ot_at.at[k]), (normed_in.at[:, c], normed_at.at[k])]
        return [pltpu.make_async_copy(src, dst, sems_read.at[k, n]) for n, (src, dst) in enumerate(pairs)]

    loads = [(w_out_in, w_out), (att_in, att)]
    loads += [(w_up_in.at[:, j * width:(j + 1) * width], w_up.at[j]) for j in range(blocks)]
    loads += [(w_down_in.at[j * width:(j + 1) * width, :], w_down.at[j]) for j in range(blocks)]
    loads += [(cot_in.at[c * quarter:(c + 1) * quarter, :], cot.at[c]) for c in range(cubes)]
    loads += [(w_qkv.at[:, pl.ds(pl.multiple_of(p * width + parity * half, half), half)],
               w_mine.at[:, p * half:(p + 1) * half]) for p in range(3)]
    loads = [pltpu.make_async_copy(src, dst, sems_load.at[k]) for k, (src, dst) in enumerate(loads)]
    for item in loads:
        item.start()
    for c in range(min(2, cubes)):
        for item in reads(c):
            item.start()

    meets = {}
    for names in small_groups(n_dp, n_group):
        for t in range(1, 1 << len(names)):
            chosen = [name for k, name in enumerate(names) if (t >> k) & 1]
            meets[tuple(sorted(chosen))] = flip(chosen)
    for chosen in [[core]] + [[name] for name in others] + [
            list(pair) for i, first in enumerate(others) for pair in ((first, other) for other in others[i + 1:])]:
        meets[tuple(sorted(chosen))] = flip(chosen)
    greet(list(meets.values()))

    one_row = lax.broadcasted_iota(jnp.int32, (16, per * 2 * cap), 0)
    for p in range(packs):
        qbd[p] = jnp.zeros(qbd.shape[1:], BF)
        dobd[p] = jnp.zeros(dobd.shape[1:], BF)
    as_columns(visible, columns)
    grad_qkv[...] = jnp.zeros(grad_qkv.shape, F32)
    small[...] = jnp.zeros(small.shape, F32)

    def rows_of(c):
        return pl.ds(c * quarter, quarter)

    def start_rows(c):
        shown = columns[c] == 1.0
        return shown, jnp.where(shown, enc[rows_of(c), :].astype(F32), mask_token[...])

    def turn_copy(c):
        return copy_to(turn.at[c], grads_at.at[c, 1], sems_turn, c, sibling)

    def out_copy(c):
        return pltpu.make_async_copy(second.at[c], out.at[rows_of(c), :], sems_out.at[0, c])

    def enc_copy(c):
        return pltpu.make_async_copy(second.at[c], grad_enc.at[rows_of(c), :], sems_out.at[1, c])

    def enter(c, _):
        value = start_rows(c)[1] + dot(att[c], w_out[...], TN)
        middle[c] = value
        normal, _ = norm_stats(value)
        second[c] = (normal * gain2[...] + offset2[...]).astype(BF)
        return 0

    def block(j, c):
        rows, cotan = second[c], cot[c]
        hidden = dot(rows, w_up[j])
        square = hidden * hidden
        tanh = jnp.tanh(hidden * (GELU_A + GELU_B * square))
        slope = 0.5 * (1.0 + tanh)
        active = (hidden * slope).astype(BF)
        slope = slope + 0.5 * hidden * (1.0 - tanh * tanh) * (GELU_A + 3.0 * GELU_B * square)
        grad_hidden = (dot(cotan, w_down[j], NT) * slope).astype(BF)
        grad_up = dot(rows, grad_hidden, TN)
        grad_down = dot(active, cotan, TN)
        kept = jnp.where(parity == 0, grad_up, grad_down)
        given = jnp.where(parity == 0, grad_down, grad_up)
        outcome = dot(active, w_down[j])
        grads = dot(grad_hidden, w_up[j], NT)
        result[c] = outcome + jnp.where(j > 0, result[c], 0.0)
        grads_sum[c] = grads + jnp.where(j > 0, grads_sum[c], 0.0)
        acc[j] = kept + jnp.where(c > 0, acc[j], 0.0)
        spare[...] = given + jnp.where(c > 0, spare[...], 0.0)

        def hand_over():
            give[j, :width] = spare[...].astype(BF)

        pl.when(c == cubes - 1)(hand_over)

    def leave(c):
        second[c] = (middle[c] + result[c]).astype(BF)
        out_copy(c).start()
        normal, recip = norm_stats(middle[c])
        grads = grads_sum[c]
        small[3:4, :] += jnp.sum(grads * normal, axis=0, keepdims=True)
        small[4:5, :] += jnp.sum(grads, axis=0, keepdims=True)
        total = cot[c].astype(F32) + norm_back(grads, normal, recip, gain2[...])
        middle[c] = total
        branch = total.astype(BF)
        back = dot(w_out[...], branch, NT).astype(BF)
        backs[c] = branch
        turn[c] = jnp.where(parity == 0, back[half:], back[:half])
        grads_at[c, 0] = jnp.where(parity == 0, back[:half], back[half:])
        turn_copy(c).start()

    def out_weights():
        total = dot(att[0], backs[0])
        for c in range(1, cubes):
            total += dot(att[c], backs[c])
        acc[blocks, :half] = jnp.where(parity == 0, total[:half], total[half:])
        give[blocks, :half] = jnp.where(parity == 0, total[half:], total[:half]).astype(BF)

    firsts = [summing(j) for j in range(blocks + 1)]
    seconds = [spreading(sets) for sets in SPREADS]
    plan = []
    for number, (steps, places) in enumerate(zip(firsts + seconds, SUM_AT + SPREAD_AT)):
        if len(places) != len(steps):
            places = [places[0] + 2 * k for k in range(len(steps))]
        stage = 0 if number < len(firsts) else len(steps)
        plan += [(place, stage + k, number, step) for k, (place, step) in enumerate(zip(places, steps))]
    plan = [(entry[0], entry[-1]) for entry in sorted(plan, key=lambda entry: entry[:3])]
    lead = blocks * cubes + cubes + 1

    def advance(place):
        for at, step in plan:
            if at == place:
                step()

    for item in loads[:2]:
        item.wait()
    lax.fori_loop(0, cubes, enter, 0)
    for item in loads[2:]:
        item.wait()
    place = blocks * cubes

    def blocks_step(u, _):
        block(u // cubes, lax.rem(u, cubes))
        for at, step in plan:
            if at <= place:
                pl.when(u == at - 1)(step)
        return 0

    lax.fori_loop(0, place, blocks_step, 0)
    for c in range(cubes):
        leave(c)
        place += 1
        advance(place)
    out_weights()
    place += 1
    advance(place)
    for c in range(cubes):
        out_copy(c).wait()

    def extra_rows(first, values):
        high, mid, low = pieces(-values)
        rows = jnp.where(
            one_row == 0, first,
            jnp.where(one_row == 1, high.astype(F32),
                      jnp.where(one_row == 2, mid.astype(F32),
                                jnp.where(one_row == 3, low.astype(F32), 0.0))))
        return rows.astype(BF)

    def attend_back(c, s):
        slot = lax.rem(c, 2)
        for p in range(packs):
            lanes = slice(p * pack, (p + 1) * pack)
            deltas = []
            for j in range(per):
                rows = slice(p * pack + j * hd, p * pack + (j + 1) * hd)
                cols = slice(j * 2 * cap, (j + 1) * 2 * cap)
                qbd[p, j * hd:(j + 1) * hd, cols] = qt_at[slot, s, rows, :]
                grads = dot_slots[s, rows, :]
                dobd[p, j * hd:(j + 1) * hd, cols] = grads
                deltas.append(jnp.sum(
                    grads.astype(F32) * ot_at[slot, s, rows, :].astype(F32), axis=0, keepdims=True))
            qbd[p, pack:pack + 16, :] = extra_rows(1.0, lse[c, s, p:p + 1, :])
            dobd[p, pack:pack + 16, :] = extra_rows(0.0, jnp.concatenate(deltas, axis=1))
            extra = kaug_at[slot, s]
            keys = kv_at[slot, s, :, lanes]
            values = kv_at[slot, s, :, half + p * pack:half + (p + 1) * pack]
            probs = jnp.exp2(dot(jnp.concatenate([keys, extra], axis=1), qbd[p]))
            centred = dot(jnp.concatenate([values, extra], axis=1), dobd[p])
            grad_scores = (probs * centred).astype(BF)
            grad_kv[s, :, half + p * pack:half + (p + 1) * pack] = dot(
                probs.astype(BF), dobd[p, :pack, :], NT).astype(BF)
            grad_kv[s, :, lanes] = (dot(grad_scores, qbd[p, :pack, :], NT) * LN2).astype(BF)
            mixed = dot(keys.T, grad_scores) * factor
            for j in range(per):
                rows = slice(p * pack + j * hd, p * pack + (j + 1) * hd)
                cols = slice(j * 2 * cap, (j + 1) * 2 * cap)
                grad_qt[s, rows, :] = mixed[j * hd:(j + 1) * hd, cols].astype(BF)

    def back_rows(r, c):
        hot = onehot(dest[r, pl.ds(c, 1), :], slots)
        placed = jnp.concatenate(
            [grad_kv[s, r * cap:(r + 1) * cap, :] for s in range(groups)], axis=0)
        grads = dot(hot, placed, TN).astype(BF)
        if r < 2:
            queries = jnp.concatenate(
                [grad_qt[s, :, r * cap:(r + 1) * cap] for s in range(groups)], axis=1)
            queries = dot(queries, hot).T.astype(BF)
            grads = jnp.concatenate([queries, grads], axis=1)
        weight = dot(normed_at[lax.rem(c, 2), r], grads, TN)
        first = 3 - weight.shape[1] // half
        for k in range(first, 3):
            grad_qkv[k] += weight[:, (k - first) * half:(k - first + 1) * half]
        return grads

    def back_project(r, c):
        grads = back_rows(r, c)
        return dot(grads, w_mine[:, 3 * half - grads.shape[1]:], NT)

    def prepare(c):
        for item in reads(c):
            item.wait()
        for r in range(2):
            rows = grads_at[c, r]
            hot = onehot(dest[r, pl.ds(c, 1), :], slots)
            spread = dot(rows, hot, NT).astype(BF)
            for s in range(groups):
                dot_slots[s, :, r * cap:(r + 1) * cap] = spread[:, s * cap:(s + 1) * cap]

    def cube(c, _):
        def point(i):
            for at, step in plan:
                if at > lead and (at - lead - 1) % POINTS == i and (at - lead - 1) // POINTS < cubes:
                    pl.when(c == (at - lead - 1) // POINTS)(step)

        turn_copy(c).wait()
        prepare(c)
        point(0)

        def one(s, _):
            attend_back(c, s)
            for i in range(groups):
                pl.when(s == i)(functools.partial(point, i + 1))
            return 0

        lax.fori_loop(0, groups, one, 0)
        out_fwd[c] = back_project(3, c).astype(BF)
        forward = copy_to(out_fwd.at[c], in_fwd.at[c], sems_fwd, c, sibling)
        forward.start()
        point(5)
        partial = back_project(2, c)
        forward.wait_recv()
        out_across[c] = (partial + in_fwd[c].astype(F32)).astype(BF)
        copy_to(out_across.at[c], in_across.at[c], sems_across, c, across).start()
        point(6)
        near_rows = back_rows(1, c)
        own_rows = back_rows(0, c)
        pl.when(c == cubes - 1)(qkv_steps[0])
        point(7)
        out_sib[c] = dot(near_rows, w_mine[...], NT).astype(BF)
        copy_to(out_sib.at[c], in_sib.at[c], sems_sib, c, sibling).start()
        own_sum[c] = dot(own_rows, w_mine[...], NT)

        def more():
            for item in reads(c + 2):
                item.start()

        pl.when(c + 2 < cubes)(more)
        point(8)
        return 0

    lax.fori_loop(0, cubes, cube, 0)
    tail = [(at - lead - POINTS * cubes, step) for at, step in plan if at > lead + POINTS * cubes]

    def last(c):
        copy_to(out_sib.at[c], in_sib.at[c], sems_sib, c, sibling).wait()
        copy_to(out_across.at[c], in_across.at[c], sems_across, c, across).wait()
        copy_to(out_fwd.at[c], in_fwd.at[c], sems_fwd, c, sibling).wait_send()
        grads = own_sum[c] + in_sib[c].astype(F32) + in_across[c].astype(F32)
        shown, start = start_rows(c)
        normal, recip = norm_stats(start)
        small[0:1, :] += jnp.sum(grads * normal, axis=0, keepdims=True)
        small[1:2, :] += jnp.sum(grads, axis=0, keepdims=True)
        total = middle[c] + norm_back(grads, normal, recip, gain[...])
        second[c] = jnp.where(shown, total, 0.0).astype(BF)
        enc_copy(c).start()
        small[2:3, :] += jnp.sum(jnp.where(shown, 0.0, total), axis=0, keepdims=True)

    fill = list(range(cubes))
    pending = []

    def small_step():
        total = smalls[pending[0]].finish()
        pending.append(pending.pop(0) + 1)
        if pending[0] < len(smalls):
            smalls[pending[0]].start(total)
        else:
            pending.clear()
            sum_small[...] = total

    for k in range(1, len(qkv_steps)):
        if fill:
            last(fill.pop(0))
            if not fill:
                smalls[0].start(small[...])
                pending.append(0)
            qkv_steps[k]()
        else:
            qkv_steps[k]()
            if k == len(qkv_steps) - 2:
                for item in swap_copies(0):
                    item.start()
            if pending:
                small_step()
        while tail and tail[0][0] <= k:
            tail.pop(0)[1]()
    for item in swap_copies(1):
        item.start()
    for _, step in tail:
        step()
    while pending:
        small_step()
    for c in range(cubes):
        enc_copy(c).wait()
    for item in swap_copies(0) + swap_copies(1):
        item.wait()


POINTS = 9
PARTS = 4
SUM_AT = [
    [3, 5, 9, 12, 16],
    [6, 8, 12, 17, 20],
    [9, 11, 15, 19, 22],
    [12, 14, 18, 21, 25],
    [16, 18, 21, 26, 29],
]
SPREADS = [[0], [1], [2], [3], [4]]
SPREAD_AT = [
    [16, 20, 23, 28, 30],
    [20, 24, 28, 32, 34],
    [22, 27, 30, 35, 37],
    [25, 29, 33, 37, 39],
    [29, 33, 37, 39, 41],
]


def layer_call(
    att, kv, kaug, qt, ot, lse, normed, dest, w_qkv, enc, visible, mask_token, gain,
    cot, w_out, w_up, w_down, gain2, offset2, n_dp, n_group,
):
    cubes, width, quarter = att.shape
    groups = kv.shape[1]
    cap = quarter // 3
    half = width // 2
    packs = half // 128
    wide = (128 // (width // HEADS)) * 2 * cap
    blocks = w_up.shape[1] // width
    vmem = pl.BlockSpec(memory_space=pltpu.VMEM)
    far = pl.BlockSpec(memory_space=pl.ANY)
    shape = jax.ShapeDtypeStruct
    dma = pltpu.SemaphoreType.DMA
    rows = pltpu.VMEM((cubes, quarter, width), BF)
    sums = pltpu.VMEM((cubes, quarter, width), F32)
    squares = pltpu.VMEM((blocks, width, width), BF)
    pair = (dma((cubes,)), dma((cubes,)))
    stages = len(chip_bits(n_dp, n_group))
    staging = staging_rows(width, stages)
    kept = max(width >> halvings_of(width, stages), half >> halvings_of(half, stages))
    kept_qkv = width >> halvings_of(width, stages)
    small = small_groups(n_dp, n_group)
    return pl.pallas_call(
        functools.partial(layer_kernel, n_dp, n_group),
        out_shape=(
            shape(enc.shape, BF),
            shape(enc.shape, BF),
            shape((2 * blocks + 1, width, width), BF),
            shape((2, 3, width, half), BF),
            shape((8, width), F32),
        ),
        in_specs=[far] * 5 + [vmem, far, vmem, far] + [vmem] * 4 + [far] * 4 + [vmem] * 2,
        out_specs=(far, far, far, far, vmem),
        scratch_shapes=[
            pltpu.VMEM((2,) + kv.shape[1:], BF),
            pltpu.VMEM((2,) + kaug.shape[1:], BF),
            pltpu.VMEM((2,) + qt.shape[1:], BF),
            pltpu.VMEM((2,) + ot.shape[1:], BF),
            pltpu.VMEM((2, groups, quarter, width), BF),
            pltpu.VMEM((cubes, 2, half, quarter), BF),
            pltpu.VMEM((cubes, half, quarter), BF),
            dma((2, 5)),
            pair,
            rows,
            pltpu.VMEM(w_out.shape, BF),
            squares,
            squares,
            pltpu.VMEM(att.shape, BF),
            sums,
            rows,
            rows,
            sums,
            sums,
            pltpu.VMEM((width, width), F32),
            pltpu.VMEM((width, 3 * half), BF),
            dma((2 + 2 * blocks + cubes + 3,)),
            dma((2, cubes)),
            pltpu.VMEM((blocks + 1, width, width), F32),
            pltpu.VMEM((blocks + 1, max(width, staging), width), BF),
            pltpu.VMEM((blocks + 1, width, width), BF),
            pltpu.VMEM((blocks + 1, staging, width), BF),
            pltpu.VMEM((blocks + 1, kept, width), BF),
            (dma((2 * blocks + 2,)), dma((2 * blocks + 2,))),
            (dma((blocks + 1, PARTS, 2 * stages + 3)), dma((blocks + 1, PARTS, 2 * stages + 3))),
            pltpu.VMEM((3, width, half), F32),
            pltpu.VMEM((8, width), F32),
            pltpu.VMEM((3, staging, half), BF),
            pltpu.VMEM((3, staging, half), BF),
            pltpu.VMEM((3, kept_qkv, half), BF),
            tuple(pltpu.VMEM((1 << len(names), 8, width), F32) for names in small),
            (dma((3, 2 * stages + 3)), dma((3, 2 * stages + 3))),
            (dma((6,)), dma((6,))),
            (dma((len(small), 8)), dma((len(small), 8))),
            pltpu.VMEM((cubes, quarter, 1), F32),
            pltpu.VMEM((groups, half, 2 * cap), BF),
            pltpu.VMEM((packs, 256, wide), BF),
            pltpu.VMEM((packs, 256, wide), BF),
            pltpu.VMEM((groups, half, 2 * cap), BF),
            rows, rows, rows,
            pair, pair, pair,
        ],
        compiler_params=pltpu.CompilerParams(
            collective_id=1, has_side_effects=True, vmem_limit_bytes=63 * 2**20),
        name="layer",
    )(att, kv, kaug, qt, ot, lse, normed, dest, w_qkv, enc, visible, mask_token, gain,
      cot, w_out, w_up, w_down, gain2, offset2)


def cast_kernel(ups, downs, outs, qkvs, small, tokens, grads, up, down, out, qkv, tokens_out, grads_out, *vectors):
    width, half = outs.shape[1], qkvs.shape[3]
    for k in range(ups.shape[0]):
        up[:, k * width:(k + 1) * width] = ups[k].astype(F32)
    down[...] = downs[...].astype(F32)
    out[...] = outs[...].astype(F32)
    for part in range(3):
        for side in range(2):
            at = part * width + side * half
            qkv[:, at:at + half] = qkvs[side, part].astype(F32)
    tokens_out[...] = tokens[...]
    grads_out[...] = grads[...]
    for k, vector in enumerate(vectors):
        vector[...] = small[k:k + 1, :]


def cast_call(ffn, qkv, small, tokens, grads):
    width = qkv.shape[2]
    blocks = ffn.shape[0] // (2 * width)
    steps = 2
    rows = width // steps
    tall = blocks * rows
    token_rows = pl.BlockSpec((tokens.shape[0] // steps, width), lambda i: (i, 0))
    shape = jax.ShapeDtypeStruct
    return pl.pallas_call(
        cast_kernel,
        grid=(steps,),
        in_specs=[
            pl.BlockSpec((blocks, rows, width), lambda i: (0, i, 0)),
            pl.BlockSpec((tall, width), lambda i: (steps + i, 0)),
            pl.BlockSpec((rows, width), lambda i: (2 * blocks * steps + i, 0)),
            pl.BlockSpec((2, 3, rows, width // 2), lambda i: (0, 0, i, 0)),
            pl.BlockSpec(small.shape, lambda i: (0, 0)),
            token_rows,
            token_rows,
        ],
        out_specs=[
            pl.BlockSpec((rows, blocks * width), lambda i: (i, 0)),
            pl.BlockSpec((tall, width), lambda i: (i, 0)),
            pl.BlockSpec((rows, width), lambda i: (i, 0)),
            pl.BlockSpec((rows, 3 * width), lambda i: (i, 0)),
            token_rows,
            token_rows,
        ] + [pl.BlockSpec((1, width), lambda i: (0, 0))] * 5,
        out_shape=(
            shape((width, blocks * width), F32),
            shape((blocks * width, width), F32),
            shape((width, width), F32),
            shape((width, 3 * width), F32),
            shape(tokens.shape, BF),
            shape(tokens.shape, BF),
        ) + (shape((1, width), F32),) * 5,
        name="cast",
    )(ffn.reshape(2 * blocks + 1, width, width), ffn, ffn, qkv, small, tokens, grads)


def on_device(
    enc, visible, band_group, cotangent, ln1_gain, ln1_bias, w_qkv, w_out,
    ln2_gain, ln2_bias, w_up, w_down, mask_token,
):
    groups = lax.axis_size("group")
    tok_dev, width = enc.shape
    quarter = CUBE_TOK // groups
    cubes = tok_dev // quarter
    codes = (visible * 8 + band_group).reshape(cubes, quarter)
    gain1, mask_row = ln1_gain[None, :], mask_token[None, :]
    att, normed, dest, kv, kaug, qt, ot, lse = forward_call(
        enc, codes, gain1, ln1_bias[None, :], mask_row, w_qkv, cubes, groups)
    out, grad_enc, sum_ffn, sum_qkv, small = layer_call(
        att, kv, kaug, qt, ot, lse, normed, dest, w_qkv, enc, codes, mask_row, gain1, cotangent, w_out, w_up,
        w_down, ln2_gain[None, :], ln2_bias[None, :], lax.axis_size("dp"), groups)
    (sum_up, sum_down, sum_out, sum_w_qkv, out, grad_enc, gain1_sum, bias1_sum, mask_sum, gain2_sum, bias2_sum,
     ) = cast_call(sum_ffn.reshape(9 * width, width), sum_qkv, small, out, grad_enc)
    gain1_sum, bias1_sum, mask_sum, gain2_sum, bias2_sum = (
        vector.reshape(width) for vector in (gain1_sum, bias1_sum, mask_sum, gain2_sum, bias2_sum))
    return (
        out, grad_enc, gain1_sum, bias1_sum, sum_w_qkv, sum_out, gain2_sum, bias2_sum, sum_up, sum_down, mask_sum)


def solution(mesh):
    rows, line = P(("dp", "group"), None), P(("dp", "group"))
    return jax.shard_map(
        on_device, mesh=mesh, in_specs=(rows, line, line, rows) + (P(),) * 9,
        out_specs=(rows, rows) + (P(),) * 9, check_vma=False)
```

```python
import functools
import jax
import jax.numpy as jnp
from jax import lax
from jax.experimental import pallas as pl
from jax.experimental.pallas import tpu as pltpu
from jax.sharding import PartitionSpec as P

HEADS = 16
CUBE_TOK = 1536
EPS = 1e-05
LOG2E = 1.4426950408889634
LN2 = 0.6931471805599453
GELU_A = 0.7978845608028654
GELU_B = 0.7978845608028654 * 0.044715
FLOOR = -1e20
MASKED = -1e30

NN = (((1,), (0,)), ((), ()))
NT = (((1,), (1,)), ((), ()))
TN = (((0,), (0,)), ((), ()))
MESH = pl.DeviceIdType.MESH
BF = jnp.bfloat16
F32 = jnp.float32


def dot(left, right, dims=NN):
    return lax.dot_general(left, right, dims, preferred_element_type=F32)


def norm_stats(values):
    centre = values - jnp.mean(values, axis=-1, keepdims=True)
    spread = jnp.mean(centre * centre, axis=-1, keepdims=True)
    recip = lax.rsqrt(spread + EPS)
    return centre * recip, recip


def norm_back(grad_rows, normal, recip, gain):
    scaled = grad_rows * gain
    return recip * (
        scaled
        - jnp.mean(scaled, axis=-1, keepdims=True)
        - normal * jnp.mean(scaled * normal, axis=-1, keepdims=True)
    )


def onehot(dest_row, slots):
    rows = lax.broadcasted_iota(jnp.int32, (slots, dest_row.shape[1]), 0)
    return jnp.where(rows == dest_row, 1.0, 0.0).astype(BF)


def peer(bits):
    me = lax.axis_index("group")
    for bit in bits:
        me = me + (1 - 2 * (lax.rem(me // bit, 2))) * bit
    return (lax.axis_index("dp"), me)


def copy_to(src, dst, sems, index, device):
    return pltpu.make_async_remote_copy(
        src_ref=src, dst_ref=dst, send_sem=sems[0].at[index], recv_sem=sems[1].at[index],
        device_id=device, device_id_type=MESH,
    )


def greet(devices, meanwhile):
    barrier = pltpu.get_barrier_semaphore()
    for device in devices:
        pl.semaphore_signal(barrier, inc=1, device_id=device, device_id_type=MESH)
    meanwhile()
    pl.semaphore_wait(barrier, len(devices))


def own_dest(ids, capacity, groups):
    tokens = ids.shape[1]
    upper = (
        lax.broadcasted_iota(jnp.int32, (tokens, tokens), 0)
        < lax.broadcasted_iota(jnp.int32, (tokens, tokens), 1)
    )
    upper = jnp.where(upper, 1.0, 0.0).astype(BF)
    total = jnp.zeros(ids.shape, F32)
    for group in range(groups):
        hit = jnp.where(ids == group, 1.0, 0.0)
        ranks = dot(hit.astype(BF), upper)
        total = total + hit * (ranks + float(group * capacity))
    return total.astype(jnp.int32)


def bits_of(size):
    return [1 << k for k in range(size.bit_length() - 1)]


def bit_value(name):
    axis, bit = name
    return lax.rem(lax.axis_index(axis) // bit, 2)


def flip(names):
    place = {axis: lax.axis_index(axis) for axis in ("dp", "group")}
    for axis, bit in names:
        place[axis] = place[axis] + (1 - 2 * bit_value((axis, bit))) * bit
    return (place["dp"], place["group"])


class Butterfly:
    def __init__(self, acc, send, recv, settled, out, sems, names):
        self.acc, self.send, self.recv, self.settled, self.out = acc, send, recv, settled, out
        self.sems, self.names = sems, names
        self.rows = acc.shape[0]
        self.halvings = halvings_of(self.rows, len(names))
        self.groups = [[name] for name in names]
        if self.halvings >= 4:
            last = names[self.halvings - 2:self.halvings]
            self.groups[self.halvings - 2:self.halvings] = [last]
        self.legs = sum((1 << len(group)) - 1 for group in self.groups)
        self.halving_groups = [
            g for g in range(len(self.groups)) if self.done(g) < self.halvings]

    def done(self, g):
        return sum(len(group) for group in self.groups[:g])

    def start_row(self, k):
        low = 0
        for j in range(min(k, self.halvings)):
            low = low + bit_value(self.names[j]) * (self.rows >> (j + 1))
        return low

    def span(self, low, count):
        return pl.ds(pl.multiple_of(low, 16), count)

    def partners(self, g):
        names, done = self.groups[g], self.done(g)
        number = sum((1 << len(group)) - 1 for group in self.groups[:g])
        found = []
        for t in range(1, 1 << len(names)):
            low = self.start_row(done)
            if done < self.halvings:
                for k, name in enumerate(names):
                    value = 1 - bit_value(name) if (t >> k) & 1 else bit_value(name)
                    low = low + value * (self.rows >> (done + k + 1))
            found.append(([name for k, name in enumerate(names) if (t >> k) & 1], number + t - 1, low))
        return found

    def hops(self, g):
        done, size = self.done(g), len(self.groups[g])
        if done < self.halvings:
            count = self.rows >> (done + size)
            at = self.rows - (self.rows >> done)
        else:
            count = self.rows >> self.halvings
            at = self.rows + (done - self.halvings - 1) * count
        found = []
        for n, (names, number, low) in enumerate(self.partners(g)):
            where = pl.ds(at + n * count, count)
            item = copy_to(self.send.at[where], self.recv.at[where], self.sems, number, flip(names))
            found.append((item, where, self.span(low, count)))
        return found, count

    def reduce_start(self, g):
        for item, where, rows in self.hops(g)[0]:
            self.send[where, :] = self.acc[rows, :].astype(BF)
            item.start()

    def reduce_finish(self, g):
        found, count = self.hops(g)
        rows = self.span(self.start_row(self.done(g) + len(self.groups[g])), count)
        for item, where, _ in found:
            item.wait()
        for _, where, _ in found:
            if self.done(g) < self.halvings:
                self.acc[rows, :] += self.recv[where, :].astype(F32)
            else:
                self.acc[rows, :] = self.send[where, :].astype(F32) + self.recv[where, :].astype(F32)

    def own_piece(self):
        return self.span(self.start_row(self.halvings), self.rows >> self.halvings)

    def keep(self):
        return pltpu.make_async_copy(
            self.settled, self.out.at[self.own_piece(), :], self.sems[0].at[2 * self.legs])

    def settle(self):
        self.settled[...] = self.acc[self.own_piece(), :].astype(BF)
        self.keep().start()

    def gather(self, g):
        done = self.done(g) + len(self.groups[g])
        rows = self.span(self.start_row(done), self.rows >> done)
        src = self.settled if done == self.halvings else self.out.at[rows, :]
        return [
            copy_to(src, self.out.at[rows, :], self.sems, self.legs + number, flip(names))
            for names, number, _ in self.partners(g)]


def halvings_of(rows, stages):
    count = 0
    while count < stages and (rows >> (count + 1)) % 16 == 0:
        count += 1
    return count


def staging_rows(rows, stages):
    count = halvings_of(rows, stages)
    return rows + (stages - count - 1) * (rows >> count)


def reduce_steps(butterflies):
    stages = len(butterflies[0].groups)

    def first():
        for b in butterflies:
            b.reduce_start(0)

    steps = [first]
    for g in range(stages):
        def step(g=g):
            for b in butterflies:
                b.reduce_finish(g)
                if g + 1 < stages:
                    b.reduce_start(g + 1)
                else:
                    b.settle()
        steps.append(step)
    return steps


def gather_steps(butterflies):
    last = butterflies[0].halving_groups[-1]

    def start(b, g):
        for item in b.gather(g):
            item.start()

    def first():
        for b in butterflies:
            start(b, last)

    steps = [first]
    for g in range(last, -1, -1):
        def step(g=g):
            for b in butterflies:
                for item in b.gather(g):
                    item.wait()
                if g == last:
                    b.keep().wait()
                if g > 0:
                    start(b, g - 1)
        steps.append(step)
    return steps


def joined(before, after):
    def both():
        before[-1]()
        after[0]()

    return before[:-1] + [both] + after[1:]


def path_orders(names, count):
    head, tail = names[:count], names[count:]
    return [head[k:] + head[:k] + tail for k in range(count)]


def balanced_orders(names):
    first, second, third, tail = names[0], names[1], names[2], names[3:]
    return [[second, first, third] + tail, [second, third, first] + tail] + [[third, second, first] + tail] * 2


def chip_bits(n_dp, n_group):
    return [("group", b) for b in bits_of(n_group) if b > 1] + [("dp", b) for b in bits_of(n_dp)]


def lanes_of(p):
    return slice(p * 128, (p + 1) * 128)


PARTS = 4

def small_groups(n_dp, n_group):
    names = [("group", b) for b in bits_of(n_group)] + [("dp", b) for b in bits_of(n_dp)]
    groups = [names[:3]]
    rest = names[3:]
    while rest:
        groups.append(rest[:2])
        rest = rest[2:]
    return groups


class SmallSum:
    def __init__(self, buf, sems, names):
        self.buf, self.sems, self.names = buf, sems, names
        self.count = 1 << len(names)

    def copies(self):
        place = 0
        for k, name in enumerate(self.names):
            place = place + bit_value(name) * (1 << k)
        items = []
        for t in range(1, self.count):
            others = [name for k, name in enumerate(self.names) if (t >> k) & 1]
            items.append(copy_to(self.buf.at[place], self.buf.at[place], self.sems, t, flip(others)))
        return place, items

    def start(self, values):
        place, items = self.copies()
        self.buf[place] = values
        for item in items:
            item.start()

    def finish(self):
        _, items = self.copies()
        for item in items:
            item.wait()
        total = self.buf[0]
        for j in range(1, self.count):
            total = total + self.buf[j]
        return total


def as_columns(codes, columns):
    shown = jnp.where(codes[...] >= 8, 1.0, 0.0)
    shown = jnp.concatenate([shown, jnp.zeros((8 - shown.shape[0], shown.shape[1]), F32)], axis=0).T
    for c in range(codes.shape[0]):
        columns[c] = shown[:, c:c + 1]


def forward_kernel(
    enc, codes, gain, offset, mask_token, w_qkv,
    att, normed_out, dest, kv_out, kaug_out, qt_out, ot_out, lse,
    sems_load,
    normed, kv, kaug, qt, ot, columns, w_mine, wq_t, qbd, vt, away, sems_in, sems_dest, sems_fwd, sems_att, sems_store,
):
    cubes, quarter = normed.shape[1], normed.shape[2]
    width = enc.shape[1]
    half = width // 2
    groups = kv.shape[1]
    cap = qt.shape[3] // 2
    slots = groups * cap
    hd = width // HEADS
    pack = 128
    per = pack // hd
    packs = half // pack
    factor = LOG2E * hd ** -0.5
    sibling, across, cross = peer((1,)), peer((2,)), peer((1, 2))
    parity = lax.rem(lax.axis_index("group"), 2)

    mine = pl.ds(pl.multiple_of(parity * half, half), half)

    loads = [pltpu.make_async_copy(w_qkv.at[:, pl.ds(pl.multiple_of(p * width + parity * half, half), half)],
                                   w_mine.at[:, p * half:(p + 1) * half], sems_load.at[p]) for p in range(3)]
    for item in loads:
        item.start()

    def start_rows(c):
        rows = enc[pl.ds(c * quarter, quarter), :].astype(F32)
        return jnp.where(columns[c] == 1.0, rows, mask_token[...])

    def own_rows(c, _):
        normal, _ = norm_stats(start_rows(c))
        normed[0, c] = (normal * gain[...] + offset[...]).astype(BF)
        return 0

    def send_rows(c, _):
        copy_to(normed.at[0, c], normed.at[2, c], sems_in, cubes + c, across).start()
        copy_to(normed.at[0, c], normed.at[1, c], sems_in, c, sibling).start()
        return 0

    def before_sending():
        dest[0] = jnp.zeros(dest.shape[1:], jnp.int32)
        dest[0, :cubes] = own_dest(codes[...] & 7, cap, groups)
        as_columns(codes, columns)
        lax.fori_loop(0, cubes, own_rows, 0)

    greet([sibling, across, cross], before_sending)
    lax.fori_loop(0, cubes, send_rows, 0)
    to_peers = []
    for index, device in enumerate((sibling, across, cross)):
        item = copy_to(dest.at[0], dest.at[index + 1], sems_dest, index, device)
        item.start()
        to_peers.append(item)

    for item in loads:
        item.wait()
    wq_t[...] = w_mine[:, :half].T

    one_row = lax.broadcasted_iota(jnp.int32, (16, per * 2 * cap), 0)
    for p in range(packs):
        qbd[p] = jnp.zeros(qbd.shape[1:], BF)
        qbd[p, pack:pack + 16, :] = jnp.where(one_row == 0, 1.0, 0.0).astype(BF)
        vt[p, pack:pack + 16, :] = jnp.ones((16, vt.shape[2]), BF)

    def project(r, c):
        rows = normed[r, c]
        row = dest[r, pl.ds(c, 1), :]
        hot = onehot(row, slots)
        values = dot(rows, w_mine[:, half:]).astype(BF)
        placed = dot(hot, values).astype(BF)
        lane = lax.broadcasted_iota(jnp.int32, (cap, 128), 1)
        place = lax.broadcasted_iota(jnp.int32, (cap, 128), 0)
        for s in range(groups):
            kv[c, s, r * cap:(r + 1) * cap, :] = placed[s * cap:(s + 1) * cap, :]
            inside = jnp.logical_and(row >= s * cap, row < (s + 1) * cap)
            count = jnp.sum(jnp.where(inside, 1, 0), axis=1, keepdims=True)
            bias = jnp.where(place < count, 0.0, MASKED)
            extra = jnp.where(lane == 0, bias, jnp.where(lane < 4, 1.0, 0.0))
            kaug[c, s, r * cap:(r + 1) * cap, :] = extra.astype(BF)
        if r < 2:
            queries = (dot(wq_t[...], rows, NT) * factor).astype(BF)
            spread = dot(queries, hot, NT).astype(BF)
            for s in range(groups):
                qt[c, s, :, r * cap:(r + 1) * cap] = spread[:, s * cap:(s + 1) * cap]

    def near_rows(c, _):
        project(0, c)
        copy_to(normed.at[0, c], normed.at[1, c], sems_in, c, sibling).wait_recv()
        project(1, c)
        return 0

    for item in to_peers:
        item.wait_recv()
    lax.fori_loop(0, cubes, near_rows, 0)

    def attend(c, s):
        for p in range(packs):
            lanes = slice(p * pack, (p + 1) * pack)
            for j in range(per):
                qbd[p, j * hd:(j + 1) * hd, j * 2 * cap:(j + 1) * 2 * cap] = qt[
                    c, s, p * pack + j * hd:p * pack + (j + 1) * hd, :]
            vt[p, :pack, :] = kv[c, s, :, half + p * pack:half + (p + 1) * pack].T
            keys = jnp.concatenate([kv[c, s, :, lanes], kaug[c, s]], axis=1)
            scores = dot(keys, qbd[p])
            top = jnp.maximum(jnp.max(scores, axis=0, keepdims=True), FLOOR)
            probs = jnp.exp2(scores - top).astype(BF)
            mixed = dot(vt[p], probs)
            total = jnp.maximum(mixed[pack:pack + 1, :], 1e-30)
            lse[c, s, p:p + 1, :] = top + jnp.log2(total)
            scale = 1.0 / total
            for j in range(per):
                cols = slice(j * 2 * cap, (j + 1) * 2 * cap)
                ot[c, s, p * pack + j * hd:p * pack + (j + 1) * hd, :] = (
                    mixed[j * hd:(j + 1) * hd, cols] * scale[:, cols]
                ).astype(BF)

    def stores(c):
        pairs = [(ot.at[c], ot_out.at[c]), (kv.at[c], kv_out.at[c]), (kaug.at[c], kaug_out.at[c]),
                 (qt.at[c], qt_out.at[c]), (normed.at[:, c], normed_out.at[:, c])]
        return [pltpu.make_async_copy(src, dst, sems_store.at[c, k]) for k, (src, dst) in enumerate(pairs)]

    def attended_copy(c):
        return copy_to(away.at[c], att.at[c, mine, :], sems_att, c, sibling)

    def cube(c, _):
        copy_to(normed.at[0, c], normed.at[2, c], sems_in, cubes + c, across).wait_recv()
        forward = copy_to(normed.at[2, c], normed.at[3, c], sems_fwd, c, sibling)
        forward.start()
        project(2, c)
        forward.wait_recv()
        project(3, c)
        for item in stores(c)[1:]:
            item.start()

        def one(s, _):
            attend(c, s)
            return 0

        lax.fori_loop(0, groups, one, 0)
        for r in (1, 0):
            hot = onehot(dest[r, pl.ds(c, 1), :], slots)
            placed = jnp.concatenate(
                [ot[c, s, :, r * cap:(r + 1) * cap] for s in range(groups)], axis=1)
            rows = dot(placed, hot).astype(BF)
            if r == 1:
                away[c] = rows
                attended_copy(c).start()
            else:
                att[c, mine, :] = rows
        stores(c)[0].start()
        return 0

    lax.fori_loop(0, cubes, cube, 0)

    def finish(c, _):
        for item in stores(c):
            item.wait()
        attended_copy(c).wait()
        copy_to(normed.at[0, c], normed.at[2, c], sems_in, cubes + c, across).wait_send()
        copy_to(normed.at[0, c], normed.at[1, c], sems_in, c, sibling).wait_send()
        copy_to(normed.at[2, c], normed.at[3, c], sems_fwd, c, sibling).wait_send()
        return 0

    lax.fori_loop(0, cubes, finish, 0)
    for item in to_peers:
        item.wait_send()


def forward_call(enc, codes, gain, offset, mask_token, w_qkv, cubes, groups):
    tokens, width = enc.shape
    quarter = tokens // cubes
    cap = quarter // 3
    half = width // 2
    packs = half // 128
    wide = (128 // (width // HEADS)) * 2 * cap
    vmem = pl.BlockSpec(memory_space=pltpu.VMEM)
    far = pl.BlockSpec(memory_space=pl.ANY)
    shape = jax.ShapeDtypeStruct
    dma = pltpu.SemaphoreType.DMA
    return pl.pallas_call(
        forward_kernel,
        out_shape=(
            shape((cubes, width, quarter), BF),
            shape((groups, cubes, quarter, width), BF),
            shape((groups, 8, quarter), jnp.int32),
            shape((cubes, groups, groups * cap, width), BF),
            shape((cubes, groups, groups * cap, 128), BF),
            shape((cubes, groups, half, 2 * cap), BF),
            shape((cubes, groups, half, 2 * cap), BF),
            shape((cubes, groups, 8, wide), F32),
        ),
        in_specs=[vmem] * 5 + [far],
        out_specs=(vmem, far, vmem, far, far, far, far, vmem),
        scratch_shapes=[
            dma((3,)),
            pltpu.VMEM((groups, cubes, quarter, width), BF),
            pltpu.VMEM((cubes, groups, groups * cap, width), BF),
            pltpu.VMEM((cubes, groups, groups * cap, 128), BF),
            pltpu.VMEM((cubes, groups, half, 2 * cap), BF),
            pltpu.VMEM((cubes, groups, half, 2 * cap), BF),
            pltpu.VMEM((cubes, quarter, 1), F32),
            pltpu.VMEM((width, 3 * half), BF),
            pltpu.VMEM((half, width), BF),
            pltpu.VMEM((packs, 256, wide), BF),
            pltpu.VMEM((packs, 144, groups * cap), BF),
            pltpu.VMEM((cubes, half, quarter), BF),
            (dma((2 * cubes,)), dma((2 * cubes,))),
            (dma((3,)), dma((3,))),
            (dma((cubes,)), dma((cubes,))),
            (dma((cubes,)), dma((cubes,))),
            dma((cubes, 5)),
        ],
        compiler_params=pltpu.CompilerParams(
            collective_id=0, has_side_effects=True, vmem_limit_bytes=60 * 2**20),
        name="forward",
    )(enc, codes, gain, offset, mask_token, w_qkv)


def pieces(values):
    high = values.astype(BF)
    rest = values - high.astype(F32)
    mid = rest.astype(BF)
    low = (rest - mid.astype(F32)).astype(BF)
    return high, mid, low


def layer_kernel(
    n_dp, n_group,
    att_in, kv_in, kaug_in, qt_in, ot_in, lse, normed_in, dest, w_qkv, enc, visible, mask_token, gain,
    cot_in, w_out_in, w_up_in, w_down_in, gain2, offset2,
    out, grad_enc, sum_ffn, sum_qkv, sum_small,
    kv_at, kaug_at, qt_at, ot_at, normed_at, grads_at, turn, sems_read, sems_turn,
    cot, w_out, w_up, w_down, att, middle, second, backs, result, grads_sum, spare, w_mine, sems_load, sems_out,
    acc, give, pair, recv, settled, sems_core, sems_ffn,
    grad_qkv, small, send_qkv, recv_qkv, settled_qkv, small_bufs, sems_qkv, sems_pair, sems_small,
    columns, dot_slots, qbd, dobd, grad_qt, in_sib, in_fwd, in_across, sems_sib, sems_fwd, sems_across,
):
    cubes, quarter, width = middle.shape
    half = width // 2
    blocks = w_up.shape[0]
    groups = kv_at.shape[1]
    cap = qt_at.shape[3] // 2
    slots = groups * cap
    hd = width // HEADS
    pack = 128
    per = pack // hd
    packs = half // pack
    factor = hd ** -0.5
    sibling, across = peer((1,)), peer((2,))
    parity = lax.rem(lax.axis_index("group"), 2)
    mine = pl.ds(pl.multiple_of(parity * half, half), half)
    theirs = pl.ds(pl.multiple_of((1 - parity) * half, half), half)
    grad_kv, own_sum, out_fwd, out_sib, out_across = w_up, result, cot, second, backs

    core = ("group", 1)
    others = chip_bits(n_dp, n_group)
    paths = balanced_orders(others)
    qkv = [
        Butterfly(grad_qkv.at[p], send_qkv.at[p], recv_qkv.at[p], settled_qkv.at[p], sum_qkv.at[parity, p],
                  (sems_qkv[0].at[p], sems_qkv[1].at[p]), order)
        for p, order in enumerate([balanced_orders(others)[k] for k in (0, 2, 1)])]
    qkv_steps = joined(reduce_steps(qkv), gather_steps(qkv))

    def swap_copies(side):
        items = []
        for p, b in enumerate(qkv):
            count = b.rows // 2
            value = bit_value(b.names[0])
            rows = b.out.at[b.span((value if side == 0 else 1 - value) * count, count), :]
            items.append(copy_to(rows, rows, sems_pair, 3 * side + p, sibling))
        return items
    smalls = [
        SmallSum(small_bufs[k], (sems_small[0].at[k], sems_small[1].at[k]), names)
        for k, names in enumerate(small_groups(n_dp, n_group))]

    def place_of(j, side):
        if j < blocks:
            return sum_ffn.at[j + side * blocks]
        return sum_ffn.at[2 * blocks, pl.ds(pl.multiple_of(side * half, half), half)]

    def rows_in(j):
        return width if j < blocks else half

    def butterflies(j):
        count = rows_in(j)
        return [
            Butterfly(acc.at[j, :count, lanes_of(p)], give.at[j, :, lanes_of(p)], recv.at[j, :, lanes_of(p)],
                      settled.at[j, :count >> halvings_of(count, len(others)), lanes_of(p)],
                      place_of(j, parity).at[:, lanes_of(p)],
                      (sems_ffn[0].at[j, p], sems_ffn[1].at[j, p]), paths[p]) for p in range(PARTS)]

    def summing(j):
        count = rows_in(j)
        inner = reduce_steps(butterflies(j))
        exchange = copy_to(give.at[j, :count], pair.at[j, :count], sems_core, j, sibling)

        def second_step():
            exchange.wait()
            acc[j, :count] += pair[j, :count].astype(F32)
            inner[0]()

        return [exchange.start, second_step] + inner[1:]

    def spreading(sets):
        steps = gather_steps([b for j in sets for b in butterflies(j)])

        def exchanges():
            return [
                copy_to(place_of(j, parity), place_of(j, parity), sems_core, blocks + 1 + j, sibling) for j in sets]

        def last_but_one():
            steps[-1]()
            for item in exchanges():
                item.start()

        def final():
            for item in exchanges():
                item.wait()

        return steps[:-1] + [last_but_one, final]

    def reads(c):
        k = lax.rem(c, 2)
        pairs = [(kv_in.at[c], kv_at.at[k]), (kaug_in.at[c], kaug_at.at[k]), (qt_in.at[c], qt_at.at[k]),
                 (ot_in.at[c], ot_at.at[k]), (normed_in.at[:, c], normed_at.at[k])]
        return [pltpu.make_async_copy(src, dst, sems_read.at[k, n]) for n, (src, dst) in enumerate(pairs)]

    loads = [(w_out_in, w_out), (att_in, att)]
    loads += [(w_up_in.at[:, j * width:(j + 1) * width], w_up.at[j]) for j in range(blocks)]
    loads += [(w_down_in.at[j * width:(j + 1) * width, :], w_down.at[j]) for j in range(blocks)]
    loads += [(cot_in.at[c * quarter:(c + 1) * quarter, :], cot.at[c]) for c in range(cubes)]
    loads += [(w_qkv.at[:, pl.ds(pl.multiple_of(p * width + parity * half, half), half)],
               w_mine.at[:, p * half:(p + 1) * half]) for p in range(3)]
    loads = [pltpu.make_async_copy(src, dst, sems_load.at[k]) for k, (src, dst) in enumerate(loads)]
    for item in loads:
        item.start()
    for c in range(min(2, cubes)):
        for item in reads(c):
            item.start()

    meets = {}
    for names in small_groups(n_dp, n_group):
        for t in range(1, 1 << len(names)):
            chosen = [name for k, name in enumerate(names) if (t >> k) & 1]
            meets[tuple(sorted(chosen))] = flip(chosen)
    for chosen in [[core]] + [[name] for name in others] + [
            list(pair) for i, first in enumerate(others) for pair in ((first, other) for other in others[i + 1:])]:
        meets[tuple(sorted(chosen))] = flip(chosen)
    one_row = lax.broadcasted_iota(jnp.int32, (16, per * 2 * cap), 0)
    def rows_of(c):
        return pl.ds(c * quarter, quarter)

    def start_rows(c):
        shown = columns[c] == 1.0
        return shown, jnp.where(shown, enc[rows_of(c), :].astype(F32), mask_token[...])

    def turn_copy(c):
        return copy_to(turn.at[c], grads_at.at[c, 1], sems_turn, c, sibling)

    def out_copy(c):
        return pltpu.make_async_copy(second.at[c], out.at[rows_of(c), :], sems_out.at[0, c])

    def enc_copy(c):
        return pltpu.make_async_copy(second.at[c], grad_enc.at[rows_of(c), :], sems_out.at[1, c])

    def enter(c, _):
        value = start_rows(c)[1] + dot(att[c], w_out[...], TN)
        middle[c] = value
        normal, _ = norm_stats(value)
        second[c] = (normal * gain2[...] + offset2[...]).astype(BF)
        return 0

    def block(j, c):
        rows, cotan = second[c], cot[c]
        hidden = dot(rows, w_up[j])
        square = hidden * hidden
        tanh = jnp.tanh(hidden * (GELU_A + GELU_B * square))
        slope = 0.5 * (1.0 + tanh)
        active = (hidden * slope).astype(BF)
        slope = slope + 0.5 * hidden * (1.0 - tanh * tanh) * (GELU_A + 3.0 * GELU_B * square)
        grad_hidden = (dot(cotan, w_down[j], NT) * slope).astype(BF)
        grad_up = dot(rows, grad_hidden, TN)
        grad_down = dot(active, cotan, TN)
        kept = jnp.where(parity == 0, grad_up, grad_down)
        given = jnp.where(parity == 0, grad_down, grad_up)
        outcome = dot(active, w_down[j])
        grads = dot(grad_hidden, w_up[j], NT)
        result[c] = outcome + jnp.where(j > 0, result[c], 0.0)
        grads_sum[c] = grads + jnp.where(j > 0, grads_sum[c], 0.0)
        acc[j] = kept + jnp.where(c > 0, acc[j], 0.0)
        spare[...] = given + jnp.where(c > 0, spare[...], 0.0)

        def hand_over():
            give[j, :width] = spare[...].astype(BF)

        pl.when(c == cubes - 1)(hand_over)

    def leave(c):
        second[c] = (middle[c] + result[c]).astype(BF)
        out_copy(c).start()
        normal, recip = norm_stats(middle[c])
        grads = grads_sum[c]
        small[3:4, :] += jnp.sum(grads * normal, axis=0, keepdims=True)
        small[4:5, :] += jnp.sum(grads, axis=0, keepdims=True)
        total = cot[c].astype(F32) + norm_back(grads, normal, recip, gain2[...])
        middle[c] = total
        branch = total.astype(BF)
        back = dot(w_out[...], branch, NT).astype(BF)
        backs[c] = branch
        turn[c] = jnp.where(parity == 0, back[half:], back[:half])
        grads_at[c, 0] = jnp.where(parity == 0, back[:half], back[half:])
        turn_copy(c).start()

    def out_weights():
        total = dot(att[0], backs[0])
        for c in range(1, cubes):
            total += dot(att[c], backs[c])
        acc[blocks, :half] = jnp.where(parity == 0, total[:half], total[half:])
        give[blocks, :half] = jnp.where(parity == 0, total[half:], total[:half]).astype(BF)

    firsts = [summing(j) for j in range(blocks + 1)]
    seconds = [spreading(sets) for sets in SPREADS]
    plan = []
    for number, (steps, places) in enumerate(zip(firsts + seconds, SUM_AT + SPREAD_AT)):
        if len(places) != len(steps):
            places = [places[0] + 2 * k for k in range(len(steps))]
        stage = 0 if number < len(firsts) else len(steps)
        plan += [(place, stage + k, number, step) for k, (place, step) in enumerate(zip(places, steps))]
    plan = [(entry[0], entry[-1]) for entry in sorted(plan, key=lambda entry: entry[:3])]
    lead = blocks * cubes + cubes + 1

    def advance(place):
        for at, step in plan:
            if at == place:
                step()

    def before_sums():
        for p in range(packs):
            qbd[p] = jnp.zeros(qbd.shape[1:], BF)
            dobd[p] = jnp.zeros(dobd.shape[1:], BF)
        as_columns(visible, columns)
        grad_qkv[...] = jnp.zeros(grad_qkv.shape, F32)
        small[...] = jnp.zeros(small.shape, F32)
        for item in loads[:2]:
            item.wait()
        lax.fori_loop(0, cubes, enter, 0)

    greet(list(meets.values()), before_sums)
    for item in loads[2:]:
        item.wait()
    place = blocks * cubes

    def blocks_step(u, _):
        block(u // cubes, lax.rem(u, cubes))
        for at, step in plan:
            if at <= place:
                pl.when(u == at - 1)(step)
        return 0

    lax.fori_loop(0, place, blocks_step, 0)
    for c in range(cubes):
        leave(c)
        place += 1
        advance(place)
    out_weights()
    place += 1
    advance(place)
    for c in range(cubes):
        out_copy(c).wait()

    def extra_rows(first, values):
        high, mid, low = pieces(-values)
        rows = jnp.where(
            one_row == 0, first,
            jnp.where(one_row == 1, high.astype(F32),
                      jnp.where(one_row == 2, mid.astype(F32),
                                jnp.where(one_row == 3, low.astype(F32), 0.0))))
        return rows.astype(BF)

    def attend_back(c, s):
        slot = lax.rem(c, 2)
        for p in range(packs):
            lanes = slice(p * pack, (p + 1) * pack)
            deltas = []
            for j in range(per):
                rows = slice(p * pack + j * hd, p * pack + (j + 1) * hd)
                cols = slice(j * 2 * cap, (j + 1) * 2 * cap)
                qbd[p, j * hd:(j + 1) * hd, cols] = qt_at[slot, s, rows, :]
                grads = dot_slots[s, rows, :]
                dobd[p, j * hd:(j + 1) * hd, cols] = grads
                deltas.append(jnp.sum(
                    grads.astype(F32) * ot_at[slot, s, rows, :].astype(F32), axis=0, keepdims=True))
            qbd[p, pack:pack + 16, :] = extra_rows(1.0, lse[c, s, p:p + 1, :])
            dobd[p, pack:pack + 16, :] = extra_rows(0.0, jnp.concatenate(deltas, axis=1))
            extra = kaug_at[slot, s]
            keys = kv_at[slot, s, :, lanes]
            values = kv_at[slot, s, :, half + p * pack:half + (p + 1) * pack]
            probs = jnp.exp2(dot(jnp.concatenate([keys, extra], axis=1), qbd[p]))
            centred = dot(jnp.concatenate([values, extra], axis=1), dobd[p])
            grad_scores = (probs * centred).astype(BF)
            grad_kv[s, :, half + p * pack:half + (p + 1) * pack] = dot(
                probs.astype(BF), dobd[p, :pack, :], NT).astype(BF)
            grad_kv[s, :, lanes] = (dot(grad_scores, qbd[p, :pack, :], NT) * LN2).astype(BF)
            mixed = dot(keys.T, grad_scores) * factor
            for j in range(per):
                rows = slice(p * pack + j * hd, p * pack + (j + 1) * hd)
                cols = slice(j * 2 * cap, (j + 1) * 2 * cap)
                grad_qt[s, rows, :] = mixed[j * hd:(j + 1) * hd, cols].astype(BF)

    def back_rows(r, c):
        hot = onehot(dest[r, pl.ds(c, 1), :], slots)
        placed = jnp.concatenate(
            [grad_kv[s, r * cap:(r + 1) * cap, :] for s in range(groups)], axis=0)
        grads = dot(hot, placed, TN).astype(BF)
        if r < 2:
            queries = jnp.concatenate(
                [grad_qt[s, :, r * cap:(r + 1) * cap] for s in range(groups)], axis=1)
            queries = dot(queries, hot).T.astype(BF)
            grads = jnp.concatenate([queries, grads], axis=1)
        weight = dot(normed_at[lax.rem(c, 2), r], grads, TN)
        first = 3 - weight.shape[1] // half
        for k in range(first, 3):
            grad_qkv[k] += weight[:, (k - first) * half:(k - first + 1) * half]
        return grads

    def back_project(r, c):
        grads = back_rows(r, c)
        return dot(grads, w_mine[:, 3 * half - grads.shape[1]:], NT)

    def prepare(c):
        for item in reads(c):
            item.wait()
        for r in range(2):
            rows = grads_at[c, r]
            hot = onehot(dest[r, pl.ds(c, 1), :], slots)
            spread = dot(rows, hot, NT).astype(BF)
            for s in range(groups):
                dot_slots[s, :, r * cap:(r + 1) * cap] = spread[:, s * cap:(s + 1) * cap]

    def cube(c, _):
        def point(i):
            for at, step in plan:
                if at > lead and (at - lead - 1) % POINTS == i and (at - lead - 1) // POINTS < cubes:
                    pl.when(c == (at - lead - 1) // POINTS)(step)

        turn_copy(c).wait()
        prepare(c)
        point(0)

        def one(s, _):
            attend_back(c, s)
            for i in range(groups):
                pl.when(s == i)(functools.partial(point, i + 1))
            return 0

        lax.fori_loop(0, groups, one, 0)
        out_fwd[c] = back_project(3, c).astype(BF)
        forward = copy_to(out_fwd.at[c], in_fwd.at[c], sems_fwd, c, sibling)
        forward.start()
        point(5)
        partial = back_project(2, c)
        forward.wait_recv()
        out_across[c] = (partial + in_fwd[c].astype(F32)).astype(BF)
        copy_to(out_across.at[c], in_across.at[c], sems_across, c, across).start()
        point(6)
        near_rows = back_rows(1, c)
        own_rows = back_rows(0, c)
        pl.when(c == cubes - 1)(qkv_steps[0])
        point(7)
        out_sib[c] = dot(near_rows, w_mine[...], NT).astype(BF)
        copy_to(out_sib.at[c], in_sib.at[c], sems_sib, c, sibling).start()
        own_sum[c] = dot(own_rows, w_mine[...], NT)

        def more():
            for item in reads(c + 2):
                item.start()

        pl.when(c + 2 < cubes)(more)
        point(8)
        return 0

    lax.fori_loop(0, cubes, cube, 0)
    tail = [(at - lead - POINTS * cubes, step) for at, step in plan if at > lead + POINTS * cubes]

    def last(c):
        copy_to(out_sib.at[c], in_sib.at[c], sems_sib, c, sibling).wait()
        copy_to(out_across.at[c], in_across.at[c], sems_across, c, across).wait()
        copy_to(out_fwd.at[c], in_fwd.at[c], sems_fwd, c, sibling).wait_send()
        grads = own_sum[c] + in_sib[c].astype(F32) + in_across[c].astype(F32)
        shown, start = start_rows(c)
        normal, recip = norm_stats(start)
        small[0:1, :] += jnp.sum(grads * normal, axis=0, keepdims=True)
        small[1:2, :] += jnp.sum(grads, axis=0, keepdims=True)
        total = middle[c] + norm_back(grads, normal, recip, gain[...])
        second[c] = jnp.where(shown, total, 0.0).astype(BF)
        enc_copy(c).start()
        small[2:3, :] += jnp.sum(jnp.where(shown, 0.0, total), axis=0, keepdims=True)

    fill = list(range(cubes))
    pending = []

    def small_step():
        total = smalls[pending[0]].finish()
        pending.append(pending.pop(0) + 1)
        if pending[0] < len(smalls):
            smalls[pending[0]].start(total)
        else:
            pending.clear()
            sum_small[...] = total

    for k in range(1, len(qkv_steps)):
        if fill:
            last(fill.pop(0))
            if not fill:
                smalls[0].start(small[...])
                pending.append(0)
            qkv_steps[k]()
        else:
            qkv_steps[k]()
            if k == len(qkv_steps) - 2:
                for item in swap_copies(0):
                    item.start()
            if pending:
                small_step()
        while tail and tail[0][0] <= k:
            tail.pop(0)[1]()
    for item in swap_copies(1):
        item.start()
    for _, step in tail:
        step()
    while pending:
        small_step()
    for c in range(cubes):
        enc_copy(c).wait()
    for item in swap_copies(0) + swap_copies(1):
        item.wait()


POINTS = 9
PARTS = 4
SUM_AT = [
    [3, 5, 9, 12, 16],
    [6, 8, 12, 17, 20],
    [9, 11, 15, 19, 22],
    [12, 14, 18, 21, 25],
    [16, 18, 21, 26, 29],
]
SPREADS = [[0], [1], [2], [3], [4]]
SPREAD_AT = [
    [16, 20, 23, 28, 30],
    [20, 24, 28, 32, 34],
    [22, 27, 30, 35, 37],
    [25, 29, 33, 37, 39],
    [29, 33, 37, 39, 41],
]


def layer_call(
    att, kv, kaug, qt, ot, lse, normed, dest, w_qkv, enc, visible, mask_token, gain,
    cot, w_out, w_up, w_down, gain2, offset2, n_dp, n_group,
):
    cubes, width, quarter = att.shape
    groups = kv.shape[1]
    cap = quarter // 3
    half = width // 2
    packs = half // 128
    wide = (128 // (width // HEADS)) * 2 * cap
    blocks = w_up.shape[1] // width
    vmem = pl.BlockSpec(memory_space=pltpu.VMEM)
    far = pl.BlockSpec(memory_space=pl.ANY)
    shape = jax.ShapeDtypeStruct
    dma = pltpu.SemaphoreType.DMA
    rows = pltpu.VMEM((cubes, quarter, width), BF)
    sums = pltpu.VMEM((cubes, quarter, width), F32)
    squares = pltpu.VMEM((blocks, width, width), BF)
    pair = (dma((cubes,)), dma((cubes,)))
    stages = len(chip_bits(n_dp, n_group))
    staging = staging_rows(width, stages)
    kept = max(width >> halvings_of(width, stages), half >> halvings_of(half, stages))
    kept_qkv = width >> halvings_of(width, stages)
    small = small_groups(n_dp, n_group)
    return pl.pallas_call(
        functools.partial(layer_kernel, n_dp, n_group),
        out_shape=(
            shape(enc.shape, BF),
            shape(enc.shape, BF),
            shape((2 * blocks + 1, width, width), BF),
            shape((2, 3, width, half), BF),
            shape((8, width), F32),
        ),
        in_specs=[far] * 5 + [vmem, far, vmem, far] + [vmem] * 4 + [far] * 4 + [vmem] * 2,
        out_specs=(far, far, far, far, vmem),
        scratch_shapes=[
            pltpu.VMEM((2,) + kv.shape[1:], BF),
            pltpu.VMEM((2,) + kaug.shape[1:], BF),
            pltpu.VMEM((2,) + qt.shape[1:], BF),
            pltpu.VMEM((2,) + ot.shape[1:], BF),
            pltpu.VMEM((2, groups, quarter, width), BF),
            pltpu.VMEM((cubes, 2, half, quarter), BF),
            pltpu.VMEM((cubes, half, quarter), BF),
            dma((2, 5)),
            pair,
            rows,
            pltpu.VMEM(w_out.shape, BF),
            squares,
            squares,
            pltpu.VMEM(att.shape, BF),
            sums,
            rows,
            rows,
            sums,
            sums,
            pltpu.VMEM((width, width), F32),
            pltpu.VMEM((width, 3 * half), BF),
            dma((2 + 2 * blocks + cubes + 3,)),
            dma((2, cubes)),
            pltpu.VMEM((blocks + 1, width, width), F32),
            pltpu.VMEM((blocks + 1, max(width, staging), width), BF),
            pltpu.VMEM((blocks + 1, width, width), BF),
            pltpu.VMEM((blocks + 1, staging, width), BF),
            pltpu.VMEM((blocks + 1, kept, width), BF),
            (dma((2 * blocks + 2,)), dma((2 * blocks + 2,))),
            (dma((blocks + 1, PARTS, 2 * stages + 3)), dma((blocks + 1, PARTS, 2 * stages + 3))),
            pltpu.VMEM((3, width, half), F32),
            pltpu.VMEM((8, width), F32),
            pltpu.VMEM((3, staging, half), BF),
            pltpu.VMEM((3, staging, half), BF),
            pltpu.VMEM((3, kept_qkv, half), BF),
            tuple(pltpu.VMEM((1 << len(names), 8, width), F32) for names in small),
            (dma((3, 2 * stages + 3)), dma((3, 2 * stages + 3))),
            (dma((6,)), dma((6,))),
            (dma((len(small), 8)), dma((len(small), 8))),
            pltpu.VMEM((cubes, quarter, 1), F32),
            pltpu.VMEM((groups, half, 2 * cap), BF),
            pltpu.VMEM((packs, 256, wide), BF),
            pltpu.VMEM((packs, 256, wide), BF),
            pltpu.VMEM((groups, half, 2 * cap), BF),
            rows, rows, rows,
            pair, pair, pair,
        ],
        compiler_params=pltpu.CompilerParams(
            collective_id=1, has_side_effects=True, vmem_limit_bytes=63 * 2**20),
        name="layer",
    )(att, kv, kaug, qt, ot, lse, normed, dest, w_qkv, enc, visible, mask_token, gain,
      cot, w_out, w_up, w_down, gain2, offset2)


def cast_kernel(ups, downs, outs, qkvs, small, tokens, grads, up, down, out, qkv, tokens_out, grads_out, *vectors):
    width, half = outs.shape[1], qkvs.shape[3]
    for k in range(ups.shape[0]):
        up[:, k * width:(k + 1) * width] = ups[k].astype(F32)
    down[...] = downs[...].astype(F32)
    out[...] = outs[...].astype(F32)
    for part in range(3):
        for side in range(2):
            at = part * width + side * half
            qkv[:, at:at + half] = qkvs[side, part].astype(F32)
    tokens_out[...] = tokens[...]
    grads_out[...] = grads[...]
    for k, vector in enumerate(vectors):
        vector[...] = small[k:k + 1, :]


def cast_call(ffn, qkv, small, tokens, grads):
    width = qkv.shape[2]
    blocks = ffn.shape[0] // (2 * width)
    steps = 2
    rows = width // steps
    tall = blocks * rows
    token_rows = pl.BlockSpec((tokens.shape[0] // steps, width), lambda i: (i, 0))
    shape = jax.ShapeDtypeStruct
    return pl.pallas_call(
        cast_kernel,
        grid=(steps,),
        in_specs=[
            pl.BlockSpec((blocks, rows, width), lambda i: (0, i, 0)),
            pl.BlockSpec((tall, width), lambda i: (steps + i, 0)),
            pl.BlockSpec((rows, width), lambda i: (2 * blocks * steps + i, 0)),
            pl.BlockSpec((2, 3, rows, width // 2), lambda i: (0, 0, i, 0)),
            pl.BlockSpec(small.shape, lambda i: (0, 0)),
            token_rows,
            token_rows,
        ],
        out_specs=[
            pl.BlockSpec((rows, blocks * width), lambda i: (i, 0)),
            pl.BlockSpec((tall, width), lambda i: (i, 0)),
            pl.BlockSpec((rows, width), lambda i: (i, 0)),
            pl.BlockSpec((rows, 3 * width), lambda i: (i, 0)),
            token_rows,
            token_rows,
        ] + [pl.BlockSpec((1, width), lambda i: (0, 0))] * 5,
        out_shape=(
            shape((width, blocks * width), F32),
            shape((blocks * width, width), F32),
            shape((width, width), F32),
            shape((width, 3 * width), F32),
            shape(tokens.shape, BF),
            shape(tokens.shape, BF),
        ) + (shape((1, width), F32),) * 5,
        name="cast",
    )(ffn.reshape(2 * blocks + 1, width, width), ffn, ffn, qkv, small, tokens, grads)


def on_device(
    enc, visible, band_group, cotangent, ln1_gain, ln1_bias, w_qkv, w_out,
    ln2_gain, ln2_bias, w_up, w_down, mask_token,
):
    groups = lax.axis_size("group")
    tok_dev, width = enc.shape
    quarter = CUBE_TOK // groups
    cubes = tok_dev // quarter
    codes = (visible * 8 + band_group).reshape(cubes, quarter)
    gain1, mask_row = ln1_gain[None, :], mask_token[None, :]
    att, normed, dest, kv, kaug, qt, ot, lse = forward_call(
        enc, codes, gain1, ln1_bias[None, :], mask_row, w_qkv, cubes, groups)
    out, grad_enc, sum_ffn, sum_qkv, small = layer_call(
        att, kv, kaug, qt, ot, lse, normed, dest, w_qkv, enc, codes, mask_row, gain1, cotangent, w_out, w_up,
        w_down, ln2_gain[None, :], ln2_bias[None, :], lax.axis_size("dp"), groups)
    (sum_up, sum_down, sum_out, sum_w_qkv, out, grad_enc, gain1_sum, bias1_sum, mask_sum, gain2_sum, bias2_sum,
     ) = cast_call(sum_ffn.reshape(9 * width, width), sum_qkv, small, out, grad_enc)
    gain1_sum, bias1_sum, mask_sum, gain2_sum, bias2_sum = (
        vector.reshape(width) for vector in (gain1_sum, bias1_sum, mask_sum, gain2_sum, bias2_sum))
    return (
        out, grad_enc, gain1_sum, bias1_sum, sum_w_qkv, sum_out, gain2_sum, bias2_sum, sum_up, sum_down, mask_sum)


def solution(mesh):
    rows, line = P(("dp", "group"), None), P(("dp", "group"))
    return jax.shard_map(
        on_device, mesh=mesh, in_specs=(rows, line, line, rows) + (P(),) * 9,
        out_specs=(rows, rows) + (P(),) * 9, check_vma=False)
```
